32 devices in a mesh: dp: 16 (over z, y, core), branch: 2 (over x).
Axes of the slice: x: 2, y: 2, z: 4, core: 2. Of those that a mesh axis runs over, the one named last changes fastest.
Arguments:
- embed_rows: bfloat16 [1179648, 160], P(('dp', 'branch')), may hold values from -6 to 6
- lengths: int32 [32, 24576], P(('dp', 'branch')), may hold values from 1 to 16, 36864 in all within a row
- cotangent: bfloat16 [24576, 5120], P(('dp', 'branch')), may hold values from -6 to 6
- p_proj: bfloat16 [32, 24], replicated, may hold values from -1 to 1
- gain_one: float32 [768], replicated, may hold values from 0.25 to 1.75
- bias_one: float32 [768], replicated, may hold values from -3 to 3
- w_up: bfloat16 [768, 1536], P(None, 'dp'), may hold values from -0.21875 to 0.21875
- b_up: float32 [1536], replicated, may hold values from -3 to 3
- w_down: bfloat16 [1536, 2560], P('dp'), may hold values from -0.15625 to 0.15625
- b_down: float32 [2560], replicated, may hold values from -3 to 3
- w_comp: bfloat16 [16, 32], replicated, may hold values from -1 to 1
- w_res: bfloat16 [32, 32], replicated, may hold values from -1 to 1
- gain_two: float32 [160], replicated, may hold values from 0.25 to 1.75
- bias_two: float32 [160], replicated, may hold values from -3 to 3
Outputs:
- output: bfloat16 [24576, 5120], P(('dp', 'branch'))
- rows_grad: bfloat16 [1179648, 160], P(('dp', 'branch'))
- p_proj_grad: float32 [32, 24], replicated
- gain_one_grad: float32 [768], replicated
- bias_one_grad: float32 [768], replicated
- w_up_grad: float32 [768, 1536], P(None, 'dp')
- b_up_grad: float32 [1536], replicated
- w_down_grad: float32 [1536, 2560], P('dp')
- b_down_grad: float32 [2560], replicated
- w_comp_grad: float32 [16, 32], replicated
- w_res_grad: float32 [32, 32], replicated
- gain_two_grad: float32 [160], replicated
- bias_two_grad: float32 [160], replicated
The draws below stay inside these ranges and needn't reach their ends.
Inputs may be any that keep to these rules, and one draw needn't show every extreme that they name: Each row of 24576 bag lengths sums to 36864, and each row holds a bag of exactly 16 rows.
All inputs are finite; a program needn't handle non-finite values.
Results may differ from the reference program's by a relative error of at most 0.0085.
Values may be sent and summed in bfloat16 or wider, within the bound.
No kernel may reach another device: no remote copies, remote signals or barrier semaphores. Data moves between devices by JAX's collectives and lax.ppermute only.
A program may use at most 448 MiB of HBM per device.

```python
import math
import jax
import jax.numpy as jnp
import numpy as np
from jax import lax

D = 160
NTOK = 32
K = 24
FMB_H = 1536
NF = 16
NL = 16
EX_DEV = 768
BAG_MOST = 16
BAGS_DEV = 24576
ROWS_DEV = 36864
EXAMPLES = 24576
ROWS = 1179648
N_DP = 16


def level_of(rng, extent, pieces, smallest, largest):
    def one(axis_at, shards_of):
        draws = jax.random.uniform(jax.random.fold_in(jax.random.fold_in(rng, 6), axis_at), (shards_of,), jnp.float32, smallest / len(pieces), largest / len(pieces))
        return jnp.repeat(jnp.exp(draws), extent[axis_at] // shards_of).reshape((-1,) + (1,) * (len(extent) - axis_at - 1))

    gain = one(*pieces[0])
    for cut in pieces[1:]:
        gain = gain * one(*cut)
    return gain


def length_profile(amount, total, bound, skew):
    loads = [(1 << 20) // math.isqrt(standing ** skew) + 1 for standing in range(2, amount + 1)]
    spare, holding = total - bound - (amount - 1), [1] * (amount - 1)
    while spare > 0:
        candidates = [i for i in range(amount - 1) if holding[i] < bound]
        whole, budget = sum([loads[i] for i in candidates]), spare
        for i in candidates:
            more = min(bound - holding[i], max(1, budget * loads[i] // whole), spare)
            holding[i] = holding[i] + more
            spare = spare - more
    return np.array([bound] + holding)


def ragged(key, number_of, total, most, slope):
    if number_of == 2:
        one = jax.random.randint(key, (), max(1, total - most), min(most, total - 1) + 1)
        return jnp.stack([one, total - one])
    sizes = jnp.asarray(length_profile(number_of, total, most, slope), jnp.int32)
    couples = (number_of - 1) // 2
    donor, receiver = sizes[1:1 + 2 * couples:2], sizes[2:2 + 2 * couples:2]
    margin = jnp.minimum(donor - 1, most - receiver)
    moved = jax.random.randint(jax.random.fold_in(key, 1), (couples,), 0, 1 << 20) % (margin + 1)
    sizes = sizes.at[1:1 + 2 * couples:2].set(donor - moved).at[2:2 + 2 * couples:2].set(receiver + moved)
    return sizes[jax.random.permutation(jax.random.fold_in(key, 2), number_of)]


def bell_draw(rng, shape, spread, reach, cuts=(), kind=jnp.bfloat16):
    factor_of = level_of(rng, shape, cuts, -0.22, 0.18) if cuts else 1.0
    entries = jax.random.normal(rng, shape, jnp.float32) * spread * factor_of
    return jnp.minimum(jnp.maximum(entries, -reach), reach).astype(kind)


def setup_inputs(seed: int = 0) -> dict:
    keys = jax.random.split(jax.random.key(seed), 15)
    embed_rows = bell_draw(keys[0], (ROWS, D), 0.8, 6.0, ((0, 32),))
    lengths = jax.vmap(lambda own: ragged(own, BAGS_DEV, ROWS_DEV, BAG_MOST, 2))(jax.random.split(keys[1], (2 * N_DP))).reshape((2 * N_DP, BAGS_DEV)).astype(jnp.int32)
    cotangent = bell_draw(keys[2], (EXAMPLES, NTOK * D), 1.0, 6.0, ((0, 32),))
    p_proj = bell_draw(keys[3], (NTOK, K), NTOK ** -0.5, 1.0)
    gain_one = jnp.clip(1.0 + 0.15 * jax.random.normal(keys[4], (NTOK * K,), jnp.float32), 0.25, 1.75)
    bias_one = bell_draw(keys[5], (NTOK * K,), 0.5, 3.0, (), jnp.float32)
    w_up = bell_draw(keys[6], (NTOK * K, FMB_H), (NTOK * K) ** -0.5, 0.21875, ((1, 16),))
    b_up = bell_draw(keys[7], (FMB_H,), 0.5, 3.0, (), jnp.float32)
    w_down = bell_draw(keys[8], (FMB_H, NF * D), FMB_H ** -0.5, 0.15625, ((0, 16),))
    b_down = bell_draw(keys[9], (NF * D,), 0.5, 3.0, (), jnp.float32)
    w_comp = bell_draw(keys[10], (NL, NTOK), NTOK ** -0.5, 1.0)
    w_res = bell_draw(keys[11], (NTOK, NTOK), NTOK ** -0.5, 1.0)
    gain_two = jnp.clip(1.0 + 0.15 * jax.random.normal(keys[12], (D,), jnp.float32), 0.25, 1.75)
    bias_two = bell_draw(keys[13], (D,), 0.5, 3.0, (), jnp.float32)
    return {"embed_rows": embed_rows, "lengths": lengths, "cotangent": cotangent, "p_proj": p_proj, "gain_one": gain_one, "bias_one": bias_one, "w_up": w_up, "b_up": b_up, "w_down": w_down, "b_down": b_down, "w_comp": w_comp, "w_res": w_res, "gain_two": gain_two, "bias_two": bias_two}


@jax.custom_vjp
def low(v):
    return lax.optimization_barrier(v.astype(jnp.bfloat16)).astype(jnp.float32)

@jax.custom_vjp
def low_back(v):
    return v

def low_keep(v):
    return (low(v), None)

def low_pass(kept, grad):
    return (grad,)

def back_keep(v):
    return (v, None)

def back_low(kept, grad):
    return (low(grad),)
low.defvjp(low_keep, low_pass)
low_back.defvjp(back_keep, back_low)

def normalize(values, scales, offset):
    average = lax.optimization_barrier(jnp.mean(values, axis=-1, keepdims=True))
    centred = values - average
    variance = lax.optimization_barrier(jnp.mean(centred * centred, axis=-1, keepdims=True))
    return centred * lax.rsqrt(variance + 1e-05) * scales + offset

def reference(embed_rows, lengths, cotangent, p_proj, gain_one, bias_one, w_up, b_up, w_down, b_down, w_comp, w_res, gain_two, bias_two):
    highest = lax.Precision.HIGHEST
    counts = lengths.reshape(-1)
    bounds = jnp.cumsum(counts)
    places = jnp.arange(embed_rows.shape[0], dtype=jnp.int32)
    segment = jnp.searchsorted(bounds, places, side='right').astype(jnp.int32)

    def forward(rows_in, proj_w, gain_a, bias_a, up_w, up_b, down_w, down_b, comp_w, res_w, gain_b, bias_b):
        bag_sums = jax.ops.segment_sum(rows_in, segment, num_segments=counts.shape[0])
        feats = low(bag_sums).reshape(-1, EX_DEV, NTOK, D)

        def block(tokens):
            projected = low_back(low(jnp.einsum('etf,tj->efj', tokens, proj_w, precision=highest)))
            pairwise = low_back(jnp.einsum('etf,efj->etj', tokens, projected, precision=highest).reshape(-1, NTOK * K))
            normed = low(normalize(pairwise, gain_a, bias_a))
            hidden_pre = low_back(jnp.dot(normed, up_w, precision=highest) + up_b)
            hidden = low(jax.nn.gelu(hidden_pre))
            fm_out = low_back(low(jnp.dot(hidden, down_w, precision=highest) + down_b)).reshape(-1, NF, D)
            comp_out = low_back(low(jnp.einsum('it,etf->eif', comp_w, tokens, precision=highest)))
            residual_mix = low_back(jnp.einsum('ts,esf->etf', res_w, tokens, precision=highest))
            summed = jnp.concatenate([fm_out, comp_out], axis=1) + residual_mix
            return normalize(summed, gain_b, bias_b).reshape(-1, NTOK * D)
        return lax.map(jax.checkpoint(block), feats).reshape(-1, NTOK * D)
    single = jnp.float32
    inputs = (embed_rows.astype(single), p_proj.astype(single), gain_one, bias_one, w_up.astype(single), b_up, w_down.astype(single), b_down, w_comp.astype(single), w_res.astype(single), gain_two, bias_two)
    output, back_fn = jax.vjp(forward, *inputs)
    grads = back_fn(cotangent.astype(single))
    return (output.astype(jnp.bfloat16), grads[0].astype(jnp.bfloat16), grads[1], grads[2], grads[3], grads[4], grads[5], grads[6], grads[7], grads[8], grads[9], grads[10], grads[11])
```

```python
import functools

import jax
import jax.numpy as jnp
import numpy as np
from jax import lax
from jax.experimental import pallas as pl
from jax.experimental.pallas import tpu as pltpu
from jax.sharding import PartitionSpec as P

EPS = 1e-05
GROUP = 8
BLOCK = 128
CHUNK = 256
VMEM_LIMIT = 58 * 1024 * 1024

f32 = jnp.float32
bf16 = jnp.bfloat16

NN = (((1,), (0,)), ((), ()))
NT = (((1,), (1,)), ((), ()))
TN = (((0,), (0,)), ((), ()))


def mul(left, right, dims=NN):
    return lax.dot_general(left, right, dims, preferred_element_type=f32)


def params(**more):
    return pltpu.CompilerParams(vmem_limit_bytes=VMEM_LIMIT, **more)


def one_hot(low, high):
    row = lax.broadcasted_iota(jnp.int32, (CHUNK, low.shape[1]), 0)
    inside = jnp.logical_and(row >= low, row < high)
    return jnp.where(inside, 1.0, 0.0).astype(bf16)


def turn(tile, shift):
    return pltpu.roll(tile, shift % 128, 1) if shift % 128 else tile


def tokens_kernel(
    offs, starts, ends, rows, mixer, gain, bias, xt_ref, pair_ref, normed_ref, res_ref, pair_s, nat_s
):
    step = pl.program_id(0)
    groups = xt_ref.shape[0]
    row_total = rows.shape[1]
    features = rows.shape[0]
    tokens = nat_s.shape[0]
    ranks = pair_s.shape[1] // tokens
    lanes = tokens * GROUP
    per_tile = 128 // tokens
    example = lax.broadcasted_iota(jnp.int32, (GROUP, 128), 0)
    place = lax.broadcasted_iota(jnp.int32, (GROUP, 128), 1) // tokens

    def group(i, carry):
        number = step * groups + i
        first = offs[number]
        base = (first // 128) * 128
        count = (offs[number + 1] - base + CHUNK - 1) // CHUNK
        low = starts[pl.ds(i, 1), :]
        high = ends[pl.ds(i, 1), :]

        def chunk(c, total):
            wanted = base + c * CHUNK
            at = pl.multiple_of(jnp.minimum(wanted, row_total - CHUNK), 128)
            hot = one_hot(jnp.maximum(low, wanted) - at, high - at)
            return total + mul(rows[:, pl.ds(at, CHUNK)], hot)

        x = lax.fori_loop(0, count, chunk, jnp.zeros((features, lanes), f32)).astype(bf16)
        xt_ref[i] = x
        nat = mul(mixer[...], x, NT)
        m = mul(nat[lanes:].astype(bf16), x)
        here = pl.ds(pl.multiple_of(i * GROUP, GROUP), GROUP)
        for c in range(ranks // per_tile):
            tile = None
            for s in range(per_tile):
                at = GROUP * (c * per_tile + s)
                slab = m[at : at + GROUP]
                one = jnp.where(example < per_tile, slab[:, :128], slab[:, 128:])
                one = turn(one, s * tokens)
                mine = place == (example + s) % per_tile
                tile = one if s == 0 else jnp.where(mine, one, tile)
            pair_s[here, c * 128 : c * 128 + 128] = tile
        for t in range(tokens):
            nat_s[t, here, :features] = nat[GROUP * t : GROUP * t + GROUP]
        return carry

    lax.fori_loop(0, groups, group, 0)
    pair = pair_s[...].T
    pair_ref[...] = pair
    centred = pair - jnp.mean(pair, axis=0, keepdims=True)
    scale = lax.rsqrt(jnp.mean(centred * centred, axis=0, keepdims=True) + EPS)
    normed_ref[...] = (centred * scale * gain[...] + bias[...]).astype(bf16)

    def back(t, carry):
        at = pl.ds(pl.multiple_of(t * features, 32), features)
        res_ref[at, :] = nat_s[t].T[:features]
        return carry

    lax.fori_loop(0, tokens, back, 0)


def final_kernel(with_fm, features, *refs):
    if with_fm:
        res, fm, offset, cot, gain, bias, out, gmix, gain_acc, bias_acc, down_acc, cot_s, out_s = refs
    else:
        res, cot, gain, bias, out, gmix, gain_acc, bias_acc, cot_s, out_s = refs

    @pl.when(pl.program_id(0) == 0)
    def clear():
        gain_acc[...] = jnp.zeros_like(gain_acc)
        bias_acc[...] = jnp.zeros_like(bias_acc)
        if with_fm:
            down_acc[...] = jnp.zeros_like(down_acc)

    cot_s[...] = cot[...].astype(f32).T

    def token(i, carry):
        at = pl.ds(pl.multiple_of(i * features, 32), features)
        summed = res[at, :]
        if with_fm:
            summed = summed + (fm[at, :] + offset[at, :]).astype(bf16).astype(f32)
        centred = summed - jnp.mean(summed, axis=0, keepdims=True)
        scale = lax.rsqrt(jnp.mean(centred * centred, axis=0, keepdims=True) + EPS)
        hat = centred * scale
        out_s[at, :] = hat * gain[...] + bias[...]
        g = cot_s[at, :]
        gain_acc[...] += g * hat
        bias_acc[...] += g
        q = g * gain[...]
        mean_q = jnp.mean(q, axis=0, keepdims=True)
        mean_qx = jnp.mean(q * hat, axis=0, keepdims=True)
        mix = (scale * (q - mean_q - hat * mean_qx)).astype(bf16)
        gmix[at, :] = mix
        if with_fm:
            down_acc[at, :] += mix.astype(f32)
        return carry

    lax.fori_loop(0, res.shape[0] // features, token, 0)
    out[...] = out_s[...].T.astype(bf16)


def back_kernel(
    gn, pair, gain, gmix, xt, mixer, gt, gain_acc, bias_acc, small_acc, gp_s, nat_s
):
    groups, features, lanes = xt.shape
    tokens = nat_s.shape[0]
    ranks = gp_s.shape[1] // tokens
    per_tile = 128 // tokens

    @pl.when(pl.program_id(0) == 0)
    def clear():
        gain_acc[...] = jnp.zeros_like(gain_acc)
        bias_acc[...] = jnp.zeros_like(bias_acc)
        small_acc[...] = jnp.zeros_like(small_acc)

    values = pair[...]
    centred = values - jnp.mean(values, axis=0, keepdims=True)
    scale = lax.rsqrt(jnp.mean(centred * centred, axis=0, keepdims=True) + EPS)
    hat = centred * scale
    g = gn[...]
    gain_acc[...] += g * hat
    bias_acc[...] += g
    h = g * gain[...]
    mean_h = jnp.mean(h, axis=0, keepdims=True)
    mean_hx = jnp.mean(h * hat, axis=0, keepdims=True)
    gp_s[...] = (scale * (h - mean_h - hat * mean_hx)).T

    def spread(t, carry):
        at = pl.ds(pl.multiple_of(t * features, 32), features)
        nat_s[t, :, :features] = gmix[at, :].astype(f32).T
        return carry

    lax.fori_loop(0, tokens, spread, 0)
    example = lax.broadcasted_iota(jnp.int32, (GROUP, 128), 0)
    place = lax.broadcasted_iota(jnp.int32, (GROUP, 128), 1) // tokens
    own = place == example % per_tile
    keep_low = jnp.logical_and(own, example < per_tile)
    keep_high = jnp.logical_and(own, example >= per_tile)

    def group(i, carry):
        here = pl.ds(pl.multiple_of(i * GROUP, GROUP), GROUP)
        x = xt[i]
        g_mix = nat_s[:, here, :features].reshape(tokens * GROUP, features).astype(bf16)
        slabs = []
        for j in range(ranks):
            c, s = j // per_tile, j % per_tile
            one = turn(gp_s[here, c * 128 : c * 128 + 128], -s * tokens)
            slabs.append(
                jnp.concatenate([jnp.where(keep_low, one, 0.0), jnp.where(keep_high, one, 0.0)], axis=1)
            )
        g_pair = jnp.concatenate(slabs, axis=0).astype(bf16)
        projected = mul(mixer[lanes:], x, NT).astype(bf16)
        g_projected = mul(g_pair, x, NT).astype(bf16)
        small = jnp.concatenate([g_mix, g_projected], axis=0)
        small_acc[...] += mul(small, x)
        left = jnp.concatenate([small, projected], axis=0)
        right = jnp.concatenate([mixer[...], g_pair], axis=0)
        gt[i] = mul(left, right, TN).astype(bf16)
        return carry

    lax.fori_loop(0, groups, group, 0)


def spread_kernel(first_group, starts, ends, gt, out):
    step = pl.program_id(0)
    chunks = out.shape[1] // CHUNK
    last = gt.shape[0] - 1

    def chunk(c, carry):
        number = step * chunks + c
        base = number * CHUNK
        one = first_group[number]
        two = jnp.minimum(one + 1, last)
        hot_one = one_hot(starts[pl.ds(one, 1), :] - base, ends[pl.ds(one, 1), :] - base)
        end_two = jnp.where(two > one, ends[pl.ds(two, 1), :] - base, 0)
        hot_two = one_hot(starts[pl.ds(two, 1), :] - base, end_two)
        at = pl.ds(pl.multiple_of(c * CHUNK, CHUNK), CHUNK)
        out[:, at] = (mul(gt[one], hot_one, NT) + mul(gt[two], hot_two, NT)).astype(bf16)
        return carry

    lax.fori_loop(0, chunks, chunk, 0)


def whole(shape):
    return pl.BlockSpec(shape, lambda *_: (0,) * len(shape))


def rank_of(tokens):
    per_tile = 128 // tokens
    slab, example = np.arange(per_tile)[:, None], np.arange(GROUP)[None, :]
    return np.eye(per_tile, dtype=np.float32)[(slab + example) % per_tile]


def make_mixer(w_res, w_comp, p_proj):
    tokens = w_res.shape[0]
    fm_tokens = tokens - w_comp.shape[0]
    mix = w_res.astype(f32) + jnp.pad(w_comp.astype(f32), ((fm_tokens, 0), (0, 0)))
    mix = jnp.broadcast_to(mix[:, None, :], (tokens, GROUP, tokens))
    by_tile = p_proj.T.astype(f32).reshape(-1, 128 // tokens, tokens)
    project = jnp.einsum("cqt,seq->cset", by_tile, rank_of(tokens))
    both = jnp.concatenate([mix, project.reshape(-1, GROUP, tokens)], axis=0)
    wide = both[:, :, None, :] * np.eye(GROUP, dtype=np.float32)[None, :, :, None]
    return wide.reshape(both.shape[0] * GROUP, GROUP * tokens).astype(bf16)


def token_stage(offs, starts, ends, rows, mixer, gain, bias, tokens):
    features, row_total = rows.shape
    group_count, lanes = starts.shape
    examples = group_count * GROUP
    pairs = gain.shape[0]
    groups = BLOCK // GROUP
    return pl.pallas_call(
        tokens_kernel,
        name="tokens",
        grid_spec=pltpu.PrefetchScalarGridSpec(
            num_scalar_prefetch=1,
            grid=(examples // BLOCK,),
            in_specs=[
                pl.BlockSpec((groups, lanes), lambda i, _: (i, 0)),
                pl.BlockSpec((groups, lanes), lambda i, _: (i, 0)),
                pl.BlockSpec(memory_space=pltpu.VMEM),
                whole(mixer.shape),
                whole(gain.shape),
                whole(bias.shape),
            ],
            out_specs=[
                pl.BlockSpec((groups, features, lanes), lambda i, _: (i, 0, 0)),
                pl.BlockSpec((pairs, BLOCK), lambda i, _: (0, i)),
                pl.BlockSpec((pairs, BLOCK), lambda i, _: (0, i)),
                pl.BlockSpec((tokens * features, BLOCK), lambda i, _: (0, i)),
            ],
            scratch_shapes=[
                pltpu.VMEM((BLOCK, pairs), f32),
                pltpu.VMEM((tokens, BLOCK, 256), f32),
            ],
        ),
        out_shape=[
            jax.ShapeDtypeStruct((group_count, features, lanes), bf16),
            jax.ShapeDtypeStruct((pairs, examples), f32),
            jax.ShapeDtypeStruct((pairs, examples), bf16),
            jax.ShapeDtypeStruct((tokens * features, examples), f32),
        ],
        compiler_params=params(),
        cost_estimate=pl.CostEstimate(
            flops=2 * features * lanes * (row_total * 2 + 1000 * group_count),
            bytes_accessed=row_total * features * 2 + 30 * examples * 1024,
            transcendentals=0,
        ),
    )(offs, starts, ends, rows, mixer, gain, bias)


def final_stage(res, fm, offset, cot, gain, bias, features, half, previous):
    width, examples = res.shape
    part = width // 2
    with_fm = fm is not None
    tall = pl.BlockSpec((part, BLOCK), lambda i: (0, i))
    flat = pl.BlockSpec((BLOCK, part), lambda i: (i, half))
    in_specs = [pl.BlockSpec((part, BLOCK), lambda i: (half, i))]
    operands = [res]
    if with_fm:
        in_specs += [tall, whole(offset.shape)]
        operands += [fm, offset]
    in_specs += [flat, whole(gain.shape), whole(bias.shape)]
    operands += [cot, gain, bias]
    out_specs = [flat, tall, whole((features, BLOCK)), whole((features, BLOCK))]
    out_shape = [
        jax.ShapeDtypeStruct((examples, width), bf16),
        jax.ShapeDtypeStruct((part, examples), bf16),
        jax.ShapeDtypeStruct((features, BLOCK), f32),
        jax.ShapeDtypeStruct((features, BLOCK), f32),
    ]
    if with_fm:
        out_specs.append(whole((part, BLOCK)))
        out_shape.append(jax.ShapeDtypeStruct((part, BLOCK), f32))
    kernel = functools.partial(final_kernel, with_fm, features)
    aliases = {}
    if previous is not None:
        in_specs.append(pl.BlockSpec(memory_space=pl.ANY))
        operands.append(previous)
        aliases = {len(operands) - 1: 0}
        inner, at = kernel, len(operands) - 1
        kernel = lambda *refs: inner(*refs[:at], *refs[at + 1 :])
    return pl.pallas_call(
        kernel,
        name="final_fm" if with_fm else "final_comp",
        grid=(examples // BLOCK,),
        in_specs=in_specs,
        out_specs=out_specs,
        out_shape=out_shape,
        scratch_shapes=[pltpu.VMEM((part, BLOCK), f32), pltpu.VMEM((part, BLOCK), f32)],
        input_output_aliases=aliases,
        compiler_params=params(),
        cost_estimate=pl.CostEstimate(
            flops=200 * part * examples, bytes_accessed=12 * part * examples, transcendentals=0
        ),
    )(*operands)


def back_stage(gn, pair, gain, gmix, xt, mixer, tokens):
    pairs, examples = pair.shape
    group_count, features, lanes = xt.shape
    groups = BLOCK // GROUP
    wide = pl.BlockSpec((pairs, BLOCK), lambda i: (0, i))
    ranks = pairs // tokens
    return pl.pallas_call(
        back_kernel,
        name="back",
        grid=(examples // BLOCK,),
        in_specs=[
            wide,
            wide,
            whole(gain.shape),
            pl.BlockSpec((tokens * features, BLOCK), lambda i: (0, i)),
            pl.BlockSpec((groups, features, lanes), lambda i: (i, 0, 0)),
            whole(mixer.shape),
        ],
        out_specs=[
            pl.BlockSpec((groups, features, lanes), lambda i: (i, 0, 0)),
            whole((pairs, BLOCK)),
            whole((pairs, BLOCK)),
            whole(mixer.shape),
        ],
        out_shape=[
            jax.ShapeDtypeStruct((group_count, features, lanes), bf16),
            jax.ShapeDtypeStruct((pairs, BLOCK), f32),
            jax.ShapeDtypeStruct((pairs, BLOCK), f32),
            jax.ShapeDtypeStruct(mixer.shape, f32),
        ],
        scratch_shapes=[
            pltpu.VMEM((BLOCK, pairs), f32),
            pltpu.VMEM((tokens, BLOCK, 256), f32),
        ],
        compiler_params=params(),
        cost_estimate=pl.CostEstimate(
            flops=2 * features * lanes * 2000 * group_count,
            bytes_accessed=40 * examples * 1024,
            transcendentals=0,
        ),
    )(gn, pair, gain, gmix, xt, mixer)


def spread_stage(offs, starts, ends, gt, row_total):
    group_count, features, lanes = gt.shape
    step_rows = CHUNK * 8
    while row_total % step_rows != 0:
        step_rows = step_rows // 2
    bases = jnp.arange(row_total // CHUNK, dtype=jnp.int32) * CHUNK
    first_group = jnp.sum((offs[1:][None, :] <= bases[:, None]).astype(jnp.int32), axis=1)
    return pl.pallas_call(
        spread_kernel,
        name="spread",
        grid_spec=pltpu.PrefetchScalarGridSpec(
            num_scalar_prefetch=1,
            grid=(row_total // step_rows,),
            in_specs=[
                whole(starts.shape),
                whole(ends.shape),
                whole(gt.shape),
            ],
            out_specs=pl.BlockSpec((features, step_rows), lambda i, _: (0, i)),
        ),
        out_shape=jax.ShapeDtypeStruct((features, row_total), bf16),
        compiler_params=params(),
        cost_estimate=pl.CostEstimate(
            flops=4 * features * lanes * row_total,
            bytes_accessed=row_total * features * 4,
            transcendentals=0,
        ),
    )(first_group, starts, ends, gt)


def bag_bounds(lengths):
    ends = jnp.cumsum(lengths.reshape(-1))
    starts = ends - lengths.reshape(-1)
    return starts, ends


def column(vector, lanes=BLOCK):
    return jnp.broadcast_to(vector[:, None], (vector.shape[0], lanes))


def gelu(v):
    inner = np.sqrt(2 / np.pi).astype(np.float32) * (v + 0.044715 * (v * v * v))
    return 0.5 * v * (1.0 + jnp.tanh(inner))


def gelu_slope(v):
    root = np.sqrt(2 / np.pi).astype(np.float32)
    bent = jnp.tanh(root * (v + 0.044715 * (v * v * v)))
    return 0.5 * (1.0 + bent) + 0.5 * v * (1.0 - bent * bent) * root * (1.0 + 3 * 0.044715 * (v * v))


def shards(
    embed_rows,
    lengths,
    cotangent,
    p_proj,
    gain_one,
    bias_one,
    w_up,
    b_up,
    w_down,
    b_down,
    w_comp,
    w_res,
    gain_two,
    bias_two,
    gather=None,
    scatter=None,
    reduce=None,
):
    tokens = w_res.shape[0]
    features = embed_rows.shape[1]
    ranks = p_proj.shape[1]
    pairs = tokens * ranks
    row_total = embed_rows.shape[0]
    fm_width = b_down.shape[0]

    def by_rank(vector):
        return jnp.swapaxes(vector.reshape(-1, tokens, ranks), 1, 2).reshape(vector.shape)

    def by_token(vector):
        return jnp.swapaxes(vector.reshape(-1, ranks, tokens), 1, 2).reshape(vector.shape)

    own = jnp.concatenate([by_rank(w_up.T), w_down], axis=1)
    every = gather(own)
    full_up, full_down = every[:, :pairs], every[:, pairs:]

    starts, ends = bag_bounds(lengths)
    lanes = GROUP * tokens
    starts = starts.reshape(-1, lanes)
    ends = ends.reshape(-1, lanes)
    offs = jnp.concatenate([starts[:, 0], ends[-1:, -1]])
    mixer = make_mixer(w_res, w_comp, p_proj)
    gain_a, bias_a = column(by_rank(gain_one)), column(by_rank(bias_one))
    gain_b, bias_b = column(gain_two), column(bias_two)

    xt, pair, normed, res = token_stage(
        offs, starts, ends, embed_rows.T, mixer, gain_a, bias_a, tokens
    )
    out, mix_comp, gain_acc1, bias_acc1 = final_stage(
        res, None, None, cotangent, gain_b, bias_b, features, 1, None
    )
    hidden_pre = mul(full_up, normed) + b_up[:, None]
    hidden = gelu(hidden_pre).astype(bf16)
    fm = mul(full_down, hidden, TN)
    out, mix_fm, gain_acc0, bias_acc0, down_acc = final_stage(
        res, fm, column(b_down), cotangent, gain_b, bias_b, features, 0, out
    )
    down_grad = mul(hidden, mix_fm, NT).astype(bf16)
    down_grad = scatter(down_grad)
    g_hidden = mul(full_down, mix_fm)
    g_pre = (g_hidden * gelu_slope(hidden_pre)).astype(bf16)
    up_grad = mul(g_pre, normed, NT).astype(bf16)
    up_grad = scatter(up_grad)
    b_up_grad = jnp.sum(g_pre.astype(f32), axis=1)
    g_normed = mul(full_up, g_pre, TN)
    mix = jnp.concatenate([mix_fm, mix_comp], axis=0)
    gt, gain_acc, bias_acc, small_acc = back_stage(g_normed, pair, gain_a, mix, xt, mixer, tokens)
    rows_grad = spread_stage(offs, starts, ends, gt, row_total).T

    cells = small_acc.reshape(tokens + ranks, GROUP, GROUP, tokens)
    cells = jnp.einsum("aeet->aet", cells)
    by_slab = cells[tokens:].reshape(-1, 128 // tokens, GROUP, tokens)
    proj_grad = jnp.einsum("cset,seq->tcq", by_slab, rank_of(tokens), precision=lax.Precision.HIGHEST)
    small = [
        proj_grad.reshape(-1),
        by_token(jnp.sum(gain_acc, axis=1)),
        by_token(jnp.sum(bias_acc, axis=1)),
        b_up_grad,
        jnp.sum(down_acc, axis=1),
        jnp.sum(cells[:tokens], axis=1).reshape(-1),
        jnp.sum(gain_acc0 + gain_acc1, axis=1),
        jnp.sum(bias_acc0 + bias_acc1, axis=1),
    ]
    sizes = np.cumsum([part.shape[0] for part in small])[:-1]
    parts = jnp.split(reduce(jnp.concatenate(small)), sizes)
    res_grad = parts[5].reshape(tokens, tokens)
    return (
        out,
        rows_grad,
        parts[0].reshape(tokens, ranks),
        parts[1],
        parts[2],
        by_token(up_grad.astype(f32)).T,
        parts[3],
        down_grad.astype(f32),
        parts[4],
        res_grad[tokens - w_comp.shape[0] :],
        res_grad,
        parts[6],
        parts[7],
    )


def gather_hidden(own):
    return lax.all_gather(own, "dp", axis=0, tiled=True)


def scatter_hidden(partial):
    mine = lax.psum_scatter(partial, "dp", scatter_dimension=0, tiled=True)
    return lax.psum(mine, "branch")


def reduce_small(vector):
    return lax.psum(vector, ("dp", "branch"))


def solution(mesh):
    spread = P(("dp", "branch"), None)
    in_specs = (
        spread,
        spread,
        spread,
        P(),
        P(),
        P(),
        P(None, "dp"),
        P(),
        P("dp", None),
        P(),
        P(),
        P(),
        P(),
        P(),
    )
    out_specs = (
        spread,
        spread,
        P(),
        P(),
        P(),
        P(None, "dp"),
        P(),
        P("dp", None),
        P(),
        P(),
        P(),
        P(),
        P(),
    )
    body = functools.partial(
        shards, gather=gather_hidden, scatter=scatter_hidden, reduce=reduce_small
    )
    return jax.shard_map(body, mesh=mesh, in_specs=in_specs, out_specs=out_specs, check_vma=False)
```

```python
import functools

import jax
import jax.numpy as jnp
import numpy as np
from jax import lax
from jax.experimental import pallas as pl
from jax.experimental.pallas import tpu as pltpu
from jax.sharding import PartitionSpec as P

EPS = 1e-05
GROUP = 8
BLOCK = 128
CHUNK = 256
UNROLL = 4
SPREAD_ROWS = 8 * CHUNK
VMEM_LIMIT = 63 * 1000 * 1000

f32 = jnp.float32
bf16 = jnp.bfloat16

NN = (((1,), (0,)), ((), ()))
NT = (((1,), (1,)), ((), ()))
TN = (((0,), (0,)), ((), ()))


def mul(left, right, dims=NN):
    return lax.dot_general(left, right, dims, preferred_element_type=f32)


def params(**more):
    return pltpu.CompilerParams(vmem_limit_bytes=VMEM_LIMIT, **more)


def one_hot(low, high, rows):
    row = lax.broadcasted_iota(jnp.int16, (rows, low.shape[1]), 0)
    inside = jnp.logical_and(row >= low.astype(jnp.int16), row < high.astype(jnp.int16))
    return jnp.where(inside, jnp.ones((), bf16), jnp.zeros((), bf16))


def turn(tile, shift):
    return pltpu.roll(tile, shift % 128, 1) if shift % 128 else tile


def tokens_kernel(
    offs, starts, ends, rows, mixer, gain, bias, xt_ref, pair_ref, normed_ref, res_ref, pair_s, nat_s, sum_s
):
    step = pl.program_id(0)
    groups = xt_ref.shape[0]
    row_total = rows.shape[1]
    features = rows.shape[0]
    tokens = nat_s.shape[0]
    ranks = pair_s.shape[1] // tokens
    lanes = tokens * GROUP
    per_tile = 128 // tokens
    span = 2 * CHUNK
    example = lax.broadcasted_iota(jnp.int32, (GROUP, 128), 0)
    place = lax.broadcasted_iota(jnp.int32, (GROUP, 128), 1) // tokens

    def some(k, carry):
        todo = [k * UNROLL + u for u in range(UNROLL)]
        bases = []
        for u, i in enumerate(todo):
            first = offs[step * groups + i]
            base = (first // 128) * 128
            bases.append(base)
            low = starts[pl.ds(i, 1), :]
            high = ends[pl.ds(i, 1), :]
            at = pl.multiple_of(jnp.minimum(base, row_total - span), 128)
            sum_s[u] = mul(rows[:, pl.ds(at, span)], one_hot(low - at, high - at, span))
        for u, i in enumerate(todo):
            base = bases[u] + span
            left = offs[step * groups + i + 1] - base

            @pl.when(left > 0)
            def more(u=u, i=i, base=base, left=left):
                low = starts[pl.ds(i, 1), :]
                high = ends[pl.ds(i, 1), :]

                def chunk(c, total):
                    wanted = base + c * CHUNK
                    at = pl.multiple_of(jnp.minimum(wanted, row_total - CHUNK), 128)
                    hot = one_hot(jnp.maximum(low, wanted) - at, high - at, CHUNK)
                    return total + mul(rows[:, pl.ds(at, CHUNK)], hot)

                sum_s[u] = lax.fori_loop(0, (left + CHUNK - 1) // CHUNK, chunk, sum_s[u])

        for u, i in enumerate(todo):
            x = sum_s[u].astype(bf16)
            xt_ref[i] = x
            nat = mul(mixer[...], x, NT)
            m = mul(nat[lanes:].astype(bf16), x)
            here = pl.ds(pl.multiple_of(i * GROUP, GROUP), GROUP)
            for c in range(ranks // per_tile):
                tile = None
                for s in range(per_tile):
                    at = GROUP * (c * per_tile + s)
                    slab = m[at : at + GROUP]
                    one = jnp.where(example < per_tile, slab[:, :128], slab[:, 128:])
                    one = turn(one, s * tokens)
                    mine = place == (example + s) % per_tile
                    tile = one if s == 0 else jnp.where(mine, one, tile)
                pair_s[here, c * 128 : c * 128 + 128] = tile
            for t in range(tokens):
                nat_s[t, here, :features] = nat[GROUP * t : GROUP * t + GROUP]
        return carry

    lax.fori_loop(0, groups // UNROLL, some, 0)
    pair = pair_s[...].T
    pair_ref[...] = pair
    centred = pair - jnp.mean(pair, axis=0, keepdims=True)
    scale = lax.rsqrt(jnp.mean(centred * centred, axis=0, keepdims=True) + EPS)
    normed_ref[...] = (centred * scale * gain[...] + bias[...]).astype(bf16)

    def back(k, carry):
        for u in range(4):
            t = k * 4 + u
            at = pl.ds(pl.multiple_of(t * features, 32), features)
            res_ref[at, :] = nat_s[t].astype(bf16).T[:features]
        return carry

    lax.fori_loop(0, tokens // 4, back, 0)


def norm_token(summed, g, gain, bias):
    centred = summed - jnp.mean(summed, axis=0, keepdims=True)
    scale = lax.rsqrt(jnp.mean(centred * centred, axis=0, keepdims=True) + EPS)
    hat = centred * scale
    q = g * gain
    g_hat = g * hat
    mean_q = jnp.mean(q, axis=0, keepdims=True)
    mean_qx = jnp.mean(q * hat, axis=0, keepdims=True)
    return (hat * gain + bias).astype(bf16), (scale * (q - mean_q - hat * mean_qx)).astype(bf16), g_hat


def folded(value):
    return sum(value[:, i : i + 128] for i in range(0, value.shape[1], 128))


def doubled(value, lanes):
    return jnp.concatenate([value] * (lanes // value.shape[1]), axis=1)


def final_kernel(features, res, cot, gain, bias, out, gmix, gain_acc, bias_acc, cot_s, out_s):
    @pl.when(pl.program_id(0) == 0)
    def clear():
        gain_acc[...] = jnp.zeros_like(gain_acc)
        bias_acc[...] = jnp.zeros_like(bias_acc)

    cot_s[...] = cot[...].T
    unroll = 4

    def some(k, carry):
        hats, gs = [], []
        for u in range(unroll):
            at = pl.ds(pl.multiple_of((k * unroll + u) * features, 32), features)
            g = cot_s[at, :].astype(f32)
            out_s[at, :], gmix[at, :], g_hat = norm_token(res[at, :].astype(f32), g, gain[...], bias[...])
            hats.append(g_hat)
            gs.append(g)
        gain_acc[...] += sum(hats)
        bias_acc[...] += sum(gs)
        return carry

    lax.fori_loop(0, res.shape[0] // features // unroll, some, 0)
    out[...] = out_s[...].T


def mlp_kernel(
    features,
    every,
    normed,
    res,
    cot,
    b_up,
    b_down,
    gain,
    bias,
    out,
    mix,
    hidden,
    g_pre,
    g_normed,
    gain_acc,
    bias_acc,
    up_acc,
    down_acc,
    pre_s,
    fm_s,
    cot_s,
    out_s,
):
    pairs, lanes = normed.shape
    units = hidden.shape[0]
    width = res.shape[0]
    unit_tile = 256
    token_tile = 4 * features

    @pl.when(pl.program_id(0) == 0)
    def clear():
        for acc in (gain_acc, bias_acc, up_acc, down_acc):
            acc[...] = jnp.zeros_like(acc)

    cot_s[...] = cot[...].T
    for at in range(0, units, unit_tile):
        here = slice(at, at + unit_tile)
        pre = mul(every[here, :pairs], normed[...]) + doubled(b_up[here, :], lanes)
        pre_s[here, :] = pre
        hidden[here, :] = gelu(pre).astype(bf16)
    wide_gain, wide_bias = doubled(gain[...], lanes), doubled(bias[...], lanes)
    for first in range(0, width, token_tile):
        fm_s[...] = mul(every[:, pairs + first : pairs + first + token_tile], hidden[...], TN)
        hats, gs = [], []
        for u in range(4):
            here = slice(first + u * features, first + (u + 1) * features)
            fm = fm_s[u * features : (u + 1) * features, :] + doubled(b_down[here, :], lanes)
            g = cot_s[here, :].astype(f32)
            summed = res[here, :].astype(f32) + fm.astype(bf16).astype(f32)
            out_s[here, :], g_mix, g_hat = norm_token(summed, g, wide_gain, wide_bias)
            mix[here, :] = g_mix
            down_acc[here, :] += folded(g_mix.astype(f32))
            hats.append(folded(g_hat))
            gs.append(folded(g))
        gain_acc[...] += sum(hats)
        bias_acc[...] += sum(gs)
    for at in range(0, units, unit_tile):
        here = slice(at, at + unit_tile)
        g_hidden = mul(every[here, pairs:], mix[...])
        value = (g_hidden * gelu_slope(pre_s[here, :])).astype(bf16)
        g_pre[here, :] = value
        up_acc[here, :] += folded(value.astype(f32))
    g_normed[...] = mul(every[:, :pairs], g_pre[...], TN)
    out[...] = out_s[...].T


def back_kernel(gn, pair, gain, gmix, xt, mixer, *refs):
    *before, gt, gain_acc, bias_acc, mix_acc, project_acc, gp_s, nat_s = refs
    sums = (gain_acc, bias_acc, mix_acc, project_acc)
    groups, features, lanes = xt.shape
    tokens = nat_s.shape[0]
    ranks = gp_s.shape[1] // tokens
    per_tile = 128 // tokens

    @pl.when(pl.program_id(0) == 0)
    def clear():
        for i, acc in enumerate(sums):
            acc[...] = before[i][...] if before else jnp.zeros_like(acc)

    values = pair[...]
    centred = values - jnp.mean(values, axis=0, keepdims=True)
    scale = lax.rsqrt(jnp.mean(centred * centred, axis=0, keepdims=True) + EPS)
    hat = centred * scale
    g = gn[...]
    gain_acc[...] += g * hat
    bias_acc[...] += g
    h = g * gain[...]
    mean_h = jnp.mean(h, axis=0, keepdims=True)
    mean_hx = jnp.mean(h * hat, axis=0, keepdims=True)
    gp_s[...] = (scale * (h - mean_h - hat * mean_hx)).T

    def spread(k, carry):
        for u in range(4):
            t = k * 4 + u
            at = pl.ds(pl.multiple_of(t * features, 32), features)
            nat_s[t, :, :features] = gmix[at, :].T
        return carry

    lax.fori_loop(0, tokens // 4, spread, 0)
    example = lax.broadcasted_iota(jnp.int32, (GROUP, 128), 0)
    place = lax.broadcasted_iota(jnp.int32, (GROUP, 128), 1) // tokens
    own = place == example % per_tile
    keep_low = jnp.logical_and(own, example < per_tile)
    keep_high = jnp.logical_and(own, example >= per_tile)

    def some(k, carry):
        pairs_here = []
        for u in range(UNROLL // 2):
            both = pl.ds(pl.multiple_of((k * UNROLL + 2 * u) * GROUP, 2 * GROUP), 2 * GROUP)
            mixes = nat_s[:, both, :features].astype(f32)
            pairs_here += [mixes[:, :GROUP], mixes[:, GROUP:]]
        project = mixer[lanes:]
        four = pl.ds(pl.multiple_of(k * UNROLL, UNROLL), UNROLL)
        stacked = xt[four].reshape(UNROLL * features, lanes)
        projected = mul(stacked, project, NT).astype(bf16)
        g_pairs, g_parts = [], []
        mix_total = mix_acc[...]
        for u in range(UNROLL):
            here = pl.ds(pl.multiple_of((k * UNROLL + u) * GROUP, GROUP), GROUP)
            slabs = []
            for j in range(ranks):
                c, s = j // per_tile, j % per_tile
                one = turn(gp_s[here, c * 128 : c * 128 + 128], -s * tokens)
                slabs.append(
                    jnp.concatenate([jnp.where(keep_low, one, 0.0), jnp.where(keep_high, one, 0.0)], axis=1)
                )
            g_pairs.append(jnp.concatenate(slabs, axis=0).astype(bf16))
            g_parts.append(mul(xt[k * UNROLL + u], g_pairs[u], NT).astype(bf16))
        g_projected = jnp.concatenate(g_parts, axis=0)
        project_acc[...] += mul(stacked, g_projected, TN)
        shared = mul(g_projected, project)
        for u in range(UNROLL):
            g_mix = pairs_here[u].reshape(tokens * GROUP, features).astype(bf16)
            mix_total = mix_total + mul(g_mix, xt[k * UNROLL + u])
            rows = slice(u * features, (u + 1) * features)
            part = mul(projected[rows], g_pairs[u]) + mul(g_mix, mixer[:lanes], TN)
            gt[k * UNROLL + u] = (shared[rows] + part).astype(bf16)
        mix_acc[...] = mix_total
        return carry

    lax.fori_loop(0, groups // UNROLL, some, 0)


def spread_kernel(start, first_group, starts, ends, gt, out, window_s, semaphores):
    step = pl.program_id(0)
    chunks = out.shape[1] // CHUNK
    window = window_s.shape[1]
    last = gt.shape[0] - 1

    def window_of(i):
        return jnp.minimum(first_group[(start + i) * chunks], last + 1 - window)

    def fetch(i):
        slot = i % 2
        source = gt.at[pl.ds(window_of(i), window)]
        return pltpu.make_async_copy(source, window_s.at[slot], semaphores.at[slot])

    @pl.when(step == 0)
    def begin():
        fetch(step).start()

    @pl.when(step + 1 < pl.num_programs(0))
    def ahead():
        fetch(step + 1).start()

    fetch(step).wait()
    origin = window_of(step)
    slot = step % 2

    def some(k, carry):
        for u in range(UNROLL):
            c = k * UNROLL + u
            number = (start + step) * chunks + c
            base = number * CHUNK
            one = first_group[number]
            two = jnp.minimum(one + 1, last)
            hot_one = one_hot(starts[pl.ds(one, 1), :] - base, ends[pl.ds(one, 1), :] - base, CHUNK)
            end_two = jnp.where(two > one, ends[pl.ds(two, 1), :] - base, 0)
            hot_two = one_hot(starts[pl.ds(two, 1), :] - base, end_two, CHUNK)
            at = pl.ds(pl.multiple_of(c * CHUNK, CHUNK), CHUNK)
            part_one = mul(window_s[slot, one - origin], hot_one, NT)
            part_two = mul(window_s[slot, two - origin], hot_two, NT)
            out[:, at] = (part_one + part_two).astype(bf16)
        return carry

    lax.fori_loop(0, chunks // UNROLL, some, 0)


def passing(kernel, given, previous):
    if not previous:
        return kernel, {}
    more = len(previous)
    skip = lambda *refs: kernel(*refs[:given], *refs[given + more :])
    return skip, {given + i: i for i in range(more)}


def whole(shape):
    return pl.BlockSpec(shape, lambda *_: (0,) * len(shape))


def rank_of(tokens):
    per_tile = 128 // tokens
    slab, example = np.arange(per_tile)[:, None], np.arange(GROUP)[None, :]
    return np.eye(per_tile, dtype=np.float32)[(slab + example) % per_tile]


def make_mixer(w_res, w_comp, p_proj):
    tokens = w_res.shape[0]
    fm_tokens = tokens - w_comp.shape[0]
    mix = w_res.astype(f32) + jnp.pad(w_comp.astype(f32), ((fm_tokens, 0), (0, 0)))
    mix = jnp.broadcast_to(mix[:, None, :], (tokens, GROUP, tokens))
    by_tile = p_proj.T.astype(f32).reshape(-1, 128 // tokens, tokens)
    project = jnp.einsum("cqt,seq->cset", by_tile, rank_of(tokens))
    both = jnp.concatenate([mix, project.reshape(-1, GROUP, tokens)], axis=0)
    wide = both[:, :, None, :] * np.eye(GROUP, dtype=np.float32)[None, :, :, None]
    return wide.reshape(both.shape[0] * GROUP, GROUP * tokens).astype(bf16)


def token_stage(offs, starts, ends, rows, mixer, gain, bias, tokens):
    features, row_total = rows.shape
    group_count, lanes = starts.shape
    examples = group_count * GROUP
    pairs = gain.shape[0]
    groups = BLOCK // GROUP
    return pl.pallas_call(
        tokens_kernel,
        name="tokens",
        grid_spec=pltpu.PrefetchScalarGridSpec(
            num_scalar_prefetch=1,
            grid=(examples // BLOCK,),
            in_specs=[
                pl.BlockSpec((groups, lanes), lambda i, _: (i, 0)),
                pl.BlockSpec((groups, lanes), lambda i, _: (i, 0)),
                pl.BlockSpec(memory_space=pltpu.VMEM),
                whole(mixer.shape),
                whole(gain.shape),
                whole(bias.shape),
            ],
            out_specs=[
                pl.BlockSpec((groups, features, lanes), lambda i, _: (i, 0, 0)),
                pl.BlockSpec((pairs, BLOCK), lambda i, _: (0, i)),
                pl.BlockSpec((pairs, BLOCK), lambda i, _: (0, i)),
                pl.BlockSpec((tokens * features, BLOCK), lambda i, _: (0, i)),
            ],
            scratch_shapes=[
                pltpu.VMEM((BLOCK, pairs), f32),
                pltpu.VMEM((tokens, BLOCK, 256), f32),
                pltpu.VMEM((UNROLL, features, lanes), f32),
            ],
        ),
        out_shape=[
            jax.ShapeDtypeStruct((group_count, features, lanes), bf16),
            jax.ShapeDtypeStruct((pairs, examples), f32),
            jax.ShapeDtypeStruct((pairs, examples), bf16),
            jax.ShapeDtypeStruct((tokens * features, examples), bf16),
        ],
        compiler_params=params(),
        cost_estimate=pl.CostEstimate(
            flops=2 * features * lanes * (row_total * 2 + 1000 * group_count),
            bytes_accessed=row_total * features * 2 + 30 * examples * 1024,
            transcendentals=0,
        ),
    )(offs, starts, ends, rows, mixer, gain, bias)


def final_stage(res, cot, gain, bias, features, part):
    width, examples = res.shape
    at = (width - part) // part
    tall = pl.BlockSpec((part, BLOCK), lambda i: (at, i))
    flat = pl.BlockSpec((BLOCK, part), lambda i: (i, at))
    return pl.pallas_call(
        functools.partial(final_kernel, features),
        name="final_comp",
        grid=(examples // BLOCK,),
        in_specs=[tall, flat, whole(gain.shape), whole(bias.shape)],
        out_specs=[flat, tall, whole((features, BLOCK)), whole((features, BLOCK))],
        out_shape=[
            jax.ShapeDtypeStruct((examples, width), bf16),
            jax.ShapeDtypeStruct((width, examples), bf16),
            jax.ShapeDtypeStruct((features, BLOCK), f32),
            jax.ShapeDtypeStruct((features, BLOCK), f32),
        ],
        scratch_shapes=[pltpu.VMEM((part, BLOCK), bf16), pltpu.VMEM((part, BLOCK), bf16)],
        compiler_params=params(),
        cost_estimate=pl.CostEstimate(
            flops=200 * part * examples, bytes_accessed=8 * part * examples, transcendentals=0
        ),
    )(res, cot, gain, bias)


def mlp_stage(every, normed, res, cot, b_up, b_down, gain, bias, features, previous):
    units, columns = every.shape
    pairs, examples = normed.shape
    part = columns - pairs
    lanes = 2 * BLOCK
    wide = lambda rows: pl.BlockSpec((rows, lanes), lambda i: (0, i))
    flat = pl.BlockSpec((lanes, part), lambda i: (i, 0))
    operands = (every, normed, res, cot, b_up, b_down, gain, bias)
    kernel, aliases = passing(functools.partial(mlp_kernel, features), len(operands), previous)
    return pl.pallas_call(
        kernel,
        name="mlp",
        grid=(examples // lanes,),
        in_specs=[
            pl.BlockSpec(memory_space=pltpu.VMEM),
            wide(pairs),
            wide(part),
            flat,
            whole(b_up.shape),
            whole(b_down.shape),
            whole(gain.shape),
            whole(bias.shape),
        ]
        + [pl.BlockSpec(memory_space=pl.ANY)] * len(previous),
        out_specs=[
            flat,
            wide(part),
            wide(units),
            wide(units),
            wide(pairs),
            whole((features, BLOCK)),
            whole((features, BLOCK)),
            whole((units, BLOCK)),
            whole((part, BLOCK)),
        ],
        out_shape=[
            jax.ShapeDtypeStruct(previous[0].shape, bf16),
            jax.ShapeDtypeStruct(previous[1].shape, bf16),
            jax.ShapeDtypeStruct((units, examples), bf16),
            jax.ShapeDtypeStruct((units, examples), bf16),
            jax.ShapeDtypeStruct((pairs, examples), f32),
            jax.ShapeDtypeStruct((features, BLOCK), f32),
            jax.ShapeDtypeStruct((features, BLOCK), f32),
            jax.ShapeDtypeStruct((units, BLOCK), f32),
            jax.ShapeDtypeStruct((part, BLOCK), f32),
        ],
        scratch_shapes=[
            pltpu.VMEM((units, lanes), f32),
            pltpu.VMEM((4 * features, lanes), f32),
            pltpu.VMEM((part, lanes), bf16),
            pltpu.VMEM((part, lanes), bf16),
        ],
        input_output_aliases=aliases,
        compiler_params=params(),
        cost_estimate=pl.CostEstimate(
            flops=4 * units * columns * examples,
            bytes_accessed=2 * units * columns + 20 * part * examples,
            transcendentals=2 * units * examples,
        ),
    )(*operands, *previous)


def back_stage(gn, pair, gain, gmix, xt, mixer, tokens, start, count, previous):
    pairs, examples = pair.shape
    group_count, features, lanes = xt.shape
    groups = BLOCK // GROUP
    ranked = mixer.shape[0] - lanes
    wide = pl.BlockSpec((pairs, BLOCK), lambda i: (0, start + i))
    by_group = pl.BlockSpec((groups, features, lanes), lambda i: (start + i, 0, 0))
    sums = [(pairs, BLOCK), (pairs, BLOCK), (lanes, lanes), (lanes, ranked)]
    before = list(previous[1:])
    operands = (gn, pair, gain, gmix, xt, mixer, *before)
    kernel, aliases = passing(back_kernel, len(operands), previous[:1])
    return pl.pallas_call(
        kernel,
        name="back",
        grid=(count,),
        in_specs=[
            wide,
            wide,
            whole(gain.shape),
            pl.BlockSpec((tokens * features, BLOCK), lambda i: (0, start + i)),
            by_group,
            whole(mixer.shape),
        ]
        + [whole(item.shape) for item in before]
        + [pl.BlockSpec(memory_space=pl.ANY)] * len(previous[:1]),
        out_specs=[by_group] + [whole(shape) for shape in sums],
        out_shape=[jax.ShapeDtypeStruct((group_count, features, lanes), bf16)]
        + [jax.ShapeDtypeStruct(shape, f32) for shape in sums],
        scratch_shapes=[
            pltpu.VMEM((BLOCK, pairs), f32),
            pltpu.VMEM((tokens, BLOCK, 256), bf16),
        ],
        input_output_aliases=aliases,
        compiler_params=params(),
        cost_estimate=pl.CostEstimate(
            flops=2 * features * lanes * 2000 * groups * count,
            bytes_accessed=40 * BLOCK * count * 1024,
            transcendentals=0,
        ),
    )(*operands, *previous[:1])


def grad_kernel(rows, table, pre, hidden, normed, mix, out):
    pairs = normed.shape[0]
    shards = out.shape[0] // rows
    first = pl.program_id(0) * shards

    def gathered(ref):
        starts = [pl.multiple_of(table[first + i] * rows, rows) for i in range(shards)]
        return jnp.concatenate([ref[pl.ds(start, rows), :] for start in starts], axis=0)

    out[:, :pairs] = mul(gathered(pre), normed[...], NT).astype(bf16)
    out[:, pairs:] = mul(gathered(hidden), mix[...], NT).astype(bf16)


def grad_stage(table, pre, hidden, normed, mix, fm_width, rows):
    count = table.shape[0]
    units, examples = hidden.shape
    pairs = normed.shape[0]
    columns = pairs + fm_width
    if rows % 16 != 0:
        pick = lambda value: value.reshape(-1, rows, examples)[table].reshape(-1, examples)
        pre, hidden, table = pick(pre), pick(hidden), jnp.arange(count * rows // 16, dtype=jnp.int32)
        return grad_stage(table, pre, hidden, normed, mix, fm_width, 16).reshape(count, rows, columns)
    shards = count
    while shards % 2 == 0 and shards * rows > 384:
        shards = shards // 2
    out = pl.pallas_call(
        functools.partial(grad_kernel, rows),
        name="weight_grads",
        grid_spec=pltpu.PrefetchScalarGridSpec(
            num_scalar_prefetch=1,
            grid=(count // shards,),
            in_specs=[
                whole(pre.shape),
                whole(hidden.shape),
                whole(normed.shape),
                whole((fm_width, examples)),
            ],
            out_specs=pl.BlockSpec((shards * rows, columns), lambda i, _: (i, 0)),
        ),
        out_shape=jax.ShapeDtypeStruct((count * rows, columns), bf16),
        compiler_params=params(),
        cost_estimate=pl.CostEstimate(
            flops=2 * count * rows * examples * columns,
            bytes_accessed=2 * count * rows * columns + 2 * examples * (2 * units + columns),
            transcendentals=0,
        ),
    )(table, pre, hidden, normed, mix)
    return out.reshape(count, rows, columns)


def spread_stage(first_group, starts, ends, gt, row_total, start, count, previous):
    group_count, features, lanes = gt.shape
    operands = (starts, ends, gt)
    window = min(group_count, -(-SPREAD_ROWS // lanes) + 2)
    kernel, aliases = passing(functools.partial(spread_kernel, start), len(operands) + 1, previous)
    return pl.pallas_call(
        kernel,
        name="spread",
        grid_spec=pltpu.PrefetchScalarGridSpec(
            num_scalar_prefetch=1,
            grid=(count,),
            in_specs=[
                whole(starts.shape),
                whole(ends.shape),
                pl.BlockSpec(memory_space=pl.ANY),
            ]
            + [pl.BlockSpec(memory_space=pl.ANY)] * len(previous),
            out_specs=pl.BlockSpec((features, SPREAD_ROWS), lambda i, _: (0, start + i)),
            scratch_shapes=[
                pltpu.VMEM((2, window, features, lanes), bf16),
                pltpu.SemaphoreType.DMA((2,)),
            ],
        ),
        out_shape=jax.ShapeDtypeStruct((features, row_total), bf16),
        input_output_aliases=aliases,
        compiler_params=params(),
        cost_estimate=pl.CostEstimate(
            flops=4 * features * lanes * SPREAD_ROWS * count,
            bytes_accessed=SPREAD_ROWS * count * features * 4,
            transcendentals=0,
        ),
    )(first_group, *operands, *previous)


def bag_bounds(lengths):
    ends = jnp.cumsum(lengths.reshape(-1))
    starts = ends - lengths.reshape(-1)
    return starts, ends


def column(vector, lanes=BLOCK):
    return jnp.broadcast_to(vector[:, None], (vector.shape[0], lanes))


def gelu(v):
    inner = np.sqrt(2 / np.pi).astype(np.float32) * (v + 0.044715 * (v * v * v))
    return 0.5 * v * (1.0 + jnp.tanh(inner))


def gelu_slope(v):
    root = np.sqrt(2 / np.pi).astype(np.float32)
    bent = jnp.tanh(root * (v + 0.044715 * (v * v * v)))
    return 0.5 * (1.0 + bent) + 0.5 * v * (1.0 - bent * bent) * root * (1.0 + 3 * 0.044715 * (v * v))


def shards(
    embed_rows,
    lengths,
    cotangent,
    p_proj,
    gain_one,
    bias_one,
    w_up,
    b_up,
    w_down,
    b_down,
    w_comp,
    w_res,
    gain_two,
    bias_two,
):
    links = Links()
    tokens = w_res.shape[0]
    features = embed_rows.shape[1]
    ranks = p_proj.shape[1]
    pairs = tokens * ranks
    row_total = embed_rows.shape[0]
    fm_width = b_down.shape[0]
    examples = cotangent.shape[0]

    def by_rank(vector):
        return jnp.swapaxes(vector.reshape(-1, tokens, ranks), 1, 2).reshape(vector.shape)

    def by_token(vector):
        return jnp.swapaxes(vector.reshape(-1, ranks, tokens), 1, 2).reshape(vector.shape)

    every = links.gather(jnp.concatenate([by_rank(w_up.T), w_down], axis=1))

    starts, ends = bag_bounds(lengths)
    lanes = GROUP * tokens
    starts = starts.reshape(-1, lanes)
    ends = ends.reshape(-1, lanes)
    offs = jnp.concatenate([starts[:, 0], ends[-1:, -1]])
    bases = jnp.arange(row_total // CHUNK, dtype=jnp.int32) * CHUNK
    first_group = jnp.sum((offs[1:][None, :] <= bases[:, None]).astype(jnp.int32), axis=1)
    mixer = make_mixer(w_res, w_comp, p_proj)
    gain_a, bias_a = column(by_rank(gain_one)), column(by_rank(bias_one))
    gain_b, bias_b = column(gain_two), column(bias_two)
    down_bias = column(b_down)

    xt, pair, normed, res = token_stage(
        offs, starts, ends, embed_rows.T, mixer, gain_a, bias_a, tokens
    )
    out, mix, gain_acc1, bias_acc1 = final_stage(res, cotangent, gain_b, bias_b, features, fm_width)
    out, mix, hidden, g_pre, g_normed, gain_acc0, bias_acc0, up_acc, down_acc = mlp_stage(
        every, normed, res, cotangent, column(b_up), column(b_down), gain_b, bias_b, features, (out, mix)
    )

    unit_rows = links.unit_rows(w_down.shape[0])
    other_shards, own_shards = links.shards()
    sent = grad_stage(other_shards, g_pre, hidden, normed, mix, fm_width, unit_rows)
    arrived = links.to_other_core(sent)
    mine = grad_stage(own_shards, g_pre, hidden, normed, mix, fm_width, unit_rows)
    arrived, mine = lax.optimization_barrier((arrived, mine))

    ring = links.ring(mine, arrived)
    blocks = examples // BLOCK
    cuts = [blocks * i // 3 for i in range(4)]
    state = ()
    for i in range(3):
        g_normed, state = ring.start((g_normed, state))
        state = back_stage(
            g_normed, pair, gain_a, mix, xt, mixer, tokens, cuts[i], cuts[i + 1] - cuts[i], state
        )
        g_normed, state = ring.finish((g_normed, state))
    gt, gain_acc, bias_acc, mix_acc, project_acc = state

    mix_cells = jnp.einsum("aeet->at", mix_acc.reshape(tokens, GROUP, GROUP, tokens))
    project_cells = project_acc.reshape(GROUP, tokens, -1, 128 // tokens, GROUP)
    project_cells = jnp.einsum("etcse->tcse", project_cells)
    proj_grad = jnp.einsum("tcse,seq->tcq", project_cells, rank_of(tokens), precision=lax.Precision.HIGHEST)
    small = [
        proj_grad.reshape(-1),
        by_token(jnp.sum(gain_acc, axis=1)),
        by_token(jnp.sum(bias_acc, axis=1)),
        jnp.sum(up_acc, axis=1),
        jnp.sum(down_acc, axis=1),
        mix_cells.reshape(-1),
        jnp.sum(gain_acc0 + gain_acc1, axis=1),
        jnp.sum(bias_acc0 + bias_acc1, axis=1),
    ]
    sizes = np.cumsum([part.shape[0] for part in small])[:-1]
    vector = jnp.concatenate(small)
    vector = jnp.pad(vector, (0, -vector.shape[0] % 1024)).reshape(-1, 128)

    steps = row_total // SPREAD_ROWS
    rounds = len(links.peers)
    cuts = [steps * i // rounds for i in range(rounds + 1)]
    rows_grad = ()
    for i in range(rounds):
        vector, gt, rows_grad = ring.start((vector, gt, rows_grad))
        far = [peer(vector) for peer in links.peers[i]]
        rows_grad = spread_stage(
            first_group, starts, ends, gt, row_total, cuts[i], cuts[i + 1] - cuts[i], rows_grad
        )
        far, rows_grad, gt = lax.optimization_barrier((far, rows_grad, gt))
        vector = sum(far, vector)
        rows_grad, gt = ring.finish((rows_grad, gt))
        rows_grad = (rows_grad,)
    total = ring.end()
    parts = jnp.split(vector.reshape(-1), list(sizes) + [int(sizes[-1]) + small[-1].shape[0]])
    res_grad = parts[5].reshape(tokens, tokens)
    return (
        out,
        rows_grad[0].T,
        parts[0].reshape(tokens, ranks),
        parts[1],
        parts[2],
        by_token(total[:, :pairs]).T,
        parts[3],
        total[:, pairs:],
        parts[4],
        res_grad[tokens - w_comp.shape[0] :],
        res_grad,
        parts[6],
        parts[7],
    )


def ring_order(chips):
    return list(range(0, chips, 2)) + list(range(chips - 1, 0, -2))


def added(*terms):
    return sum([term.astype(f32) for term in terms[1:]], terms[0].astype(f32))


def ring_shards(chips):
    order = ring_order(chips)
    reach = chips // 2
    steps = [0, *range(1, reach), *range(-1, -reach, -1), reach]
    return [[order[(order.index(chip) + step) % chips] for step in steps] for chip in range(chips)]


class Ring:
    def __init__(self, *terms):
        self.chips = lax.axis_size("dp") // 2
        self.order = ring_order(self.chips)
        self.reach = self.chips // 2
        self.terms = terms
        self.left = self.reach
        self.flying = None
        middle = added(*self.shard(self.chips - 1)).astype(bf16)
        rows = middle.shape[0] // 2
        self.send = [middle[:rows], middle[rows:]]
        self.total = None

    def shard(self, number):
        return [term[number] for term in self.terms]

    def ahead(self, distance):
        return self.shard(distance)

    def behind(self, distance):
        return self.shard(self.reach - 1 + distance)

    def along(self, value, step):
        order, chips = self.order, self.chips
        pairs = [
            (2 * order[i] + core, 2 * order[(i + step) % chips] + core)
            for i in range(chips)
            for core in range(2)
        ]
        return lax.ppermute(value, "dp", pairs)

    def start(self, others):
        if self.left < 0:
            return others
        self.send, others = lax.optimization_barrier((self.send, others))
        if self.left > 0:
            self.flying = (self.along(self.send[0], 1), self.along(self.send[1], -1))
        else:
            pairs = [(i, i ^ 1) for i in range(lax.axis_size("branch"))]
            self.flying = (lax.ppermute(self.send[0], "branch", pairs),)
        return others

    def finish(self, others):
        if self.flying is None:
            return others
        arrived, others = lax.optimization_barrier((self.flying, others))
        self.flying = None
        self.left -= 1
        if self.left < 0:
            self.total = self.send[0].astype(f32) + arrived[0].astype(f32)
        elif self.left == 0:
            self.total = added(*self.shard(0), *arrived)
            self.send = [self.total.astype(bf16)]
        else:
            one, two = added(*self.ahead(self.left)), added(*self.behind(self.left))
            first, second = arrived[0].astype(f32), arrived[1].astype(f32)
            if self.left == self.reach - 1:
                rows = first.shape[0]
                first = jnp.pad(first, ((0, one.shape[0] - rows), (0, 0)))
                second = jnp.pad(second, ((two.shape[0] - rows, 0), (0, 0)))
            self.send = [(one + first).astype(bf16), (two + second).astype(bf16)]
        return others

    def end(self):
        while self.left >= 0:
            self.start(())
            self.finish(())
        return self.total


class Links:
    def __init__(self):
        size = lax.axis_size("dp")
        bits = [("branch", 1)] + [("dp", 1 << i) for i in range(size.bit_length() - 1)]
        self.peers = [self.swaps(bits[i : i + 2]) for i in range(0, len(bits), 2)]

    def swapped(self, axis, bit, value):
        return lax.ppermute(value, axis, [(i, i ^ bit) for i in range(lax.axis_size(axis))])

    def swaps(self, bits):
        swaps = [functools.partial(self.swapped, axis, bit) for axis, bit in bits]
        if len(bits) == 2:
            (axis_one, bit_one), (axis_two, bit_two) = bits
            if axis_one == axis_two:
                swaps.append(functools.partial(self.swapped, axis_one, bit_one | bit_two))
            else:
                dp, branch = lax.axis_size("dp"), lax.axis_size("branch")
                pairs = [
                    (i * branch + j, (i ^ bit_two) * branch + (j ^ bit_one))
                    for i in range(dp)
                    for j in range(branch)
                ]
                swaps.append(lambda value: lax.ppermute(value, ("dp", "branch"), pairs))
        return swaps

    def gather(self, own):
        return lax.all_gather(own, "dp", axis=0, tiled=True)

    def shards(self):
        owners = np.asarray(ring_shards(lax.axis_size("dp") // 2), np.int32)
        table = np.stack([2 * owners + 1, 2 * owners, 2 * owners, 2 * owners + 1], axis=1)
        table = table.reshape(-1, 2, owners.shape[1])
        mine = lax.dynamic_index_in_dim(jnp.asarray(table), lax.axis_index("dp"), 0, keepdims=False)
        return mine[0], mine[1]

    def unit_rows(self, rows):
        return rows

    def to_other_core(self, value):
        return self.swapped("dp", 1, value)

    def ring(self, *terms):
        return Ring(*terms)


def solution(mesh):
    spread = P(("dp", "branch"), None)
    in_specs = (
        spread,
        spread,
        spread,
        P(),
        P(),
        P(),
        P(None, "dp"),
        P(),
        P("dp", None),
        P(),
        P(),
        P(),
        P(),
        P(),
    )
    out_specs = (
        spread,
        spread,
        P(),
        P(),
        P(),
        P(None, "dp"),
        P(),
        P("dp", None),
        P(),
        P(),
        P(),
        P(),
        P(),
    )
    return jax.shard_map(shards, mesh=mesh, in_specs=in_specs, out_specs=out_specs, check_vma=False)
```

```python
import functools

import jax
import jax.numpy as jnp
import numpy as np
from jax import lax
from jax.experimental import pallas as pl
from jax.experimental.pallas import tpu as pltpu
from jax.sharding import PartitionSpec as P

EPS = 1e-05
GROUP = 8
BLOCK = 128
CHUNK = 256
UNROLL = 4
SPREAD_ROWS = 16 * CHUNK
SPREAD_UNROLL = 8

f32 = jnp.float32
bf16 = jnp.bfloat16

NN = (((1,), (0,)), ((), ()))
NT = (((1,), (1,)), ((), ()))
TN = (((0,), (0,)), ((), ()))


def mul(left, right, dims=NN):
    return lax.dot_general(left, right, dims, preferred_element_type=f32)


def params(mebibytes):
    return pltpu.CompilerParams(vmem_limit_bytes=mebibytes * 1024 * 1024)


def one_hot(low, high, rows):
    row = lax.broadcasted_iota(jnp.int16, (rows, low.shape[1]), 0)
    inside = jnp.logical_and(row >= low.astype(jnp.int16), row < high.astype(jnp.int16))
    return jnp.where(inside, jnp.ones((), bf16), jnp.zeros((), bf16))


def turn(tile, shift):
    return pltpu.roll(tile, shift % 128, 1) if shift % 128 else tile


def tokens_kernel(
    offs, starts, ends, rows, mixer, gain, bias, xt_ref, pair_ref, normed_ref, res_ref, pair_s, nat_s, sum_s
):
    step = pl.program_id(0)
    groups = pair_s.shape[0] // GROUP
    row_total = rows.shape[1]
    features = rows.shape[0]
    tokens = nat_s.shape[0]
    ranks = pair_s.shape[1] // tokens
    lanes = tokens * GROUP
    per_tile = 128 // tokens
    span = 2 * CHUNK
    example = lax.broadcasted_iota(jnp.int32, (GROUP, 128), 0)
    place = lax.broadcasted_iota(jnp.int32, (GROUP, 128), 1) // tokens

    def some(k, carry):
        todo = [k * UNROLL + u for u in range(UNROLL)]
        bases = []
        for u, i in enumerate(todo):
            first = offs[step * groups + i]
            base = (first // 128) * 128
            bases.append(base)
            low = starts[pl.ds(i, 1), :]
            high = ends[pl.ds(i, 1), :]
            at = pl.multiple_of(jnp.minimum(base, row_total - span), 128)
            sum_s[u] = mul(rows[:, pl.ds(at, span)], one_hot(low - at, high - at, span))
        for u, i in enumerate(todo):
            base = bases[u] + span
            left = offs[step * groups + i + 1] - base

            @pl.when(left > 0)
            def more(u=u, i=i, base=base, left=left):
                low = starts[pl.ds(i, 1), :]
                high = ends[pl.ds(i, 1), :]

                def chunk(c, total):
                    wanted = base + c * CHUNK
                    at = pl.multiple_of(jnp.minimum(wanted, row_total - CHUNK), 128)
                    hot = one_hot(jnp.maximum(low, wanted) - at, high - at, CHUNK)
                    return total + mul(rows[:, pl.ds(at, CHUNK)], hot)

                sum_s[u] = lax.fori_loop(0, (left + CHUNK - 1) // CHUNK, chunk, sum_s[u])

        for u, i in enumerate(todo):
            x = sum_s[u].astype(bf16)
            xt_ref[i] = x
            nat = mul(mixer[...], x, NT)
            m = mul(nat[lanes:].astype(bf16), x)
            here = pl.ds(pl.multiple_of(i * GROUP, GROUP), GROUP)
            for c in range(ranks // per_tile):
                tile = None
                for s in range(per_tile):
                    at = GROUP * (c * per_tile + s)
                    slab = m[at : at + GROUP]
                    one = jnp.where(example < per_tile, slab[:, :128], slab[:, 128:])
                    one = turn(one, s * tokens)
                    mine = place == (example + s) % per_tile
                    tile = one if s == 0 else jnp.where(mine, one, tile)
                pair_s[here, c * 128 : c * 128 + 128] = tile
            for t in range(tokens):
                nat_s[t, here, :features] = nat[GROUP * t : GROUP * t + GROUP]
        return carry

    lax.fori_loop(0, groups // UNROLL, some, 0)
    pair = pair_s[...].T
    pair_ref[...] = pair
    centred = pair - jnp.mean(pair, axis=0, keepdims=True)
    scale = lax.rsqrt(jnp.mean(centred * centred, axis=0, keepdims=True) + EPS)
    normed_ref[...] = (centred * scale * gain[...] + bias[...]).astype(bf16)

    def back(k, carry):
        for u in range(4):
            t = k * 4 + u
            at = pl.ds(pl.multiple_of(t * features, 32), features)
            res_ref[at, :] = nat_s[t].astype(bf16).T[:features]
        return carry

    lax.fori_loop(0, tokens // 4, back, 0)


def norm_token(summed, g, gain, bias):
    centred = summed - jnp.mean(summed, axis=0, keepdims=True)
    scale = lax.rsqrt(jnp.mean(centred * centred, axis=0, keepdims=True) + EPS)
    hat = centred * scale
    q = g * gain
    g_hat = g * hat
    mean_q = jnp.mean(q, axis=0, keepdims=True)
    mean_qx = jnp.mean(q * hat, axis=0, keepdims=True)
    return (hat * gain + bias).astype(bf16), (scale * (q - mean_q - hat * mean_qx)).astype(bf16), g_hat


def standing(row):
    return jnp.broadcast_to(row[...], (128, row.shape[1])).T


def folded(value):
    return sum(value[:, i : i + 128] for i in range(0, value.shape[1], 128))


def doubled(value, lanes):
    return jnp.concatenate([value] * (lanes // value.shape[1]), axis=1)


def final_kernel(features, res, cot, gain, bias, out, gmix, gain_acc, bias_acc, cot_s, out_s):
    @pl.when(pl.program_id(0) == 0)
    def clear():
        gain_acc[...] = jnp.zeros_like(gain_acc)
        bias_acc[...] = jnp.zeros_like(bias_acc)

    cot_s[...] = cot[...].T
    unroll = 4

    def some(k, carry):
        hats, gs = [], []
        for u in range(unroll):
            at = pl.ds(pl.multiple_of((k * unroll + u) * features, 32), features)
            g = cot_s[at, :].astype(f32)
            out_s[at, :], gmix[at, :], g_hat = norm_token(res[at, :].astype(f32), g, gain[...], bias[...])
            hats.append(g_hat)
            gs.append(g)
        gain_acc[...] += sum(hats)
        bias_acc[...] += sum(gs)
        return carry

    lax.fori_loop(0, res.shape[0] // features // unroll, some, 0)
    out[...] = out_s[...].T


def mlp_kernel(
    features,
    every,
    normed,
    res,
    cot,
    b_up,
    b_down,
    gain,
    bias,
    out,
    mix,
    hidden,
    g_pre,
    g_normed,
    gain_acc,
    bias_acc,
    up_acc,
    down_acc,
    pre_s,
    cot_s,
    out_s,
    up_s,
    down_s,
):
    pairs, lanes = g_normed.shape
    units = hidden.shape[0]
    width = res.shape[0]
    now = pl.ds(pl.multiple_of(pl.program_id(0) * lanes, lanes), lanes)
    unit_tile = 256
    token_tile = 4 * features

    @pl.when(pl.program_id(0) == 0)
    def clear():
        for acc in (gain_acc, bias_acc, up_acc, down_acc):
            acc[...] = jnp.zeros_like(acc)
        up_s[...] = standing(b_up)
        down_s[...] = standing(b_down)

    cot_s[...] = cot[...].T
    for at in range(0, units, unit_tile):
        here = slice(at, at + unit_tile)
        pre = mul(every[here, :pairs], normed[...]) + doubled(up_s[here, :], lanes)
        pre_s[here, :] = pre
        hidden[here, now] = gelu(pre).astype(bf16)
    wide_gain, wide_bias = doubled(gain[...], lanes), doubled(bias[...], lanes)

    def fm_tile(first):
        return mul(every[:, pairs + first : pairs + first + token_tile], hidden[:, now], TN)

    ahead = fm_tile(0)
    for first in range(0, width, token_tile):
        tile = ahead
        if first + token_tile < width:
            ahead = fm_tile(first + token_tile)
        hats, gs = [], []
        for u in range(4):
            here = slice(first + u * features, first + (u + 1) * features)
            fm = tile[u * features : (u + 1) * features, :] + doubled(down_s[here, :], lanes)
            g = cot_s[here, :].astype(f32)
            summed = res[here, :].astype(f32) + fm.astype(bf16).astype(f32)
            out_s[here, :], g_mix, g_hat = norm_token(summed, g, wide_gain, wide_bias)
            mix[here, now] = g_mix
            down_acc[here, :] += folded(g_mix.astype(f32))
            hats.append(folded(g_hat))
            gs.append(folded(g))
        gain_acc[...] += sum(hats)
        bias_acc[...] += sum(gs)
    for at in range(0, units, unit_tile):
        here = slice(at, at + unit_tile)
        g_hidden = mul(every[here, pairs:], mix[:, now])
        value = (g_hidden * gelu_slope(pre_s[here, :])).astype(bf16)
        g_pre[here, now] = value
        up_acc[here, :] += folded(value.astype(f32))
    g_normed[...] = mul(every[:, :pairs], g_pre[:, now], TN)
    out[...] = out_s[...].T


def to_natural(mix, nat_s, features, block=0):
    count, examples, _ = nat_s.shape
    now = pl.ds(pl.multiple_of(block * examples, examples), examples)

    def some(k, carry):
        for u in range(4):
            t = k * 4 + u
            at = pl.ds(pl.multiple_of(t * features, 32), features)
            nat_s[t, :, :features] = mix[at, now].T
        return carry

    lax.fori_loop(0, count // 4, some, 0)


def natural_groups(nat_s, first, count, features):
    found = []
    for u in range(count // 2):
        both = pl.ds(pl.multiple_of((first + 2 * u) * GROUP, 2 * GROUP), 2 * GROUP)
        mixes = nat_s[:, both, :features].astype(f32)
        found += [mixes[:, :GROUP], mixes[:, GROUP:]]
    return [item.reshape(-1, features).astype(bf16) for item in found]


def early_kernel(gmix, xt, mixer, gt, mix_acc, nat_s):
    _, features, lanes = xt.shape
    groups = nat_s.shape[1] // GROUP
    base = pl.program_id(0) * groups
    rows = nat_s.shape[0] * GROUP
    own = slice(lanes - rows, lanes)

    @pl.when(pl.program_id(0) == 0)
    def clear():
        mix_acc[...] = jnp.zeros_like(mix_acc)

    to_natural(gmix, nat_s, features)

    def some(k, carry):
        total = mix_acc[...]
        for u, g_mix in enumerate(natural_groups(nat_s, k * UNROLL, UNROLL, features)):
            total = total + mul(g_mix, xt[k * UNROLL + u])
            gt[base + k * UNROLL + u] = mul(g_mix, mixer[own], TN).astype(bf16)
        mix_acc[...] = total
        return carry

    lax.fori_loop(0, groups // UNROLL, some, 0)


def back_kernel(start, gn, pair, gain, gmix, xt, mixer, early, *refs):
    *before, gt, gain_acc, bias_acc, mix_acc, project_acc, gp_s, nat_s = refs
    sums = (gain_acc, bias_acc, mix_acc, project_acc)
    _, features, lanes = xt.shape
    block = start + pl.program_id(0)
    groups = gp_s.shape[0] // GROUP
    base = block * groups
    tokens = lanes // GROUP
    ranks = gp_s.shape[1] // tokens
    per_tile = 128 // tokens
    rows = nat_s.shape[0] * GROUP

    @pl.when(pl.program_id(0) == 0)
    def clear():
        for i, acc in enumerate(sums):
            acc[...] = before[i][...] if before else jnp.zeros_like(acc)

    values = pair[...]
    centred = values - jnp.mean(values, axis=0, keepdims=True)
    scale = lax.rsqrt(jnp.mean(centred * centred, axis=0, keepdims=True) + EPS)
    hat = centred * scale
    g = gn[...]
    gain_acc[...] += g * hat
    bias_acc[...] += g
    h = g * gain[...]
    mean_h = jnp.mean(h, axis=0, keepdims=True)
    mean_hx = jnp.mean(h * hat, axis=0, keepdims=True)
    gp_s[...] = (scale * (h - mean_h - hat * mean_hx)).T
    to_natural(gmix, nat_s, features, block)
    example = lax.broadcasted_iota(jnp.int32, (GROUP, 128), 0)
    place = lax.broadcasted_iota(jnp.int32, (GROUP, 128), 1) // tokens
    own = place == example % per_tile
    keep_low = jnp.logical_and(own, example < per_tile)
    keep_high = jnp.logical_and(own, example >= per_tile)

    def some(k, carry):
        project = mixer[lanes:]
        four = pl.ds(pl.multiple_of(k * UNROLL, UNROLL), UNROLL)
        stacked = xt[four].reshape(UNROLL * features, lanes)
        projected = mul(stacked, project, NT).astype(bf16)
        g_pairs, g_parts = [], []
        for u in range(UNROLL):
            here = pl.ds(pl.multiple_of((k * UNROLL + u) * GROUP, GROUP), GROUP)
            slabs = []
            for j in range(ranks):
                c, s = j // per_tile, j % per_tile
                one = turn(gp_s[here, c * 128 : c * 128 + 128], -s * tokens)
                slabs.append(
                    jnp.concatenate([jnp.where(keep_low, one, 0.0), jnp.where(keep_high, one, 0.0)], axis=1)
                )
            g_pairs.append(jnp.concatenate(slabs, axis=0).astype(bf16))
            g_parts.append(mul(xt[k * UNROLL + u], g_pairs[u], NT).astype(bf16))
        g_projected = jnp.concatenate(g_parts, axis=0)
        project_acc[...] += mul(stacked, g_projected, TN)
        shared = mul(g_projected, project)
        mix_total = mix_acc[...]
        for u, g_mix in enumerate(natural_groups(nat_s, k * UNROLL, UNROLL, features)):
            i = base + k * UNROLL + u
            mix_total = mix_total + mul(g_mix, xt[k * UNROLL + u])
            mine = slice(u * features, (u + 1) * features)
            part = mul(projected[mine], g_pairs[u]) + mul(g_mix, mixer[:rows], TN) + shared[mine]
            gt[i] = (part + early[i].astype(f32)).astype(bf16)
        mix_acc[...] = mix_total
        return carry

    lax.fori_loop(0, groups // UNROLL, some, 0)


def spread_kernel(start, first_half, starts, ends, gt, out):
    step = start + pl.program_id(0)
    chunks = out.shape[1] // CHUNK
    last = starts.shape[0] - 1
    span = CHUNK // 128 + 1

    def some(k, carry):
        for u in range(SPREAD_UNROLL):
            c = k * SPREAD_UNROLL + u
            number = step * chunks + c
            first = jnp.minimum(first_half[number], last + 1 - span)
            lows, highs, values = [], [], []
            for i in range(span):
                half = first + i
                lows.append(starts[pl.ds(half, 1), :])
                highs.append(ends[pl.ds(half, 1), :])
                values.append(gt[half // 2, :, pl.ds(pl.multiple_of(half % 2 * 128, 128), 128)])
            low = jnp.concatenate(lows, axis=1) - number * CHUNK
            high = jnp.concatenate(highs, axis=1) - number * CHUNK
            at = pl.ds(pl.multiple_of(c * CHUNK, CHUNK), CHUNK)
            hot = one_hot(low, high, CHUNK)
            out[:, at] = mul(jnp.concatenate(values, axis=1), hot, NT).astype(bf16)
        return carry

    lax.fori_loop(0, chunks // SPREAD_UNROLL, some, 0)


def passing(kernel, given, previous):
    if not previous:
        return kernel, {}
    more = len(previous)
    skip = lambda *refs: kernel(*refs[:given], *refs[given + more :])
    return skip, {given + i: i for i in range(more)}


HBM, VMEM = pltpu.HBM, pltpu.VMEM
INSIDE = pl.BlockSpec(memory_space=pltpu.VMEM)


def held(*arrays):
    return [pltpu.with_memory_space_constraint(array, pltpu.VMEM) for array in arrays]


def away(*arrays):
    return [pltpu.with_memory_space_constraint(array, pltpu.HBM) for array in arrays]


def whole(shape):
    return pl.BlockSpec(shape, lambda *_: (0,) * len(shape))


def rank_of(tokens):
    per_tile = 128 // tokens
    slab, example = np.arange(per_tile)[:, None], np.arange(GROUP)[None, :]
    return np.eye(per_tile, dtype=np.float32)[(slab + example) % per_tile]


def make_mixer(w_res, w_comp, p_proj):
    tokens = w_res.shape[0]
    fm_tokens = tokens - w_comp.shape[0]
    mix = w_res.astype(f32) + jnp.pad(w_comp.astype(f32), ((fm_tokens, 0), (0, 0)))
    mix = jnp.broadcast_to(mix[:, None, :], (tokens, GROUP, tokens))
    by_tile = p_proj.T.astype(f32).reshape(-1, 128 // tokens, tokens)
    project = jnp.einsum("cqt,seq->cset", by_tile, rank_of(tokens))
    both = jnp.concatenate([mix, project.reshape(-1, GROUP, tokens)], axis=0)
    wide = both[:, :, None, :] * np.eye(GROUP, dtype=np.float32)[None, :, :, None]
    return wide.reshape(both.shape[0] * GROUP, GROUP * tokens).astype(bf16)


def token_stage(offs, starts, ends, rows, mixer, gain, bias, tokens):
    features, row_total = rows.shape
    group_count, lanes = starts.shape
    examples = group_count * GROUP
    pairs = gain.shape[0]
    groups = BLOCK // GROUP
    return pl.pallas_call(
        tokens_kernel,
        name="tokens",
        grid_spec=pltpu.PrefetchScalarGridSpec(
            num_scalar_prefetch=1,
            grid=(examples // BLOCK,),
            in_specs=[
                pl.BlockSpec((groups, lanes), lambda i, _: (i, 0)),
                pl.BlockSpec((groups, lanes), lambda i, _: (i, 0)),
                pl.BlockSpec(memory_space=pltpu.VMEM),
                whole(mixer.shape),
                whole(gain.shape),
                whole(bias.shape),
            ],
            out_specs=[
                pl.BlockSpec((groups, features, lanes), lambda i, _: (i, 0, 0)),
                pl.BlockSpec((pairs, BLOCK), lambda i, _: (0, i)),
                pl.BlockSpec((pairs, BLOCK), lambda i, _: (0, i)),
                pl.BlockSpec((tokens * features, BLOCK), lambda i, _: (0, i)),
            ],
            scratch_shapes=[
                pltpu.VMEM((BLOCK, pairs), f32),
                pltpu.VMEM((tokens, BLOCK, 256), f32),
                pltpu.VMEM((UNROLL, features, lanes), f32),
            ],
        ),
        out_shape=[
            HBM((group_count, features, lanes), bf16),
            HBM((pairs, examples), f32),
            HBM((pairs, examples), bf16),
            HBM((tokens * features, examples), bf16),
        ],
        compiler_params=params(32),
        cost_estimate=pl.CostEstimate(
            flops=2 * features * lanes * (row_total * 2 + 1000 * group_count),
            bytes_accessed=row_total * features * 2 + 30 * examples * 1024,
            transcendentals=0,
        ),
    )(offs, starts, ends, *away(rows), mixer, gain, bias)


def final_stage(res, cot, gain, bias, features, part):
    width, examples = res.shape
    at = (width - part) // part
    tall = pl.BlockSpec((part, BLOCK), lambda i: (at, i))
    flat = pl.BlockSpec((BLOCK, part), lambda i: (i, at))
    return pl.pallas_call(
        functools.partial(final_kernel, features),
        name="final_comp",
        grid=(examples // BLOCK,),
        in_specs=[tall, flat, whole(gain.shape), whole(bias.shape)],
        out_specs=[flat, pl.BlockSpec((part, BLOCK), lambda i: (0, i)), whole((features, BLOCK)), whole((features, BLOCK))],
        out_shape=[
            HBM((examples, width), bf16),
            HBM((part, examples), bf16),
            jax.ShapeDtypeStruct((features, BLOCK), f32),
            jax.ShapeDtypeStruct((features, BLOCK), f32),
        ],
        scratch_shapes=[pltpu.VMEM((part, BLOCK), bf16), pltpu.VMEM((part, BLOCK), bf16)],
        compiler_params=params(16),
        cost_estimate=pl.CostEstimate(
            flops=200 * part * examples, bytes_accessed=8 * part * examples, transcendentals=0
        ),
    )(*away(res, cot), gain, bias)


def mlp_stage(every, normed, res, cot, b_up, b_down, gain, bias, features, previous):
    units, columns = every.shape
    pairs, examples = normed.shape
    part = columns - pairs
    lanes = 2 * BLOCK
    wide = lambda rows: pl.BlockSpec((rows, lanes), lambda i: (0, i))
    flat = pl.BlockSpec((lanes, part), lambda i: (i, 0))
    every, normed, res, cot, previous = away(every, normed, res, cot, previous)
    operands = (every, normed, res, cot, b_up, b_down, gain, bias)
    kernel, aliases = passing(functools.partial(mlp_kernel, features), len(operands), (previous,))
    return pl.pallas_call(
        kernel,
        name="mlp",
        grid=(examples // lanes,),
        in_specs=[
            pl.BlockSpec(memory_space=pltpu.VMEM),
            wide(pairs),
            wide(part),
            flat,
            whole(b_up.shape),
            whole(b_down.shape),
            whole(gain.shape),
            whole(bias.shape),
        ]
        + [pl.BlockSpec(memory_space=pl.ANY)],
        out_specs=[
            flat,
            INSIDE,
            INSIDE,
            INSIDE,
            wide(pairs),
            whole((features, BLOCK)),
            whole((features, BLOCK)),
            whole((units, BLOCK)),
            whole((part, BLOCK)),
        ],
        out_shape=[
            HBM(previous.shape, bf16),
            VMEM((part, examples), bf16),
            VMEM((units, examples), bf16),
            VMEM((units, examples), bf16),
            HBM((pairs, examples), f32),
            jax.ShapeDtypeStruct((features, BLOCK), f32),
            jax.ShapeDtypeStruct((features, BLOCK), f32),
            jax.ShapeDtypeStruct((units, BLOCK), f32),
            jax.ShapeDtypeStruct((part, BLOCK), f32),
        ],
        scratch_shapes=[
            pltpu.VMEM((units, lanes), f32),
            pltpu.VMEM((part, lanes), bf16),
            pltpu.VMEM((part, lanes), bf16),
            pltpu.VMEM((units, BLOCK), f32),
            pltpu.VMEM((part, BLOCK), f32),
        ],
        input_output_aliases=aliases,
        compiler_params=params(38),
        cost_estimate=pl.CostEstimate(
            flops=4 * units * columns * examples,
            bytes_accessed=2 * units * columns + 20 * part * examples,
            transcendentals=2 * units * examples,
        ),
    )(*operands, previous)


def early_stage(gmix, xt, mixer):
    group_count, features, lanes = xt.shape
    part, examples = gmix.shape
    count = part // features
    return pl.pallas_call(
        early_kernel,
        name="early",
        grid=(examples // BLOCK,),
        in_specs=[
            pl.BlockSpec((part, BLOCK), lambda i: (0, i)),
            pl.BlockSpec((BLOCK // GROUP, features, lanes), lambda i: (i, 0, 0)),
            whole(mixer.shape),
        ],
        out_specs=[INSIDE, whole((count * GROUP, lanes))],
        out_shape=[
            VMEM((group_count, features, lanes), bf16),
            jax.ShapeDtypeStruct((count * GROUP, lanes), f32),
        ],
        scratch_shapes=[pltpu.VMEM((count, BLOCK, 256), bf16)],
        compiler_params=params(14),
        cost_estimate=pl.CostEstimate(
            flops=2 * features * lanes * 500 * group_count,
            bytes_accessed=group_count * features * lanes * 8,
            transcendentals=0,
        ),
    )(*away(gmix, xt), mixer)


def back_stage(gn, pair, gain, gmix, xt, mixer, gt, start, count, before):
    pairs, examples = pair.shape
    group_count, features, lanes = xt.shape
    ranked = mixer.shape[0] - lanes
    fm_tokens = gmix.shape[0] // features
    wide = pl.BlockSpec((pairs, BLOCK), lambda i: (0, start + i))
    sums = [(pairs, BLOCK), (pairs, BLOCK), (fm_tokens * GROUP, lanes), (lanes, ranked)]
    gn, pair, xt = away(gn, pair, xt)
    gmix, gt = held(gmix, gt)
    by_group = pl.BlockSpec((BLOCK // GROUP, features, lanes), lambda i: (start + i, 0, 0))
    operands = (gn, pair, gain, gmix, xt, mixer, gt, *before)
    return pl.pallas_call(
        functools.partial(back_kernel, start),
        name="back",
        grid=(count,),
        in_specs=[wide, wide, whole(gain.shape), INSIDE, by_group, whole(mixer.shape), INSIDE]
        + [whole(item.shape) for item in before],
        out_specs=[INSIDE] + [whole(shape) for shape in sums],
        out_shape=[VMEM((group_count, features, lanes), bf16)]
        + [jax.ShapeDtypeStruct(shape, f32) for shape in sums],
        scratch_shapes=[
            pltpu.VMEM((BLOCK, pairs), f32),
            pltpu.VMEM((fm_tokens, BLOCK, 256), bf16),
        ],
        input_output_aliases={6: 0},
        compiler_params=params(18),
        cost_estimate=pl.CostEstimate(
            flops=2 * features * lanes * 1400 * BLOCK // GROUP * count,
            bytes_accessed=40 * BLOCK * count * 1024,
            transcendentals=0,
        ),
    )(*operands)


def exact(value, selector, dims=NN):
    total = None
    for _ in range(3):
        piece = value.astype(bf16)
        value = value - piece.astype(f32)
        total = mul(piece, selector, dims) if total is None else total + mul(piece, selector, dims)
    return total


def ones_where(condition):
    return jnp.where(condition, 1.0, 0.0).astype(bf16)


def by_token_order(pairs, tokens):
    ranks = pairs // tokens
    row = lax.broadcasted_iota(jnp.int32, (pairs, pairs), 0)
    lane = lax.broadcasted_iota(jnp.int32, (pairs, pairs), 1)
    return ones_where((row % tokens) * ranks + row // tokens == lane)


def small_rows(tokens, pairs, units, width, features):
    counts = [tokens, pairs // 128, pairs // 128, units // 128, width // 128, -(-features // 128)]
    counts.append(counts[-1])
    starts = np.cumsum([0] + counts)
    return [(int(start), count) for start, count in zip(starts, counts)], -(-int(starts[-1]) // 8) * 8


def small_kernel(tokens, places, gain_acc, bias_acc, mix_fm, mix_comp, project, up, down, gains, biases, out):
    def put(place, row):
        start, count = place
        for i in range(count):
            piece = row[:, i * 128 : i * 128 + 128]
            out[start + i : start + i + 1, : piece.shape[1]] = piece

    def lying(column):
        return jnp.sum(column.T, axis=0, keepdims=True)

    out[...] = jnp.zeros_like(out)
    lanes = mix_fm.shape[1]
    ranked = project.shape[1]
    per_tile = 128 // tokens
    mix = jnp.concatenate([mix_fm[...], mix_comp[...]], axis=0)
    row = lax.broadcasted_iota(jnp.int32, mix.shape, 0) % GROUP
    lane = lax.broadcasted_iota(jnp.int32, mix.shape, 1) // tokens
    mix = jnp.where(row == lane, mix, 0.0)
    fold = ones_where(
        lax.broadcasted_iota(jnp.int32, (lanes, tokens), 0) % tokens
        == lax.broadcasted_iota(jnp.int32, (lanes, tokens), 1)
    )
    folded_mix = exact(mix, fold).reshape(tokens, GROUP, tokens)
    row = lax.broadcasted_iota(jnp.int32, project.shape, 0) // tokens
    lane = lax.broadcasted_iota(jnp.int32, project.shape, 1) % GROUP
    cells = jnp.where(row == lane, project[...], 0.0).reshape(GROUP, tokens, ranked)
    cells = jnp.sum(cells, axis=0)
    ranks = ranked // GROUP
    row = lax.broadcasted_iota(jnp.int32, (ranks, ranked), 0)
    lane = lax.broadcasted_iota(jnp.int32, (ranks, ranked), 1)
    slab = lane // GROUP
    rank = slab // per_tile * per_tile + (lane % GROUP + slab % per_tile) % per_tile
    pick = ones_where(row == rank)
    projected = None
    for _ in range(3):
        piece = cells.astype(bf16)
        cells = cells - piece.astype(f32)
        part = mul(pick, piece, NT)
        projected = part if projected is None else projected + part
    out[:ranks, :tokens] = projected
    out[:tokens, tokens : 2 * tokens] = jnp.sum(folded_mix, axis=1)
    both = jnp.concatenate([lying(gain_acc[...]), lying(bias_acc[...])], axis=0)
    both = exact(both, by_token_order(both.shape[1], tokens))
    put(places[1], both[:1])
    put(places[2], both[1:])
    put(places[3], lying(up[...]))
    put(places[4], lying(down[...]))
    put(places[5], lying(gains[0] + gains[1]))
    put(places[6], lying(biases[0] + biases[1]))


def small_stage(tokens, places, rows, gain_acc, bias_acc, mix_fm, mix_comp, project, up, down, gains, biases):
    def kernel(*refs):
        *given, gain_0, gain_1, bias_0, bias_1, out = refs
        small_kernel(tokens, places, *given, (gain_0[...], gain_1[...]), (bias_0[...], bias_1[...]), out)

    operands = (gain_acc, bias_acc, mix_fm, mix_comp, project, up, down, *gains, *biases)
    return pl.pallas_call(
        kernel,
        name="small",
        out_shape=jax.ShapeDtypeStruct((rows, 128), f32),
        compiler_params=params(16),
        cost_estimate=pl.CostEstimate(flops=10**9, bytes_accessed=4 * 10**6, transcendentals=0),
    )(*operands)


def last_kernel(tokens, places, total, more, *refs):
    *vectors, up, down, p_proj, w_res, gain_one, bias_one, b_up, b_down, gain_two, bias_two = refs
    pairs = up.shape[1]
    value = total[...] + more[...].astype(f32)
    down[...] = value[:, pairs:]
    up[...] = exact(value[:, :pairs], by_token_order(pairs, tokens))
    vector = sum([ref[...] for ref in vectors])
    p_proj[...] = vector[: p_proj.shape[0], :tokens]
    w_res[...] = vector[:tokens, tokens : 2 * tokens]
    rest = (gain_one, bias_one, b_up, b_down, gain_two, bias_two)
    for (start, count), ref in zip(places[1:], rest):
        ref[...] = vector[start : start + count]


def last_stage(total, more, vectors, places, pairs, tokens):
    rows, columns = total.shape
    shapes = [(rows, pairs), (rows, columns - pairs), (pairs // tokens, tokens), (tokens, tokens)]
    shapes += [(count, 128) for _, count in places[1:]]
    return pl.pallas_call(
        functools.partial(last_kernel, tokens, places),
        name="last",
        out_shape=[jax.ShapeDtypeStruct(shape, f32) for shape in shapes],
        compiler_params=params(16),
        cost_estimate=pl.CostEstimate(
            flops=6 * rows * pairs * pairs, bytes_accessed=10 * rows * columns, transcendentals=0
        ),
    )(total, more, *vectors)


def grad_kernel(rows, parts, table, pre, hidden, normed, mix, sent, mine, picked_s, normed_s, out_s, arrive, leave):
    pairs = normed_s.shape[0]
    width = mix.shape[0]
    count = table.shape[0]
    half = sent.shape[0]
    bring = pltpu.make_async_copy(normed, normed_s, arrive.at[0])
    bring.start()
    flying = []

    def picked(source):
        for i in range(count):
            start = pl.multiple_of(table[i] * rows, rows)
            picked_s[i * rows : (i + 1) * rows, :] = source[pl.ds(start, rows), :]
        return picked_s[...]

    def send(at, size, value):
        here = pl.ds(at, size)
        out_s[:, here] = value.astype(bf16)
        for i, target in enumerate((sent, mine)):
            source = out_s.at[pl.ds(i * half, half), here]
            copy = pltpu.make_async_copy(source, target.at[:, here], leave.at[len(flying)])
            copy.start()
            flying.append(copy)

    part = width // parts
    left = picked(hidden)
    for i in range(parts):
        send(pairs + i * part, part, mul(left, mix[i * part : (i + 1) * part, :], NT))
    bring.wait()
    send(0, pairs, mul(picked(pre), normed_s[...], NT))
    for copy in flying:
        copy.wait()


def grad_stage(table, pre, hidden, normed, mix, rows):
    units, examples = hidden.shape
    pairs = normed.shape[0]
    columns = pairs + mix.shape[0]
    parts = 4
    anywhere = pl.BlockSpec(memory_space=pl.ANY)
    pre, hidden, mix = held(pre, hidden, mix)
    return pl.pallas_call(
        functools.partial(grad_kernel, rows, parts),
        name="weight_grads",
        grid_spec=pltpu.PrefetchScalarGridSpec(
            num_scalar_prefetch=1,
            grid=(1,),
            in_specs=[INSIDE, INSIDE, anywhere, INSIDE],
            out_specs=[anywhere] * 2,
            scratch_shapes=[
                pltpu.VMEM((units, examples), bf16),
                pltpu.VMEM((pairs, examples), bf16),
                pltpu.VMEM((units, columns), bf16),
                pltpu.SemaphoreType.DMA((1,)),
                pltpu.SemaphoreType.DMA((2 + 2 * parts,)),
            ],
        ),
        out_shape=[HBM((units // 2, columns), bf16)] * 2,
        compiler_params=params(22),
        cost_estimate=pl.CostEstimate(
            flops=2 * units * examples * columns,
            bytes_accessed=2 * units * columns + 2 * examples * (2 * units + columns),
            transcendentals=0,
        ),
    )(table, pre, hidden, *away(normed), mix)


def spread_stage(first_half, starts, ends, gt, row_total, start, count, previous):
    group_count, features, lanes = gt.shape
    operands = (starts.reshape(-1, 128), ends.reshape(-1, 128), *held(gt))
    previous = away(*previous)
    kernel, aliases = passing(functools.partial(spread_kernel, start), len(operands) + 1, previous)
    return pl.pallas_call(
        kernel,
        name="spread",
        grid_spec=pltpu.PrefetchScalarGridSpec(
            num_scalar_prefetch=1,
            grid=(count,),
            in_specs=[whole(operands[0].shape), whole(operands[1].shape), INSIDE]
            + [pl.BlockSpec(memory_space=pl.ANY)] * len(previous),
            out_specs=pl.BlockSpec((features, SPREAD_ROWS), lambda i, _: (0, start + i)),
        ),
        out_shape=HBM((features, row_total), bf16),
        input_output_aliases=aliases,
        compiler_params=params(12),
        cost_estimate=pl.CostEstimate(
            flops=4 * features * lanes * SPREAD_ROWS * count,
            bytes_accessed=SPREAD_ROWS * count * features * 4,
            transcendentals=0,
        ),
    )(first_half, *operands, *previous)


def bag_bounds(lengths):
    ends = jnp.cumsum(lengths.reshape(-1))
    starts = ends - lengths.reshape(-1)
    return starts, ends


def column(vector, lanes=BLOCK):
    return jnp.broadcast_to(vector[:, None], (vector.shape[0], lanes))


def gelu(v):
    inner = np.sqrt(2 / np.pi).astype(np.float32) * (v + 0.044715 * (v * v * v))
    return 0.5 * v * (1.0 + jnp.tanh(inner))


def gelu_slope(v):
    root = np.sqrt(2 / np.pi).astype(np.float32)
    bent = jnp.tanh(root * (v + 0.044715 * (v * v * v)))
    return 0.5 * (1.0 + bent) + 0.5 * v * (1.0 - bent * bent) * root * (1.0 + 3 * 0.044715 * (v * v))


def shards(
    embed_rows,
    lengths,
    cotangent,
    p_proj,
    gain_one,
    bias_one,
    w_up,
    b_up,
    w_down,
    b_down,
    w_comp,
    w_res,
    gain_two,
    bias_two,
):
    links = Links()
    tokens = w_res.shape[0]
    features = embed_rows.shape[1]
    ranks = p_proj.shape[1]
    pairs = tokens * ranks
    row_total = embed_rows.shape[0]
    fm_width = b_down.shape[0]
    examples = cotangent.shape[0]

    def by_rank(vector):
        return jnp.swapaxes(vector.reshape(-1, tokens, ranks), 1, 2).reshape(vector.shape)

    def by_token(vector):
        return jnp.swapaxes(vector.reshape(-1, ranks, tokens), 1, 2).reshape(vector.shape)

    every = links.gather(jnp.concatenate([by_rank(w_up.T), w_down], axis=1))

    starts, ends = bag_bounds(lengths)
    lanes = GROUP * tokens
    starts = starts.reshape(-1, lanes)
    ends = ends.reshape(-1, lanes)
    offs = jnp.concatenate([starts[:, 0], ends[-1:, -1]])
    bases = jnp.arange(row_total // CHUNK, dtype=jnp.int32) * CHUNK
    half_ends = ends.reshape(-1, 128)[:, 127]
    first_half = jnp.sum((half_ends[None, :] <= bases[:, None]).astype(jnp.int32), axis=1)
    mixer = make_mixer(w_res, w_comp, p_proj)
    gain_a, bias_a = column(by_rank(gain_one)), column(by_rank(bias_one))
    gain_b, bias_b = column(gain_two), column(bias_two)
    down_bias = column(b_down)

    xt, pair, normed, res = token_stage(
        offs, starts, ends, embed_rows.T, mixer, gain_a, bias_a, tokens
    )
    out, mix_comp, gain_acc1, bias_acc1 = final_stage(res, cotangent, gain_b, bias_b, features, fm_width)
    mix_comp, first_half = lax.optimization_barrier((mix_comp, first_half))
    gt, mix_acc1 = early_stage(mix_comp, xt, mixer)
    unit_rows = links.unit_rows(w_down.shape[0])
    table, rows = links.shards(unit_rows)
    out, mix, hidden, g_pre, g_normed, gain_acc0, bias_acc0, up_acc, down_acc = mlp_stage(
        every, normed, res, cotangent, b_up[None, :], b_down[None, :], gain_b, bias_b, features, out
    )
    sent, mine = grad_stage(table, g_pre, hidden, normed, mix, rows)

    ring = links.ring(*links.arranged(sent, mine, unit_rows))
    blocks = examples // BLOCK
    cuts = [0, blocks // 6, blocks // 3, 2 * blocks // 3, blocks]
    sums = []
    for i in range(4):
        g_normed, gt, sums = ring.start((g_normed, gt, sums))
        gt, *sums = back_stage(
            g_normed, pair, gain_a, mix, xt, mixer, gt, cuts[i], cuts[i + 1] - cuts[i], sums
        )
        g_normed, gt, sums = ring.finish((g_normed, gt, sums))
    gain_acc, bias_acc, mix_acc0, project_acc = sums
    places, rows = small_rows(tokens, pairs, b_up.shape[0], fm_width, features)
    vector = small_stage(
        tokens,
        places,
        rows,
        gain_acc,
        bias_acc,
        mix_acc0,
        mix_acc1,
        project_acc,
        up_acc,
        down_acc,
        (gain_acc0, gain_acc1),
        (bias_acc0, bias_acc1),
    )

    steps = row_total // SPREAD_ROWS
    rounds = 2
    swaps = links.rounds()
    cuts = [steps * i // rounds for i in range(rounds + 1)]
    rows_grad = ()
    for i in range(rounds):
        vector, gt, rows_grad = ring.start((vector, gt, rows_grad))
        far = [swap(vector) for swap in swaps[i]]
        rows_grad = spread_stage(
            first_half, starts, ends, gt, row_total, cuts[i], cuts[i + 1] - cuts[i], rows_grad
        )
        far, gt, rows_grad = lax.optimization_barrier((far, gt, rows_grad))
        vector = sum(far, vector)
        vector, gt, rows_grad = ring.finish((vector, gt, rows_grad))
        rows_grad = (rows_grad,)
    for some in swaps[rounds:-1]:
        vector = sum([swap(vector) for swap in some], vector)
    vectors = [vector] + [swap(vector) for swap in swaps[-1]]
    up_grad, down_grad, proj_grad, res_grad, *rest = last_stage(*ring.end(), vectors, places, pairs, tokens)
    rest = [item.reshape(-1) for item in rest]
    return (
        out,
        rows_grad[0].T,
        proj_grad.T,
        rest[0],
        rest[1],
        up_grad.T,
        rest[2],
        down_grad,
        rest[3],
        res_grad[tokens - w_comp.shape[0] :],
        res_grad,
        rest[4][:features],
        rest[5][:features],
    )


def ring_order(chips):
    return list(range(0, chips, 2)) + list(range(chips - 1, 0, -2))


def added(*terms):
    return sum([term.astype(f32) for term in terms[1:]], terms[0].astype(f32))


def ring_shards(chips):
    order = ring_order(chips)
    reach = chips // 2
    steps = [0, *range(1, reach), *range(-1, -reach, -1), reach]
    return [[order[(order.index(chip) + step) % chips] for step in steps] for chip in range(chips)]


class Ring:
    def __init__(self, sent, mine):
        self.chips = lax.axis_size("dp") // 2
        self.order = ring_order(self.chips)
        self.reach = self.chips // 2
        self.terms = [mine]
        self.left = self.reach + 1
        self.flying = None
        self.send = [sent]
        self.total = None

    def shard(self, number):
        return [term[number] for term in self.terms]

    def ahead(self, distance):
        return self.shard(distance)

    def behind(self, distance):
        return self.shard(self.reach - 1 + distance)

    def along(self, value, step):
        order, chips = self.order, self.chips
        pairs = [
            (2 * order[i] + core, 2 * order[(i + step) % chips] + core)
            for i in range(chips)
            for core in range(2)
        ]
        return lax.ppermute(value, "dp", pairs)

    def start(self, others):
        if self.left < 0:
            return others
        self.send, others = lax.optimization_barrier((self.send, others))
        if self.left > self.reach:
            pairs = [(i, i ^ 1) for i in range(lax.axis_size("dp"))]
            self.flying = (lax.ppermute(self.send[0], "dp", pairs),)
        elif self.left > 0:
            self.flying = (self.along(self.send[0], 1), self.along(self.send[1], -1))
        else:
            pairs = [(i, i ^ 1) for i in range(lax.axis_size("branch"))]
            self.flying = (lax.ppermute(self.send[0], "branch", pairs),)
        return others

    def finish(self, others):
        if self.flying is None:
            return others
        arrived, others = lax.optimization_barrier((self.flying, others))
        self.flying = None
        self.left -= 1
        if self.left < 0:
            self.more = arrived[0]
        elif self.left == self.reach:
            self.terms.append(arrived[0])
            middle = added(*self.shard(self.chips - 1)).astype(bf16)
            rows = middle.shape[0] // 2
            self.send = [middle[:rows], middle[rows:]]
        elif self.left == 0:
            self.total = added(*self.shard(0), *arrived)
            self.send = [self.total.astype(bf16)]
        else:
            one, two = added(*self.ahead(self.left)), added(*self.behind(self.left))
            first, second = arrived[0].astype(f32), arrived[1].astype(f32)
            if self.left == self.reach - 1:
                rows = first.shape[0]
                first = jnp.pad(first, ((0, one.shape[0] - rows), (0, 0)))
                second = jnp.pad(second, ((two.shape[0] - rows, 0), (0, 0)))
            self.send = [(one + first).astype(bf16), (two + second).astype(bf16)]
        return others

    def end(self):
        while self.left >= 0:
            self.start(())
            self.finish(())
        return self.total, self.more


class Links:
    def swaps(self, bits):
        dp, branch = lax.axis_size("dp"), lax.axis_size("branch")
        found = []
        for chosen in range(1, 1 << len(bits)):
            flip = functools.reduce(lambda a, b: a | b, [bit for i, bit in enumerate(bits) if chosen >> i & 1])
            pairs = [(i, i ^ flip) for i in range(dp * branch)]
            found.append(lambda value, pairs=pairs: lax.ppermute(value, ("dp", "branch"), pairs))
        return found

    def rounds(self):
        size = lax.axis_size("dp") * lax.axis_size("branch")
        bits = [1 << i for i in range(size.bit_length() - 1)]
        return [self.swaps(bits[i : i + 2]) for i in range(0, len(bits), 2)]

    def gather(self, own):
        return lax.all_gather(own, "dp", axis=0, tiled=True)

    def unit_rows(self, rows):
        return rows

    def owners(self):
        owners = np.asarray(ring_shards(lax.axis_size("dp") // 2), np.int32)
        table = np.stack([2 * owners + 1, 2 * owners, 2 * owners, 2 * owners + 1], axis=1)
        table = table.reshape(-1, 2 * owners.shape[1])
        return lax.dynamic_index_in_dim(jnp.asarray(table), lax.axis_index("dp"), 0, keepdims=False)

    def shards(self, rows):
        if rows % 16 == 0:
            return self.owners(), rows
        count = lax.axis_size("dp") * rows // 96
        return jnp.arange(count, dtype=jnp.int32), 96

    def arranged(self, sent, mine, rows):
        count = lax.axis_size("dp")
        both = sent, mine
        if rows % 16 != 0:
            blocks = jnp.concatenate(both, axis=0).reshape(count, rows, -1)[self.owners()]
            both = blocks[: count // 2], blocks[count // 2 :]
        return [item.reshape(count // 2, rows, -1) for item in both]

    def ring(self, sent, mine):
        return Ring(sent, mine)


def solution(mesh):
    spread = P(("dp", "branch"), None)
    in_specs = (
        spread,
        spread,
        spread,
        P(),
        P(),
        P(),
        P(None, "dp"),
        P(),
        P("dp", None),
        P(),
        P(),
        P(),
        P(),
        P(),
    )
    out_specs = (
        spread,
        spread,
        P(),
        P(),
        P(),
        P(None, "dp"),
        P(),
        P("dp", None),
        P(),
        P(),
        P(),
        P(),
        P(),
    )
    return jax.shard_map(shards, mesh=mesh, in_specs=in_specs, out_specs=out_specs, check_vma=False)
```

```python
import functools

import jax
import jax.numpy as jnp
import numpy as np
from jax import lax
from jax.experimental import pallas as pl
from jax.experimental.pallas import tpu as pltpu
from jax.sharding import PartitionSpec as P

EPS = 1e-05
GROUP = 8
BLOCK = 128
CHUNK = 256
SPREAD_ROWS = 16 * CHUNK

f32 = jnp.float32
bf16 = jnp.bfloat16

NN = (((1,), (0,)), ((), ()))
NT = (((1,), (1,)), ((), ()))
TN = (((0,), (0,)), ((), ()))


def mul(left, right, dims=NN):
    return lax.dot_general(left, right, dims, preferred_element_type=f32)


def params(mebibytes):
    return pltpu.CompilerParams(vmem_limit_bytes=mebibytes * 1024 * 1024)


def one_hot(low, high, rows):
    row = lax.broadcasted_iota(jnp.int16, (rows, low.shape[1]), 0)
    inside = jnp.logical_and(row >= low.astype(jnp.int16), row < high.astype(jnp.int16))
    return jnp.where(inside, jnp.ones((), bf16), jnp.zeros((), bf16))


def turn(tile, shift):
    return pltpu.roll(tile, shift % 128, 1) if shift % 128 else tile


def tokens_kernel(
    offs, starts, ends, rows, mixer, gain, bias, xt_ref, pair_ref, normed_ref, res_ref, pair_s, nat_s, sum_s
):
    step = pl.program_id(0)
    groups = pair_s.shape[0] // GROUP
    row_total = rows.shape[1]
    features = rows.shape[0]
    tokens = nat_s.shape[0]
    ranks = pair_s.shape[1] // tokens
    lanes = tokens * GROUP
    per_tile = 128 // tokens
    span = 2 * CHUNK
    example = lax.broadcasted_iota(jnp.int32, (GROUP, 128), 0)
    place = lax.broadcasted_iota(jnp.int32, (GROUP, 128), 1) // tokens

    def all_groups():
        todo = range(groups)
        bases = []
        for u, i in enumerate(todo):
            first = offs[step * groups + i]
            base = (first // 128) * 128
            bases.append(base)
            low = starts[i : i + 1, :]
            high = ends[i : i + 1, :]
            at = pl.multiple_of(jnp.minimum(base, row_total - span), 128)
            sum_s[u] = mul(rows[:, pl.ds(at, span)], one_hot(low - at, high - at, span))
        for u, i in enumerate(todo):
            base = bases[u] + span
            left = offs[step * groups + i + 1] - base

            @pl.when(left > 0)
            def more(u=u, i=i, base=base, left=left):
                low = starts[i : i + 1, :]
                high = ends[i : i + 1, :]

                def chunk(c, total):
                    wanted = base + c * CHUNK
                    at = pl.multiple_of(jnp.minimum(wanted, row_total - CHUNK), 128)
                    hot = one_hot(jnp.maximum(low, wanted) - at, high - at, CHUNK)
                    return total + mul(rows[:, pl.ds(at, CHUNK)], hot)

                sum_s[u] = lax.fori_loop(0, (left + CHUNK - 1) // CHUNK, chunk, sum_s[u])

        for u, i in enumerate(todo):
            x = sum_s[u].astype(bf16)
            xt_ref[i] = x
            nat = mul(mixer[...], x, NT)
            m = mul(nat[lanes:].astype(bf16), x)
            here = slice(i * GROUP, (i + 1) * GROUP)
            for c in range(ranks // per_tile):
                tile = None
                for s in range(per_tile):
                    at = GROUP * (c * per_tile + s)
                    slab = m[at : at + GROUP]
                    one = jnp.where(example < per_tile, slab[:, :128], slab[:, 128:])
                    one = turn(one, s * tokens)
                    mine = place == (example + s) % per_tile
                    tile = one if s == 0 else jnp.where(mine, one, tile)
                pair_s[here, c * 128 : c * 128 + 128] = tile
            for t in range(tokens):
                nat_s[t, here, :features] = nat[GROUP * t : GROUP * t + GROUP]

    all_groups()
    pair = pair_s[...].T
    pair_ref[...] = pair
    centred = pair - jnp.mean(pair, axis=0, keepdims=True)
    scale = lax.rsqrt(jnp.mean(centred * centred, axis=0, keepdims=True) + EPS)
    normed_ref[...] = (centred * scale * gain[...] + bias[...]).astype(bf16)

    for t in range(tokens):
        at = slice(t * features, (t + 1) * features)
        res_ref[at, :] = nat_s[t].astype(bf16).T[:features]


def norm_token(summed, g, gain, bias):
    centred = summed - jnp.mean(summed, axis=0, keepdims=True)
    scale = lax.rsqrt(jnp.mean(centred * centred, axis=0, keepdims=True) + EPS)
    hat = centred * scale
    q = g * gain
    g_hat = g * hat
    mean_q = jnp.mean(q, axis=0, keepdims=True)
    mean_qx = jnp.mean(q * hat, axis=0, keepdims=True)
    return (hat * gain + bias).astype(bf16), (scale * (q - mean_q - hat * mean_qx)).astype(bf16), g_hat


def standing(row):
    return jnp.broadcast_to(row[...], (128, row.shape[1])).T


def folded(value):
    return sum(value[:, i : i + 128] for i in range(0, value.shape[1], 128))


def doubled(value, lanes):
    return jnp.concatenate([value] * (lanes // value.shape[1]), axis=1)


def final_kernel(features, res, cot, gain, bias, out, gmix, gain_acc, bias_acc, cot_s, out_s):
    @pl.when(pl.program_id(0) == 0)
    def clear():
        gain_acc[...] = jnp.zeros_like(gain_acc)
        bias_acc[...] = jnp.zeros_like(bias_acc)

    cot_s[...] = cot[...].T
    unroll = 8

    def some(k, carry):
        hats, gs = [], []
        for u in range(unroll):
            at = pl.ds(pl.multiple_of((k * unroll + u) * features, 32), features)
            g = cot_s[at, :].astype(f32)
            out_s[at, :], gmix[at, :], g_hat = norm_token(res[at, :].astype(f32), g, gain[...], bias[...])
            hats.append(g_hat)
            gs.append(g)
        gain_acc[...] += sum(hats)
        bias_acc[...] += sum(gs)
        return carry

    lax.fori_loop(0, res.shape[0] // features // unroll, some, 0)
    out[...] = out_s[...].T


def mlp_kernel(
    features,
    every,
    normed,
    res,
    cot,
    b_up,
    b_down,
    gain,
    bias,
    out,
    mix,
    hidden,
    g_pre,
    g_normed,
    gain_acc,
    bias_acc,
    up_acc,
    down_acc,
    pre_s,
    cot_s,
    out_s,
    up_s,
    down_s,
):
    pairs, lanes = g_normed.shape
    units = hidden.shape[0]
    width = res.shape[0]
    now = pl.ds(pl.multiple_of(pl.program_id(0) * lanes, lanes), lanes)
    unit_tile = 256
    token_tile = 4 * features

    @pl.when(pl.program_id(0) == 0)
    def clear():
        for acc in (gain_acc, bias_acc, up_acc, down_acc):
            acc[...] = jnp.zeros_like(acc)
        up_s[...] = standing(b_up)
        down_s[...] = standing(b_down)

    cot_s[...] = cot[...].T
    for at in range(0, units, unit_tile):
        here = slice(at, at + unit_tile)
        pre = mul(every[here, :pairs], normed[...]) + doubled(up_s[here, :], lanes)
        pre_s[here, :] = pre
        hidden[here, now] = gelu(pre).astype(bf16)
    wide_gain, wide_bias = doubled(gain[...], lanes), doubled(bias[...], lanes)

    def fm_tile(first):
        return mul(every[:, pairs + first : pairs + first + token_tile], hidden[:, now], TN)

    ahead = fm_tile(0)
    for first in range(0, width, token_tile):
        tile = ahead
        if first + token_tile < width:
            ahead = fm_tile(first + token_tile)
        hats, gs = [], []
        for u in range(4):
            here = slice(first + u * features, first + (u + 1) * features)
            fm = tile[u * features : (u + 1) * features, :] + doubled(down_s[here, :], lanes)
            g = cot_s[here, :].astype(f32)
            summed = res[here, :].astype(f32) + fm.astype(bf16).astype(f32)
            out_s[here, :], g_mix, g_hat = norm_token(summed, g, wide_gain, wide_bias)
            mix[here, now] = g_mix
            down_acc[here, :] += folded(g_mix.astype(f32))
            hats.append(folded(g_hat))
            gs.append(folded(g))
        gain_acc[...] += sum(hats)
        bias_acc[...] += sum(gs)
    for at in range(0, units, unit_tile):
        here = slice(at, at + unit_tile)
        g_hidden = mul(every[here, pairs:], mix[:, now])
        value = (g_hidden * gelu_slope(pre_s[here, :])).astype(bf16)
        g_pre[here, now] = value
        up_acc[here, :] += folded(value.astype(f32))
    g_normed[...] = mul(every[:, :pairs], g_pre[:, now], TN)
    out[...] = out_s[...].T


def to_natural(mix, nat_s, features, block=0):
    count, examples, _ = nat_s.shape
    now = pl.ds(pl.multiple_of(block * examples, examples), examples)

    for t in range(count):
        nat_s[t, :, :features] = mix[t * features : (t + 1) * features, now].T


def natural_groups(nat_s, features):
    found = []
    for first in range(0, nat_s.shape[1], 2 * GROUP):
        mixes = nat_s[:, first : first + 2 * GROUP, :features].astype(f32)
        found += [mixes[:, :GROUP], mixes[:, GROUP:]]
    return [item.reshape(-1, features).astype(bf16) for item in found]


def early_kernel(gmix, xt, mixer, gt, mix_acc, nat_s):
    _, features, lanes = xt.shape
    groups = nat_s.shape[1] // GROUP
    base = pl.program_id(0) * groups
    rows = nat_s.shape[0] * GROUP
    own = slice(lanes - rows, lanes)

    @pl.when(pl.program_id(0) == 0)
    def clear():
        mix_acc[...] = jnp.zeros_like(mix_acc)

    to_natural(gmix, nat_s, features)

    total = mix_acc[...]
    for u, g_mix in enumerate(natural_groups(nat_s, features)):
        total = total + mul(g_mix, xt[u])
        gt[base + u] = mul(g_mix, mixer[own], TN).astype(bf16)
    mix_acc[...] = total


def back_kernel(start, gn, pair, gain, gmix, xt, mixer, early, *refs):
    *before, gt, gain_acc, bias_acc, mix_acc, project_acc, gp_s, nat_s = refs
    sums = (gain_acc, bias_acc, mix_acc, project_acc)
    _, features, lanes = xt.shape
    block = start + pl.program_id(0)
    groups = gp_s.shape[0] // GROUP
    base = block * groups
    tokens = lanes // GROUP
    ranks = gp_s.shape[1] // tokens
    per_tile = 128 // tokens
    rows = nat_s.shape[0] * GROUP

    @pl.when(pl.program_id(0) == 0)
    def clear():
        for i, acc in enumerate(sums):
            acc[...] = before[i][...] if before else jnp.zeros_like(acc)

    values = pair[...]
    centred = values - jnp.mean(values, axis=0, keepdims=True)
    scale = lax.rsqrt(jnp.mean(centred * centred, axis=0, keepdims=True) + EPS)
    hat = centred * scale
    g = gn[...]
    gain_acc[...] += g * hat
    bias_acc[...] += g
    h = g * gain[...]
    mean_h = jnp.mean(h, axis=0, keepdims=True)
    mean_hx = jnp.mean(h * hat, axis=0, keepdims=True)
    gp_s[...] = (scale * (h - mean_h - hat * mean_hx)).T
    to_natural(gmix, nat_s, features, block)
    example = lax.broadcasted_iota(jnp.int32, (GROUP, 128), 0)
    place = lax.broadcasted_iota(jnp.int32, (GROUP, 128), 1) // tokens
    own = place == example % per_tile
    keep_low = jnp.logical_and(own, example < per_tile)
    keep_high = jnp.logical_and(own, example >= per_tile)

    project = mixer[lanes:]
    stacked = xt[...].reshape(groups * features, lanes)
    projected = mul(stacked, project, NT).astype(bf16)
    g_pairs, g_parts = [], []
    for u in range(groups):
        here = slice(u * GROUP, (u + 1) * GROUP)
        slabs = []
        for j in range(ranks):
            c, s = j // per_tile, j % per_tile
            one = turn(gp_s[here, c * 128 : c * 128 + 128], -s * tokens)
            slabs.append(
                jnp.concatenate([jnp.where(keep_low, one, 0.0), jnp.where(keep_high, one, 0.0)], axis=1)
            )
        g_pairs.append(jnp.concatenate(slabs, axis=0).astype(bf16))
        g_parts.append(mul(xt[u], g_pairs[u], NT).astype(bf16))
    g_projected = jnp.concatenate(g_parts, axis=0)
    project_acc[...] += mul(stacked, g_projected, TN)
    shared = mul(g_projected, project)
    mix_total = mix_acc[...]
    for u, g_mix in enumerate(natural_groups(nat_s, features)):
        mix_total = mix_total + mul(g_mix, xt[u])
        mine = slice(u * features, (u + 1) * features)
        part = mul(projected[mine], g_pairs[u]) + mul(g_mix, mixer[:rows], TN) + shared[mine]
        gt[base + u] = (part + early[base + u].astype(f32)).astype(bf16)
    mix_acc[...] = mix_total


def spread_kernel(start, first_half, starts, ends, gt, out):
    step = start + pl.program_id(0)
    chunks = out.shape[1] // CHUNK
    last = starts.shape[0] - 1
    span = CHUNK // 128 + 1

    for c in range(chunks):
        number = step * chunks + c
        first = jnp.minimum(first_half[number], last + 1 - span)
        lows, highs, values = [], [], []
        for i in range(span):
            half = first + i
            lows.append(starts[pl.ds(half, 1), :])
            highs.append(ends[pl.ds(half, 1), :])
            values.append(gt[half // 2, :, pl.ds(pl.multiple_of(half % 2 * 128, 128), 128)])
        low = jnp.concatenate(lows, axis=1) - number * CHUNK
        high = jnp.concatenate(highs, axis=1) - number * CHUNK
        hot = one_hot(low, high, CHUNK)
        part = mul(jnp.concatenate(values, axis=1), hot, NT)
        out[:, c * CHUNK : (c + 1) * CHUNK] = part.astype(bf16)


def passing(kernel, given, previous):
    if not previous:
        return kernel, {}
    more = len(previous)
    skip = lambda *refs: kernel(*refs[:given], *refs[given + more :])
    return skip, {given + i: i for i in range(more)}


HBM, VMEM = pltpu.HBM, pltpu.VMEM
INSIDE = pl.BlockSpec(memory_space=pltpu.VMEM)


def held(*arrays):
    return [pltpu.with_memory_space_constraint(array, pltpu.VMEM) for array in arrays]


def away(*arrays):
    return [pltpu.with_memory_space_constraint(array, pltpu.HBM) for array in arrays]


def whole(shape):
    return pl.BlockSpec(shape, lambda *_: (0,) * len(shape))


def rank_of(tokens):
    per_tile = 128 // tokens
    slab, example = np.arange(per_tile)[:, None], np.arange(GROUP)[None, :]
    return np.eye(per_tile, dtype=np.float32)[(slab + example) % per_tile]


def make_mixer(w_res, w_comp, p_proj):
    tokens = w_res.shape[0]
    fm_tokens = tokens - w_comp.shape[0]
    mix = w_res.astype(f32) + jnp.pad(w_comp.astype(f32), ((fm_tokens, 0), (0, 0)))
    mix = jnp.broadcast_to(mix[:, None, :], (tokens, GROUP, tokens))
    by_tile = p_proj.T.astype(f32).reshape(-1, 128 // tokens, tokens)
    project = jnp.einsum("cqt,seq->cset", by_tile, rank_of(tokens))
    both = jnp.concatenate([mix, project.reshape(-1, GROUP, tokens)], axis=0)
    wide = both[:, :, None, :] * np.eye(GROUP, dtype=np.float32)[None, :, :, None]
    return wide.reshape(both.shape[0] * GROUP, GROUP * tokens).astype(bf16)


def token_stage(offs, starts, ends, rows, mixer, gain, bias, tokens):
    features, row_total = rows.shape
    group_count, lanes = starts.shape
    examples = group_count * GROUP
    pairs = gain.shape[0]
    groups = BLOCK // GROUP
    return pl.pallas_call(
        tokens_kernel,
        name="tokens",
        grid_spec=pltpu.PrefetchScalarGridSpec(
            num_scalar_prefetch=1,
            grid=(examples // BLOCK,),
            in_specs=[
                pl.BlockSpec((groups, lanes), lambda i, _: (i, 0)),
                pl.BlockSpec((groups, lanes), lambda i, _: (i, 0)),
                pl.BlockSpec(memory_space=pltpu.VMEM),
                whole(mixer.shape),
                whole(gain.shape),
                whole(bias.shape),
            ],
            out_specs=[
                pl.BlockSpec((groups, features, lanes), lambda i, _: (i, 0, 0)),
                pl.BlockSpec((pairs, BLOCK), lambda i, _: (0, i)),
                pl.BlockSpec((pairs, BLOCK), lambda i, _: (0, i)),
                pl.BlockSpec((tokens * features, BLOCK), lambda i, _: (0, i)),
            ],
            scratch_shapes=[
                pltpu.VMEM((BLOCK, pairs), f32),
                pltpu.VMEM((tokens, BLOCK, 256), f32),
                pltpu.VMEM((groups, features, lanes), f32),
            ],
        ),
        out_shape=[
            HBM((group_count, features, lanes), bf16),
            HBM((pairs, examples), f32),
            HBM((pairs, examples), bf16),
            HBM((tokens * features, examples), bf16),
        ],
        compiler_params=params(36),
        cost_estimate=pl.CostEstimate(
            flops=2 * features * lanes * (row_total * 2 + 1000 * group_count),
            bytes_accessed=row_total * features * 2 + 30 * examples * 1024,
            transcendentals=0,
        ),
    )(offs, starts, ends, *away(rows), mixer, gain, bias)


def final_stage(res, cot, gain, bias, features, part):
    width, examples = res.shape
    at = (width - part) // part
    tall = pl.BlockSpec((part, BLOCK), lambda i: (at, i))
    flat = pl.BlockSpec((BLOCK, part), lambda i: (i, at))
    return pl.pallas_call(
        functools.partial(final_kernel, features),
        name="final_comp",
        grid=(examples // BLOCK,),
        in_specs=[tall, flat, whole(gain.shape), whole(bias.shape)],
        out_specs=[flat, pl.BlockSpec((part, BLOCK), lambda i: (0, i)), whole((features, BLOCK)), whole((features, BLOCK))],
        out_shape=[
            HBM((examples, width), bf16),
            HBM((part, examples), bf16),
            jax.ShapeDtypeStruct((features, BLOCK), f32),
            jax.ShapeDtypeStruct((features, BLOCK), f32),
        ],
        scratch_shapes=[pltpu.VMEM((part, BLOCK), bf16), pltpu.VMEM((part, BLOCK), bf16)],
        compiler_params=params(16),
        cost_estimate=pl.CostEstimate(
            flops=200 * part * examples, bytes_accessed=8 * part * examples, transcendentals=0
        ),
    )(*away(res, cot), gain, bias)


def mlp_stage(every, normed, res, cot, b_up, b_down, gain, bias, features, previous):
    units, columns = every.shape
    pairs, examples = normed.shape
    part = columns - pairs
    lanes = 2 * BLOCK
    wide = lambda rows: pl.BlockSpec((rows, lanes), lambda i: (0, i))
    flat = pl.BlockSpec((lanes, part), lambda i: (i, 0))
    every, normed, res, cot, previous = away(every, normed, res, cot, previous)
    operands = (every, normed, res, cot, b_up, b_down, gain, bias)
    kernel, aliases = passing(functools.partial(mlp_kernel, features), len(operands), (previous,))
    return pl.pallas_call(
        kernel,
        name="mlp",
        grid=(examples // lanes,),
        in_specs=[
            pl.BlockSpec(memory_space=pltpu.VMEM),
            wide(pairs),
            wide(part),
            flat,
            whole(b_up.shape),
            whole(b_down.shape),
            whole(gain.shape),
            whole(bias.shape),
        ]
        + [pl.BlockSpec(memory_space=pl.ANY)],
        out_specs=[
            flat,
            INSIDE,
            INSIDE,
            INSIDE,
            wide(pairs),
            whole((features, BLOCK)),
            whole((features, BLOCK)),
            whole((units, BLOCK)),
            whole((part, BLOCK)),
        ],
        out_shape=[
            HBM(previous.shape, bf16),
            VMEM((part, examples), bf16),
            VMEM((units, examples), bf16),
            VMEM((units, examples), bf16),
            HBM((pairs, examples), f32),
            jax.ShapeDtypeStruct((features, BLOCK), f32),
            jax.ShapeDtypeStruct((features, BLOCK), f32),
            jax.ShapeDtypeStruct((units, BLOCK), f32),
            jax.ShapeDtypeStruct((part, BLOCK), f32),
        ],
        scratch_shapes=[
            pltpu.VMEM((units, lanes), f32),
            pltpu.VMEM((part, lanes), bf16),
            pltpu.VMEM((part, lanes), bf16),
            pltpu.VMEM((units, BLOCK), f32),
            pltpu.VMEM((part, BLOCK), f32),
        ],
        input_output_aliases=aliases,
        compiler_params=params(38),
        cost_estimate=pl.CostEstimate(
            flops=4 * units * columns * examples,
            bytes_accessed=2 * units * columns + 20 * part * examples,
            transcendentals=2 * units * examples,
        ),
    )(*operands, previous)


def early_stage(gmix, xt, mixer):
    group_count, features, lanes = xt.shape
    part, examples = gmix.shape
    count = part // features
    return pl.pallas_call(
        early_kernel,
        name="early",
        grid=(examples // BLOCK,),
        in_specs=[
            pl.BlockSpec((part, BLOCK), lambda i: (0, i)),
            pl.BlockSpec((BLOCK // GROUP, features, lanes), lambda i: (i, 0, 0)),
            whole(mixer.shape),
        ],
        out_specs=[INSIDE, whole((count * GROUP, lanes))],
        out_shape=[
            VMEM((group_count, features, lanes), bf16),
            jax.ShapeDtypeStruct((count * GROUP, lanes), f32),
        ],
        scratch_shapes=[pltpu.VMEM((count, BLOCK, 256), bf16)],
        compiler_params=params(16),
        cost_estimate=pl.CostEstimate(
            flops=2 * features * lanes * 500 * group_count,
            bytes_accessed=group_count * features * lanes * 8,
            transcendentals=0,
        ),
    )(*away(gmix, xt), mixer)


def back_stage(gn, pair, gain, gmix, xt, mixer, gt, start, count, before):
    pairs, examples = pair.shape
    group_count, features, lanes = xt.shape
    ranked = mixer.shape[0] - lanes
    fm_tokens = gmix.shape[0] // features
    wide = pl.BlockSpec((pairs, BLOCK), lambda i: (0, start + i))
    sums = [(pairs, BLOCK), (pairs, BLOCK), (fm_tokens * GROUP, lanes), (lanes, ranked)]
    gn, pair, xt = away(gn, pair, xt)
    gmix, gt = held(gmix, gt)
    by_group = pl.BlockSpec((BLOCK // GROUP, features, lanes), lambda i: (start + i, 0, 0))
    operands = (gn, pair, gain, gmix, xt, mixer, gt, *before)
    return pl.pallas_call(
        functools.partial(back_kernel, start),
        name="back",
        grid=(count,),
        in_specs=[wide, wide, whole(gain.shape), INSIDE, by_group, whole(mixer.shape), INSIDE]
        + [whole(item.shape) for item in before],
        out_specs=[INSIDE] + [whole(shape) for shape in sums],
        out_shape=[VMEM((group_count, features, lanes), bf16)]
        + [jax.ShapeDtypeStruct(shape, f32) for shape in sums],
        scratch_shapes=[
            pltpu.VMEM((BLOCK, pairs), f32),
            pltpu.VMEM((fm_tokens, BLOCK, 256), bf16),
        ],
        input_output_aliases={6: 0},
        compiler_params=params(20),
        cost_estimate=pl.CostEstimate(
            flops=2 * features * lanes * 1400 * BLOCK // GROUP * count,
            bytes_accessed=40 * BLOCK * count * 1024,
            transcendentals=0,
        ),
    )(*operands)


def exact(value, selector, dims=NN):
    total = None
    for _ in range(3):
        piece = value.astype(bf16)
        value = value - piece.astype(f32)
        total = mul(piece, selector, dims) if total is None else total + mul(piece, selector, dims)
    return total


def ones_where(condition):
    return jnp.where(condition, 1.0, 0.0).astype(bf16)


def by_token_order(pairs, tokens):
    ranks = pairs // tokens
    row = lax.broadcasted_iota(jnp.int32, (pairs, pairs), 0)
    lane = lax.broadcasted_iota(jnp.int32, (pairs, pairs), 1)
    return ones_where((row % tokens) * ranks + row // tokens == lane)


def small_rows(tokens, pairs, units, width, features):
    counts = [tokens, pairs // 128, pairs // 128, units // 128, width // 128, -(-features // 128)]
    counts.append(counts[-1])
    starts = np.cumsum([0] + counts)
    return [(int(start), count) for start, count in zip(starts, counts)], -(-int(starts[-1]) // 8) * 8


def small_kernel(tokens, places, gain_acc, bias_acc, mix_fm, mix_comp, project, up, down, gains, biases, out):
    def put(place, row):
        start, count = place
        for i in range(count):
            piece = row[:, i * 128 : i * 128 + 128]
            out[start + i : start + i + 1, : piece.shape[1]] = piece

    def lying(column):
        return jnp.sum(column.T, axis=0, keepdims=True)

    out[...] = jnp.zeros_like(out)
    lanes = mix_fm.shape[1]
    ranked = project.shape[1]
    per_tile = 128 // tokens
    mix = jnp.concatenate([mix_fm[...], mix_comp[...]], axis=0)
    row = lax.broadcasted_iota(jnp.int32, mix.shape, 0) % GROUP
    lane = lax.broadcasted_iota(jnp.int32, mix.shape, 1) // tokens
    mix = jnp.where(row == lane, mix, 0.0)
    fold = ones_where(
        lax.broadcasted_iota(jnp.int32, (lanes, tokens), 0) % tokens
        == lax.broadcasted_iota(jnp.int32, (lanes, tokens), 1)
    )
    folded_mix = exact(mix, fold).reshape(tokens, GROUP, tokens)
    row = lax.broadcasted_iota(jnp.int32, project.shape, 0) // tokens
    lane = lax.broadcasted_iota(jnp.int32, project.shape, 1) % GROUP
    cells = jnp.where(row == lane, project[...], 0.0).reshape(GROUP, tokens, ranked)
    cells = jnp.sum(cells, axis=0)
    ranks = ranked // GROUP
    row = lax.broadcasted_iota(jnp.int32, (ranks, ranked), 0)
    lane = lax.broadcasted_iota(jnp.int32, (ranks, ranked), 1)
    slab = lane // GROUP
    rank = slab // per_tile * per_tile + (lane % GROUP + slab % per_tile) % per_tile
    pick = ones_where(row == rank)
    projected = None
    for _ in range(3):
        piece = cells.astype(bf16)
        cells = cells - piece.astype(f32)
        part = mul(pick, piece, NT)
        projected = part if projected is None else projected + part
    out[:ranks, :tokens] = projected
    out[:tokens, tokens : 2 * tokens] = jnp.sum(folded_mix, axis=1)
    both = jnp.concatenate([lying(gain_acc[...]), lying(bias_acc[...])], axis=0)
    both = exact(both, by_token_order(both.shape[1], tokens))
    put(places[1], both[:1])
    put(places[2], both[1:])
    put(places[3], lying(up[...]))
    put(places[4], lying(down[...]))
    put(places[5], lying(gains[0] + gains[1]))
    put(places[6], lying(biases[0] + biases[1]))


def small_stage(tokens, places, rows, gain_acc, bias_acc, mix_fm, mix_comp, project, up, down, gains, biases):
    def kernel(*refs):
        *given, gain_0, gain_1, bias_0, bias_1, out = refs
        small_kernel(tokens, places, *given, (gain_0[...], gain_1[...]), (bias_0[...], bias_1[...]), out)

    operands = (gain_acc, bias_acc, mix_fm, mix_comp, project, up, down, *gains, *biases)
    return pl.pallas_call(
        kernel,
        name="small",
        out_shape=jax.ShapeDtypeStruct((rows, 128), f32),
        compiler_params=params(16),
        cost_estimate=pl.CostEstimate(flops=10**9, bytes_accessed=4 * 10**6, transcendentals=0),
    )(*operands)


def last_kernel(tokens, places, total, more, *refs):
    *vectors, up, down, p_proj, w_res, w_comp, gain_one, bias_one, b_up, b_down, gain_two, bias_two = refs
    pairs = up.shape[1]
    value = total[...] + more[...].astype(f32)
    down[...] = value[:, pairs:]
    up[...] = exact(value[:, :pairs], by_token_order(pairs, tokens))
    vector = sum([ref[...] for ref in vectors])
    p_proj[...] = vector[: p_proj.shape[0], :tokens]
    w_res[...] = vector[:tokens, tokens : 2 * tokens]
    w_comp[...] = vector[tokens - w_comp.shape[0] : tokens, tokens : 2 * tokens]
    rest = (gain_one, bias_one, b_up, b_down, gain_two, bias_two)
    for (start, count), ref in zip(places[1:], rest):
        if ref.shape[0] == 1:
            row = [vector[start + i : start + i + 1] for i in range(count)]
            ref[...] = jnp.concatenate(row, axis=1)[:, : ref.shape[1]]
        else:
            ref[...] = vector[start : start + count]


def last_stage(total, more, vectors, places, pairs, tokens, features, comp_tokens):
    rows, columns = total.shape
    shapes = [(rows, pairs), (rows, columns - pairs), (pairs // tokens, tokens), (tokens, tokens), (comp_tokens, tokens)]
    shapes += [(count, 128) for _, count in places[1:-2]] + [(1, features)] * 2
    return pl.pallas_call(
        functools.partial(last_kernel, tokens, places),
        name="last",
        out_shape=[jax.ShapeDtypeStruct(shape, f32) for shape in shapes],
        compiler_params=params(16),
        cost_estimate=pl.CostEstimate(
            flops=6 * rows * pairs * pairs, bytes_accessed=10 * rows * columns, transcendentals=0
        ),
    )(total, more, *vectors)


def grad_kernel(rows, parts, table, pre, hidden, normed, mix, *refs):
    *outs, picked_s, normed_s, out_s, arrive, leave = refs
    pairs = normed_s.shape[0]
    width = mix.shape[0]
    bring = pltpu.make_async_copy(normed, normed_s, arrive.at[0])
    bring.start()
    flying = []

    def picked(source):
        for i in range(picked_s.shape[0] // rows):
            start = pl.multiple_of(table[i] * rows, rows)
            picked_s[i * rows : (i + 1) * rows, :] = source[pl.ds(start, rows), :]
        return picked_s[...]

    def send(at, size, value):
        here = pl.ds(at, size)
        out_s[:, here] = value.astype(bf16)
        first = 0
        for out in outs:
            source = out_s.at[pl.ds(first, out.shape[0]), here]
            copy = pltpu.make_async_copy(source, out.at[:, here], leave.at[len(flying)])
            copy.start()
            flying.append(copy)
            first += out.shape[0]

    part = width // parts
    left = picked(hidden)
    for i in range(parts):
        send(pairs + i * part, part, mul(left, mix[i * part : (i + 1) * part, :], NT))
    bring.wait()
    send(0, pairs, mul(picked(pre), normed_s[...], NT))
    for copy in flying:
        copy.wait()


def grad_stage(tables, pre, hidden, normed, mix, rows):
    units, examples = hidden.shape
    pairs = normed.shape[0]
    columns = pairs + mix.shape[0]
    counts = [table.shape[0] * rows for table in tables]
    count = sum(counts)
    parts = 4
    anywhere = pl.BlockSpec(memory_space=pl.ANY)
    pre, hidden, mix = held(pre, hidden, mix)
    return pl.pallas_call(
        functools.partial(grad_kernel, rows, parts),
        name="weight_grads",
        grid_spec=pltpu.PrefetchScalarGridSpec(
            num_scalar_prefetch=1,
            grid=(1,),
            in_specs=[INSIDE, INSIDE, anywhere, INSIDE],
            out_specs=[anywhere] * len(counts),
            scratch_shapes=[
                pltpu.VMEM((count, examples), bf16),
                pltpu.VMEM((pairs, examples), bf16),
                pltpu.VMEM((count, columns), bf16),
                pltpu.SemaphoreType.DMA((1,)),
                pltpu.SemaphoreType.DMA(((1 + parts) * len(counts),)),
            ],
        ),
        out_shape=[HBM((size, columns), bf16) for size in counts],
        compiler_params=params(16),
        cost_estimate=pl.CostEstimate(
            flops=2 * count * examples * columns,
            bytes_accessed=2 * count * columns + 2 * examples * (2 * units + columns),
            transcendentals=0,
        ),
    )(jnp.concatenate(tables), pre, hidden, *away(normed), mix)


def spread_stage(first_half, starts, ends, gt, row_total, start, count, previous):
    group_count, features, lanes = gt.shape
    operands = (starts.reshape(-1, 128), ends.reshape(-1, 128), *held(gt))
    previous = away(*previous)
    kernel, aliases = passing(functools.partial(spread_kernel, start), len(operands) + 1, previous)
    return pl.pallas_call(
        kernel,
        name="spread",
        grid_spec=pltpu.PrefetchScalarGridSpec(
            num_scalar_prefetch=1,
            grid=(count,),
            in_specs=[whole(operands[0].shape), whole(operands[1].shape), INSIDE]
            + [pl.BlockSpec(memory_space=pl.ANY)] * len(previous),
            out_specs=pl.BlockSpec((features, SPREAD_ROWS), lambda i, _: (0, start + i)),
        ),
        out_shape=HBM((features, row_total), bf16),
        input_output_aliases=aliases,
        compiler_params=params(16),
        cost_estimate=pl.CostEstimate(
            flops=4 * features * lanes * SPREAD_ROWS * count,
            bytes_accessed=SPREAD_ROWS * count * features * 4,
            transcendentals=0,
        ),
    )(first_half, *operands, *previous)


def bag_bounds(lengths):
    ends = jnp.cumsum(lengths.reshape(-1))
    starts = ends - lengths.reshape(-1)
    return starts, ends


def column(vector, lanes=BLOCK):
    return jnp.broadcast_to(vector[:, None], (vector.shape[0], lanes))


def gelu(v):
    inner = np.sqrt(2 / np.pi).astype(np.float32) * (v + 0.044715 * (v * v * v))
    return 0.5 * v * (1.0 + jnp.tanh(inner))


def gelu_slope(v):
    root = np.sqrt(2 / np.pi).astype(np.float32)
    bent = jnp.tanh(root * (v + 0.044715 * (v * v * v)))
    return 0.5 * (1.0 + bent) + 0.5 * v * (1.0 - bent * bent) * root * (1.0 + 3 * 0.044715 * (v * v))


def shards(
    embed_rows,
    lengths,
    cotangent,
    p_proj,
    gain_one,
    bias_one,
    w_up,
    b_up,
    w_down,
    b_down,
    w_comp,
    w_res,
    gain_two,
    bias_two,
):
    links = Links()
    tokens = w_res.shape[0]
    features = embed_rows.shape[1]
    ranks = p_proj.shape[1]
    pairs = tokens * ranks
    row_total = embed_rows.shape[0]
    fm_width = b_down.shape[0]
    examples = cotangent.shape[0]

    def by_rank(vector):
        return jnp.swapaxes(vector.reshape(-1, tokens, ranks), 1, 2).reshape(vector.shape)

    def by_token(vector):
        return jnp.swapaxes(vector.reshape(-1, ranks, tokens), 1, 2).reshape(vector.shape)

    every = links.gather(jnp.concatenate([by_rank(w_up.T), w_down], axis=1))

    starts, ends = bag_bounds(lengths)
    lanes = GROUP * tokens
    starts = starts.reshape(-1, lanes)
    ends = ends.reshape(-1, lanes)
    offs = jnp.concatenate([starts[:, 0], ends[-1:, -1]])
    bases = jnp.arange(row_total // CHUNK, dtype=jnp.int32) * CHUNK
    half_ends = ends.reshape(-1, 128)[:, 127]
    first_half = jnp.sum((half_ends[None, :] <= bases[:, None]).astype(jnp.int32), axis=1)
    mixer = make_mixer(w_res, w_comp, p_proj)
    gain_a, bias_a = column(by_rank(gain_one)), column(by_rank(bias_one))
    gain_b, bias_b = column(gain_two), column(bias_two)
    down_bias = column(b_down)

    xt, pair, normed, res = token_stage(
        offs, starts, ends, embed_rows.T, mixer, gain_a, bias_a, tokens
    )
    out, mix_comp, gain_acc1, bias_acc1 = final_stage(res, cotangent, gain_b, bias_b, features, fm_width)
    mix_comp, first_half = lax.optimization_barrier((mix_comp, first_half))
    gt, mix_acc1 = early_stage(mix_comp, xt, mixer)
    gt, res = lax.optimization_barrier((gt, res))
    out, mix, hidden, g_pre, g_normed, gain_acc0, bias_acc0, up_acc, down_acc = mlp_stage(
        every, normed, res, cotangent, b_up[None, :], b_down[None, :], gain_b, bias_b, features, out
    )

    unit_rows = links.unit_rows(w_down.shape[0])
    tables, rows, (g_pre, hidden) = links.shards(unit_rows, g_pre, hidden)
    ring = links.ring(unit_rows)
    gradients = lambda *tables: grad_stage(tables, g_pre, hidden, normed, mix, rows)
    sent_first, sent = gradients(tables[0], tables[2])
    crossing_first = links.to_other_core(sent_first)
    crossing = links.to_other_core(sent)
    g_pre, hidden, sent = lax.optimization_barrier((g_pre, hidden, sent))
    (mine,) = gradients(tables[1])
    ring.add(*lax.optimization_barrier((mine, crossing_first)))
    g_pre, hidden = ring.start((g_pre, hidden))
    (mine,) = gradients(tables[3])
    mine, g_normed, gt = ring.finish((mine, g_normed, gt))
    ring.add(*lax.optimization_barrier((mine, crossing)))

    blocks = examples // BLOCK
    cuts = [blocks * i // 2 for i in range(3)]
    sums = []
    for i in range(2):
        g_normed, gt, sums = ring.start((g_normed, gt, sums))
        gt, *sums = back_stage(
            g_normed, pair, gain_a, mix, xt, mixer, gt, cuts[i], cuts[i + 1] - cuts[i], sums
        )
        g_normed, gt, sums = ring.finish((g_normed, gt, sums))
    gain_acc, bias_acc, mix_acc0, project_acc = sums
    places, rows = small_rows(tokens, pairs, b_up.shape[0], fm_width, features)
    vector = small_stage(
        tokens,
        places,
        rows,
        gain_acc,
        bias_acc,
        mix_acc0,
        mix_acc1,
        project_acc,
        up_acc,
        down_acc,
        (gain_acc0, gain_acc1),
        (bias_acc0, bias_acc1),
    )

    steps = row_total // SPREAD_ROWS
    swaps = links.rounds()
    cuts = [0, steps * 4 // 9, steps * 6 // 9, steps]
    rows_grad = ()
    for i in range(3):
        if i < 2:
            vector, gt, rows_grad = ring.start((vector, gt, rows_grad))
        far = [swap(vector) for swap in swaps[i]]
        rows_grad = spread_stage(
            first_half, starts, ends, gt, row_total, cuts[i], cuts[i + 1] - cuts[i], rows_grad
        )
        far, gt, rows_grad = lax.optimization_barrier((far, gt, (rows_grad,)))
        vector = sum(far, vector)
        if i != 1:
            vector, gt, rows_grad = ring.finish((vector, gt, rows_grad))
    for some in swaps[3:]:
        vector = sum([swap(vector) for swap in some], vector)
    vectors = [vector]
    up_grad, down_grad, proj_grad, res_grad, comp_grad, *rest = last_stage(
        *ring.end(), vectors, places, pairs, tokens, features, w_comp.shape[0]
    )
    rest = [item.reshape(-1) for item in rest]
    return (
        out,
        rows_grad[0].T,
        proj_grad.T,
        rest[0],
        rest[1],
        up_grad.T,
        rest[2],
        down_grad,
        rest[3],
        comp_grad,
        res_grad,
        rest[4],
        rest[5],
    )


def ring_order(chips):
    return list(range(0, chips, 2)) + list(range(chips - 1, 0, -2))


def added(*terms):
    return sum([term.astype(f32) for term in terms[1:]], terms[0].astype(f32))


def ring_shards(chips):
    order = ring_order(chips)
    reach = chips // 2
    steps = [reach]
    for distance in range(reach - 1, 0, -1):
        steps += [distance, -distance]
    steps.append(0)
    return [[order[(order.index(chip) + step) % chips] for step in steps] for chip in range(chips)]


class Ring:
    def __init__(self, rows):
        self.rows = rows
        self.chips = lax.axis_size("dp") // 2
        self.order = ring_order(self.chips)
        self.reach = self.chips // 2
        self.shards = []
        self.left = self.reach
        self.flying = None
        self.send = None
        self.total = None

    def add(self, *terms):
        terms = [term.reshape(-1, self.rows, term.shape[-1]) for term in terms]
        self.shards += [[term[i] for term in terms] for i in range(terms[0].shape[0])]

    def ahead(self, distance):
        return self.shards[1 + 2 * (self.reach - 1 - distance)]

    def behind(self, distance):
        return self.shards[2 + 2 * (self.reach - 1 - distance)]

    def along(self, value, step):
        order, chips = self.order, self.chips
        pairs = [
            (2 * order[i] + core, 2 * order[(i + step) % chips] + core)
            for i in range(chips)
            for core in range(2)
        ]
        return lax.ppermute(value, "dp", pairs)

    def start(self, others):
        if self.left < 0:
            return others
        if self.send is None:
            middle = added(*self.shards[0]).astype(bf16)
            rows = middle.shape[0] // 2
            self.send = [middle[:rows], middle[rows:]]
        self.send, others = lax.optimization_barrier((self.send, others))
        if self.left > 0:
            self.flying = (self.along(self.send[0], 1), self.along(self.send[1], -1))
        else:
            pairs = [(i, i ^ 1) for i in range(lax.axis_size("branch"))]
            self.flying = (lax.ppermute(self.send[0], "branch", pairs),)
        return others

    def finish(self, others):
        if self.flying is None:
            return others
        arrived, others = lax.optimization_barrier((self.flying, others))
        self.flying = None
        self.left -= 1
        if self.left < 0:
            self.more = arrived[0]
        elif self.left == 0:
            self.total = added(*self.shards[-1], *arrived)
            self.send = [self.total.astype(bf16)]
        else:
            one, two = added(*self.ahead(self.left)), added(*self.behind(self.left))
            first, second = arrived[0].astype(f32), arrived[1].astype(f32)
            if self.left == self.reach - 1:
                rows = first.shape[0]
                first = jnp.pad(first, ((0, one.shape[0] - rows), (0, 0)))
                second = jnp.pad(second, ((two.shape[0] - rows, 0), (0, 0)))
            self.send = [(one + first).astype(bf16), (two + second).astype(bf16)]
        return others

    def end(self):
        while self.left >= 0:
            self.start(())
            self.finish(())
        return self.total, self.more


class Links:
    def swaps(self, bits):
        dp, branch = lax.axis_size("dp"), lax.axis_size("branch")
        found = []
        for chosen in range(1, 1 << len(bits)):
            flip = functools.reduce(lambda a, b: a | b, [bit for i, bit in enumerate(bits) if chosen >> i & 1])
            pairs = [(i, i ^ flip) for i in range(dp * branch)]
            found.append(lambda value, pairs=pairs: lax.ppermute(value, ("dp", "branch"), pairs))
        return found

    def rounds(self):
        size = lax.axis_size("dp") * lax.axis_size("branch")
        bits = [1 << i for i in range(size.bit_length() - 1)]
        return [self.swaps(bits[i : i + 2]) for i in range(0, len(bits), 2)]

    def gather(self, own):
        return lax.all_gather(own, "dp", axis=0, tiled=True)

    def unit_rows(self, rows):
        return rows

    def owners(self):
        owners = np.asarray(ring_shards(lax.axis_size("dp") // 2), np.int32)
        table = np.stack([2 * owners + 1, 2 * owners, 2 * owners, 2 * owners + 1], axis=1)
        table = table.reshape(-1, 2 * owners.shape[1])
        return lax.dynamic_index_in_dim(jnp.asarray(table), lax.axis_index("dp"), 0, keepdims=False)

    def shards(self, rows, *units):
        table = self.owners()
        first = 3
        if rows % 16 != 0:
            units = [item.reshape(table.shape[0], rows, -1)[table].reshape(item.shape) for item in units]
            table = jnp.arange(units[0].shape[0] // 96, dtype=jnp.int32)
            rows, first = 96, 1
        half = table.shape[0] // 2
        cuts = [(0, first), (half, half + first), (first, half), (half + first, 2 * half)]
        return [table[a:b] for a, b in cuts], rows, units

    def to_other_core(self, value):
        return lax.ppermute(value, "dp", [(i, i ^ 1) for i in range(lax.axis_size("dp"))])

    def ring(self, rows):
        return Ring(rows)


def solution(mesh):
    spread = P(("dp", "branch"), None)
    in_specs = (
        spread,
        spread,
        spread,
        P(),
        P(),
        P(),
        P(None, "dp"),
        P(),
        P("dp", None),
        P(),
        P(),
        P(),
        P(),
        P(),
    )
    out_specs = (
        spread,
        spread,
        P(),
        P(),
        P(),
        P(None, "dp"),
        P(),
        P("dp", None),
        P(),
        P(),
        P(),
        P(),
        P(),
    )
    return jax.shard_map(shards, mesh=mesh, in_specs=in_specs, out_specs=out_specs, check_vma=False)
```

```python
import functools

import jax
import jax.numpy as jnp
import numpy as np
from jax import lax
from jax.experimental import pallas as pl
from jax.experimental.pallas import tpu as pltpu
from jax.sharding import PartitionSpec as P

EPS = 1e-05
GROUP = 8
BLOCK = 128
CHUNK = 256
SPREAD_ROWS = 16 * CHUNK

f32 = jnp.float32
bf16 = jnp.bfloat16

NN = (((1,), (0,)), ((), ()))
NT = (((1,), (1,)), ((), ()))
TN = (((0,), (0,)), ((), ()))


def mul(left, right, dims=NN):
    return lax.dot_general(left, right, dims, preferred_element_type=f32)


def params(mebibytes):
    return pltpu.CompilerParams(vmem_limit_bytes=mebibytes * 1024 * 1024)


def one_hot(low, high, rows):
    row = lax.broadcasted_iota(jnp.int16, (rows, low.shape[1]), 0)
    inside = jnp.logical_and(row >= low.astype(jnp.int16), row < high.astype(jnp.int16))
    return jnp.where(inside, jnp.ones((), bf16), jnp.zeros((), bf16))


def turn(tile, shift):
    return pltpu.roll(tile, shift % 128, 1) if shift % 128 else tile


def tokens_kernel(
    offs, starts, ends, rows, mixer, gain, bias, xt_ref, pair_ref, normed_ref, fm_ref, comp_ref, pair_s, nat_s, sum_s
):
    step = pl.program_id(0)
    groups = pair_s.shape[0] // GROUP
    row_total = rows.shape[1]
    features = rows.shape[0]
    tokens = nat_s.shape[0]
    ranks = pair_s.shape[1] // tokens
    lanes = tokens * GROUP
    per_tile = 128 // tokens
    span = 2 * CHUNK
    example = lax.broadcasted_iota(jnp.int32, (GROUP, 128), 0)
    place = lax.broadcasted_iota(jnp.int32, (GROUP, 128), 1) // tokens

    def all_groups():
        todo = range(groups)
        bases = []
        for u, i in enumerate(todo):
            first = offs[step * groups + i]
            base = (first // 128) * 128
            bases.append(base)
            low = starts[i : i + 1, :]
            high = ends[i : i + 1, :]
            at = pl.multiple_of(jnp.minimum(base, row_total - span), 128)
            sum_s[u] = mul(rows[:, pl.ds(at, span)], one_hot(low - at, high - at, span))
        for u, i in enumerate(todo):
            base = bases[u] + span
            left = offs[step * groups + i + 1] - base

            @pl.when(left > 0)
            def more(u=u, i=i, base=base, left=left):
                low = starts[i : i + 1, :]
                high = ends[i : i + 1, :]

                def chunk(c, total):
                    wanted = base + c * CHUNK
                    at = pl.multiple_of(jnp.minimum(wanted, row_total - CHUNK), 128)
                    hot = one_hot(jnp.maximum(low, wanted) - at, high - at, CHUNK)
                    return total + mul(rows[:, pl.ds(at, CHUNK)], hot)

                sum_s[u] = lax.fori_loop(0, (left + CHUNK - 1) // CHUNK, chunk, sum_s[u])

        for u, i in enumerate(todo):
            x = sum_s[u].astype(bf16)
            xt_ref[i] = x
            nat = mul(mixer[...], x, NT)
            m = mul(nat[lanes:].astype(bf16), x)
            here = slice(i * GROUP, (i + 1) * GROUP)
            for c in range(ranks // per_tile):
                tile = None
                for s in range(per_tile):
                    at = GROUP * (c * per_tile + s)
                    slab = m[at : at + GROUP]
                    one = jnp.where(example < per_tile, slab[:, :128], slab[:, 128:])
                    one = turn(one, s * tokens)
                    mine = place == (example + s) % per_tile
                    tile = one if s == 0 else jnp.where(mine, one, tile)
                pair_s[here, c * 128 : c * 128 + 128] = tile
            for t in range(tokens):
                nat_s[t, here, :features] = nat[GROUP * t : GROUP * t + GROUP]

    all_groups()
    pair = pair_s[...].T
    pair_ref[...] = pair
    centred = pair - jnp.mean(pair, axis=0, keepdims=True)
    scale = lax.rsqrt(jnp.mean(centred * centred, axis=0, keepdims=True) + EPS)
    normed_ref[...] = (centred * scale * gain[...] + bias[...]).astype(bf16)

    fm_tokens = fm_ref.shape[0] // features
    for t in range(tokens):
        turned = nat_s[t].astype(bf16).T[:features]
        if t < fm_tokens:
            fm_ref[t * features : (t + 1) * features, :] = turned
        else:
            comp_ref[(t - fm_tokens) * features : (t - fm_tokens + 1) * features, :] = turned


def norm_token(summed, g, gain, bias):
    centred = summed - jnp.mean(summed, axis=0, keepdims=True)
    scale = lax.rsqrt(jnp.mean(centred * centred, axis=0, keepdims=True) + EPS)
    hat = centred * scale
    q = g * gain
    g_hat = g * hat
    mean_q = jnp.mean(q, axis=0, keepdims=True)
    mean_qx = jnp.mean(q * hat, axis=0, keepdims=True)
    return (hat * gain + bias).astype(bf16), (scale * (q - mean_q - hat * mean_qx)).astype(bf16), g_hat


def standing(row):
    return jnp.broadcast_to(row[...], (128, row.shape[1])).T


def folded(value):
    return sum(value[:, i : i + 128] for i in range(0, value.shape[1], 128))


def doubled(value, lanes):
    return jnp.concatenate([value] * (lanes // value.shape[1]), axis=1)


def final_kernel(features, res, cot, cot_fm, gain, bias, out, gmix, turned, gain_acc, bias_acc, cot_s, out_s):
    @pl.when(pl.program_id(0) == 0)
    def clear():
        gain_acc[...] = jnp.zeros_like(gain_acc)
        bias_acc[...] = jnp.zeros_like(bias_acc)

    cot_s[...] = cot[...].T
    turned[...] = cot_fm[...].T
    unroll = 8

    def some(k, carry):
        hats, gs = [], []
        for u in range(unroll):
            at = pl.ds(pl.multiple_of((k * unroll + u) * features, 32), features)
            g = cot_s[at, :].astype(f32)
            out_s[at, :], gmix[at, :], g_hat = norm_token(res[at, :].astype(f32), g, gain[...], bias[...])
            hats.append(g_hat)
            gs.append(g)
        gain_acc[...] += sum(hats)
        bias_acc[...] += sum(gs)
        return carry

    lax.fori_loop(0, res.shape[0] // features // unroll, some, 0)
    out[...] = out_s[...].T


def mlp_kernel(features, *refs):
    every, normed_hbm, res_hbm, cot_hbm, b_up, b_down, gain, bias = refs[:8]
    out, mix, hidden, g_pre, g_normed, gain_acc, bias_acc, up_acc, down_acc = refs[8:17]
    pre_s, out_s, up_s, down_s, up_w, down_w, normed, res, cot, arrive = refs[17:]
    step = pl.program_id(0)
    pairs, lanes = g_normed.shape
    units = hidden.shape[0]
    width = res.shape[0]
    unit_tile = 256
    token_tile = 4 * features
    bring_normed = pltpu.make_async_copy(normed_hbm, normed, arrive.at[0])
    bring_up = pltpu.make_async_copy(every.at[:, pl.ds(0, pairs)], up_w, arrive.at[1])
    bring_down = pltpu.make_async_copy(every.at[:, pl.ds(pairs, width)], down_w, arrive.at[2])
    blocks = normed.shape[1] // lanes

    def bring_block(i):
        here = pl.ds(pl.multiple_of(i * lanes, lanes), lanes)
        return [
            pltpu.make_async_copy(res_hbm.at[:, here], res.at[:, here], arrive.at[3 + i]),
            pltpu.make_async_copy(cot_hbm.at[:, here], cot.at[:, here], arrive.at[3 + blocks + i]),
        ]

    @pl.when(step == 0)
    def up():
        bring_normed.start()
        bring_up.start()
        bring_down.start()
        for i in range(blocks):
            for copy in bring_block(i):
                copy.start()
        for acc in (gain_acc, bias_acc, up_acc, down_acc):
            acc[...] = jnp.zeros_like(acc)
        up_s[...] = standing(b_up)
        down_s[...] = standing(b_down)
        bring_normed.wait()
        bring_up.wait()
        for at in range(0, units, unit_tile):
            here = slice(at, at + unit_tile)
            pre = mul(up_w[here, :], normed[...]) + doubled(up_s[here, :], normed.shape[1])
            pre_s[here, :] = pre
            hidden[here, :] = gelu(pre).astype(bf16)
        bring_down.wait()

    @pl.when(step > 0)
    def rest():
        now = pl.ds(pl.multiple_of((step - 1) * lanes, lanes), lanes)
        for copy in bring_block(step - 1):
            copy.wait()
        wide_gain, wide_bias = doubled(gain[...], lanes), doubled(bias[...], lanes)

        def fm_tile(first):
            return mul(down_w[:, first : first + token_tile], hidden[:, now], TN)

        ahead = fm_tile(0)
        for first in range(0, width, token_tile):
            tile = ahead
            if first + token_tile < width:
                ahead = fm_tile(first + token_tile)
            hats, gs = [], []
            for u in range(4):
                here = slice(first + u * features, first + (u + 1) * features)
                fm = tile[u * features : (u + 1) * features, :] + doubled(down_s[here, :], lanes)
                g = cot[here, now].astype(f32)
                summed = res[here, now].astype(f32) + fm.astype(bf16).astype(f32)
                out_s[here, :], g_mix, g_hat = norm_token(summed, g, wide_gain, wide_bias)
                mix[here, now] = g_mix
                down_acc[here, :] += folded(g_mix.astype(f32))
                hats.append(folded(g_hat))
                gs.append(folded(g))
            gain_acc[...] += sum(hats)
            bias_acc[...] += sum(gs)
        for at in range(0, units, unit_tile):
            here = slice(at, at + unit_tile)
            g_hidden = mul(down_w[here, :], mix[:, now])
            value = (g_hidden * gelu_slope(pre_s[here, now])).astype(bf16)
            g_pre[here, now] = value
            up_acc[here, :] += folded(value.astype(f32))
        g_normed[...] = mul(up_w[...], g_pre[:, now], TN)
        out[...] = out_s[...].T


def to_natural(mix, nat_s, features, block=0):
    count, examples, _ = nat_s.shape
    now = pl.ds(pl.multiple_of(block * examples, examples), examples)

    for t in range(count):
        nat_s[t, :, :features] = mix[t * features : (t + 1) * features, now].T


def natural_groups(nat_s, features):
    found = []
    for first in range(0, nat_s.shape[1], 2 * GROUP):
        mixes = nat_s[:, first : first + 2 * GROUP, :features].astype(f32)
        found += [mixes[:, :GROUP], mixes[:, GROUP:]]
    return [item.reshape(-1, features).astype(bf16) for item in found]


def early_kernel(gmix, xt, mixer, gt, mix_acc, nat_s):
    _, features, lanes = xt.shape
    groups = nat_s.shape[1] // GROUP
    base = pl.program_id(0) * groups
    rows = nat_s.shape[0] * GROUP
    own = slice(lanes - rows, lanes)

    @pl.when(pl.program_id(0) == 0)
    def clear():
        mix_acc[...] = jnp.zeros_like(mix_acc)

    to_natural(gmix, nat_s, features)

    total = mix_acc[...]
    for u, g_mix in enumerate(natural_groups(nat_s, features)):
        total = total + mul(g_mix, xt[u])
        gt[base + u] = mul(g_mix, mixer[own], TN).astype(bf16)
    mix_acc[...] = total


def back_kernel(start, gn, pair, gain, gmix, xt, mixer, early, *refs):
    *before, gt, gain_acc, bias_acc, mix_acc, project_acc, gp_s, nat_s = refs
    sums = (gain_acc, bias_acc, mix_acc, project_acc)
    _, features, lanes = xt.shape
    block = start + pl.program_id(0)
    groups = gp_s.shape[0] // GROUP
    base = block * groups
    tokens = lanes // GROUP
    ranks = gp_s.shape[1] // tokens
    per_tile = 128 // tokens
    rows = nat_s.shape[0] * GROUP

    @pl.when(pl.program_id(0) == 0)
    def clear():
        for i, acc in enumerate(sums):
            acc[...] = before[i][...] if before else jnp.zeros_like(acc)

    values = pair[...]
    centred = values - jnp.mean(values, axis=0, keepdims=True)
    scale = lax.rsqrt(jnp.mean(centred * centred, axis=0, keepdims=True) + EPS)
    hat = centred * scale
    g = gn[...]
    gain_acc[...] += g * hat
    bias_acc[...] += g
    h = g * gain[...]
    mean_h = jnp.mean(h, axis=0, keepdims=True)
    mean_hx = jnp.mean(h * hat, axis=0, keepdims=True)
    gp_s[...] = (scale * (h - mean_h - hat * mean_hx)).T
    to_natural(gmix, nat_s, features, block)
    example = lax.broadcasted_iota(jnp.int32, (GROUP, 128), 0)
    place = lax.broadcasted_iota(jnp.int32, (GROUP, 128), 1) // tokens
    own = place == example % per_tile
    keep_low = jnp.logical_and(own, example < per_tile)
    keep_high = jnp.logical_and(own, example >= per_tile)

    project = mixer[lanes:]
    stacked = xt[...].reshape(groups * features, lanes)
    projected = mul(stacked, project, NT).astype(bf16)
    g_pairs, g_parts = [], []
    for u in range(groups):
        here = slice(u * GROUP, (u + 1) * GROUP)
        slabs = []
        for j in range(ranks):
            c, s = j // per_tile, j % per_tile
            one = turn(gp_s[here, c * 128 : c * 128 + 128], -s * tokens)
            slabs.append(
                jnp.concatenate([jnp.where(keep_low, one, 0.0), jnp.where(keep_high, one, 0.0)], axis=1)
            )
        g_pairs.append(jnp.concatenate(slabs, axis=0).astype(bf16))
        g_parts.append(mul(xt[u], g_pairs[u], NT).astype(bf16))
    g_projected = jnp.concatenate(g_parts, axis=0)
    project_acc[...] += mul(stacked, g_projected, TN)
    shared = mul(g_projected, project)
    mix_total = mix_acc[...]
    for u, g_mix in enumerate(natural_groups(nat_s, features)):
        mix_total = mix_total + mul(g_mix, xt[u])
        mine = slice(u * features, (u + 1) * features)
        part = mul(projected[mine], g_pairs[u]) + mul(g_mix, mixer[:rows], TN) + shared[mine]
        gt[base + u] = (part + early[base + u].astype(f32)).astype(bf16)
    mix_acc[...] = mix_total


def spread_kernel(start, first_half, starts, ends, gt, out):
    step = start + pl.program_id(0)
    chunks = out.shape[1] // CHUNK
    last = starts.shape[0] - 1
    span = CHUNK // 128 + 1

    for c in range(chunks):
        number = step * chunks + c
        first = jnp.minimum(first_half[number], last + 1 - span)
        lows, highs, values = [], [], []
        for i in range(span):
            half = first + i
            lows.append(starts[pl.ds(half, 1), :])
            highs.append(ends[pl.ds(half, 1), :])
            values.append(gt[half // 2, :, pl.ds(pl.multiple_of(half % 2 * 128, 128), 128)])
        low = jnp.concatenate(lows, axis=1) - number * CHUNK
        high = jnp.concatenate(highs, axis=1) - number * CHUNK
        hot = one_hot(low, high, CHUNK)
        part = mul(jnp.concatenate(values, axis=1), hot, NT)
        out[:, c * CHUNK : (c + 1) * CHUNK] = part.astype(bf16)


def passing(kernel, given, previous):
    if not previous:
        return kernel, {}
    more = len(previous)
    skip = lambda *refs: kernel(*refs[:given], *refs[given + more :])
    return skip, {given + i: i for i in range(more)}


HBM, VMEM = pltpu.HBM, pltpu.VMEM
INSIDE = pl.BlockSpec(memory_space=pltpu.VMEM)


def held(*arrays):
    return [pltpu.with_memory_space_constraint(array, pltpu.VMEM) for array in arrays]


def away(*arrays):
    return [pltpu.with_memory_space_constraint(array, pltpu.HBM) for array in arrays]


def whole(shape):
    return pl.BlockSpec(shape, lambda *_: (0,) * len(shape))


def rank_of(tokens):
    per_tile = 128 // tokens
    slab, example = np.arange(per_tile)[:, None], np.arange(GROUP)[None, :]
    return np.eye(per_tile, dtype=np.float32)[(slab + example) % per_tile]


def make_mixer(w_res, w_comp, p_proj):
    tokens = w_res.shape[0]
    fm_tokens = tokens - w_comp.shape[0]
    mix = w_res.astype(f32) + jnp.pad(w_comp.astype(f32), ((fm_tokens, 0), (0, 0)))
    mix = jnp.broadcast_to(mix[:, None, :], (tokens, GROUP, tokens))
    by_tile = p_proj.T.astype(f32).reshape(-1, 128 // tokens, tokens)
    project = jnp.einsum("cqt,seq->cset", by_tile, rank_of(tokens))
    both = jnp.concatenate([mix, project.reshape(-1, GROUP, tokens)], axis=0)
    wide = both[:, :, None, :] * np.eye(GROUP, dtype=np.float32)[None, :, :, None]
    return wide.reshape(both.shape[0] * GROUP, GROUP * tokens).astype(bf16)


def token_stage(offs, starts, ends, rows, mixer, gain, bias, tokens, fm_tokens):
    features, row_total = rows.shape
    group_count, lanes = starts.shape
    examples = group_count * GROUP
    pairs = gain.shape[0]
    groups = BLOCK // GROUP
    return pl.pallas_call(
        tokens_kernel,
        name="tokens",
        grid_spec=pltpu.PrefetchScalarGridSpec(
            num_scalar_prefetch=1,
            grid=(examples // BLOCK,),
            in_specs=[
                pl.BlockSpec((groups, lanes), lambda i, _: (i, 0)),
                pl.BlockSpec((groups, lanes), lambda i, _: (i, 0)),
                pl.BlockSpec(memory_space=pltpu.VMEM),
                whole(mixer.shape),
                whole(gain.shape),
                whole(bias.shape),
            ],
            out_specs=[
                pl.BlockSpec((groups, features, lanes), lambda i, _: (i, 0, 0)),
                pl.BlockSpec((pairs, BLOCK), lambda i, _: (0, i)),
                pl.BlockSpec((pairs, BLOCK), lambda i, _: (0, i)),
                pl.BlockSpec((fm_tokens * features, BLOCK), lambda i, _: (0, i)),
                pl.BlockSpec(((tokens - fm_tokens) * features, BLOCK), lambda i, _: (0, i)),
            ],
            scratch_shapes=[
                pltpu.VMEM((BLOCK, pairs), f32),
                pltpu.VMEM((tokens, BLOCK, 256), f32),
                pltpu.VMEM((groups, features, lanes), f32),
            ],
        ),
        out_shape=[
            HBM((group_count, features, lanes), bf16),
            HBM((pairs, examples), f32),
            HBM((pairs, examples), bf16),
            HBM((fm_tokens * features, examples), bf16),
            HBM(((tokens - fm_tokens) * features, examples), bf16),
        ],
        compiler_params=params(36),
        cost_estimate=pl.CostEstimate(
            flops=2 * features * lanes * (row_total * 2 + 1000 * group_count),
            bytes_accessed=row_total * features * 2 + 30 * examples * 1024,
            transcendentals=0,
        ),
    )(offs, starts, ends, *away(rows), mixer, gain, bias)


def final_stage(res, cot, gain, bias, features):
    part, examples = res.shape
    width = cot.shape[1]
    tall = pl.BlockSpec((part, BLOCK), lambda i: (0, i))
    flat = pl.BlockSpec((BLOCK, part), lambda i: (i, 1))
    first = pl.BlockSpec((BLOCK, width - part), lambda i: (i, 0))
    turned = pl.BlockSpec((width - part, BLOCK), lambda i: (0, i))
    res, cot = away(res, cot)
    return pl.pallas_call(
        functools.partial(final_kernel, features),
        name="final_comp",
        grid=(examples // BLOCK,),
        in_specs=[tall, flat, first, whole(gain.shape), whole(bias.shape)],
        out_specs=[flat, tall, turned, whole((features, BLOCK)), whole((features, BLOCK))],
        out_shape=[
            HBM((examples, width), bf16),
            HBM((part, examples), bf16),
            HBM((width - part, examples), bf16),
            jax.ShapeDtypeStruct((features, BLOCK), f32),
            jax.ShapeDtypeStruct((features, BLOCK), f32),
        ],
        scratch_shapes=[pltpu.VMEM((part, BLOCK), bf16), pltpu.VMEM((part, BLOCK), bf16)],
        compiler_params=params(16),
        cost_estimate=pl.CostEstimate(
            flops=200 * part * examples, bytes_accessed=8 * part * examples, transcendentals=0
        ),
    )(res, cot, cot, gain, bias)


def mlp_stage(every, normed, res, cot, b_up, b_down, gain, bias, features, previous):
    units, columns = every.shape
    pairs, examples = normed.shape
    part = columns - pairs
    lanes = 2 * BLOCK
    block = lambda i: jnp.maximum(i - 1, 0)
    every, normed, res, cot, previous = away(every, normed, res, cot, previous)
    operands = (every, normed, res, cot, b_up, b_down, gain, bias)
    kernel, aliases = passing(functools.partial(mlp_kernel, features), len(operands), (previous,))
    return pl.pallas_call(
        kernel,
        name="mlp",
        grid=(1 + examples // lanes,),
        in_specs=[
            pl.BlockSpec(memory_space=pl.ANY),
            pl.BlockSpec(memory_space=pl.ANY),
            pl.BlockSpec(memory_space=pl.ANY),
            pl.BlockSpec(memory_space=pl.ANY),
            whole(b_up.shape),
            whole(b_down.shape),
            whole(gain.shape),
            whole(bias.shape),
            pl.BlockSpec(memory_space=pl.ANY),
        ],
        out_specs=[
            pl.BlockSpec((lanes, part), lambda i: (block(i), 0)),
            INSIDE,
            INSIDE,
            INSIDE,
            pl.BlockSpec((pairs, lanes), lambda i: (0, block(i))),
            whole((features, BLOCK)),
            whole((features, BLOCK)),
            whole((units, BLOCK)),
            whole((part, BLOCK)),
        ],
        out_shape=[
            HBM(previous.shape, bf16),
            VMEM((part, examples), bf16),
            VMEM((units, examples), bf16),
            VMEM((units, examples), bf16),
            HBM((pairs, examples), f32),
            jax.ShapeDtypeStruct((features, BLOCK), f32),
            jax.ShapeDtypeStruct((features, BLOCK), f32),
            jax.ShapeDtypeStruct((units, BLOCK), f32),
            jax.ShapeDtypeStruct((part, BLOCK), f32),
        ],
        scratch_shapes=[
            pltpu.VMEM((units, examples), f32),
            pltpu.VMEM((part, lanes), bf16),
            pltpu.VMEM((units, BLOCK), f32),
            pltpu.VMEM((part, BLOCK), f32),
            pltpu.VMEM((units, pairs), bf16),
            pltpu.VMEM((units, part), bf16),
            pltpu.VMEM((pairs, examples), bf16),
            pltpu.VMEM((part, examples), bf16),
            pltpu.VMEM((part, examples), bf16),
            pltpu.SemaphoreType.DMA((3 + 2 * (examples // lanes),)),
        ],
        input_output_aliases=aliases,
        compiler_params=params(43),
        cost_estimate=pl.CostEstimate(
            flops=4 * units * columns * examples,
            bytes_accessed=2 * units * columns + 10 * part * examples,
            transcendentals=2 * units * examples,
        ),
    )(*operands, previous)


def early_stage(gmix, xt, mixer):
    group_count, features, lanes = xt.shape
    part, examples = gmix.shape
    count = part // features
    return pl.pallas_call(
        early_kernel,
        name="early",
        grid=(examples // BLOCK,),
        in_specs=[
            pl.BlockSpec((part, BLOCK), lambda i: (0, i)),
            pl.BlockSpec((BLOCK // GROUP, features, lanes), lambda i: (i, 0, 0)),
            whole(mixer.shape),
        ],
        out_specs=[INSIDE, whole((count * GROUP, lanes))],
        out_shape=[
            VMEM((group_count, features, lanes), bf16),
            jax.ShapeDtypeStruct((count * GROUP, lanes), f32),
        ],
        scratch_shapes=[pltpu.VMEM((count, BLOCK, 256), bf16)],
        compiler_params=params(16),
        cost_estimate=pl.CostEstimate(
            flops=2 * features * lanes * 500 * group_count,
            bytes_accessed=group_count * features * lanes * 8,
            transcendentals=0,
        ),
    )(*away(gmix, xt), mixer)


def back_stage(gn, pair, gain, gmix, xt, mixer, gt, start, count, before):
    pairs, examples = pair.shape
    group_count, features, lanes = xt.shape
    ranked = mixer.shape[0] - lanes
    fm_tokens = gmix.shape[0] // features
    wide = pl.BlockSpec((pairs, BLOCK), lambda i: (0, start + i))
    sums = [(pairs, BLOCK), (pairs, BLOCK), (fm_tokens * GROUP, lanes), (lanes, ranked)]
    gn, pair, xt = away(gn, pair, xt)
    gmix, gt = held(gmix, gt)
    by_group = pl.BlockSpec((BLOCK // GROUP, features, lanes), lambda i: (start + i, 0, 0))
    operands = (gn, pair, gain, gmix, xt, mixer, gt, *before)
    return pl.pallas_call(
        functools.partial(back_kernel, start),
        name="back",
        grid=(count,),
        in_specs=[wide, wide, whole(gain.shape), INSIDE, by_group, whole(mixer.shape), INSIDE]
        + [whole(item.shape) for item in before],
        out_specs=[INSIDE] + [whole(shape) for shape in sums],
        out_shape=[VMEM((group_count, features, lanes), bf16)]
        + [jax.ShapeDtypeStruct(shape, f32) for shape in sums],
        scratch_shapes=[
            pltpu.VMEM((BLOCK, pairs), f32),
            pltpu.VMEM((fm_tokens, BLOCK, 256), bf16),
        ],
        input_output_aliases={6: 0},
        compiler_params=params(20),
        cost_estimate=pl.CostEstimate(
            flops=2 * features * lanes * 1400 * BLOCK // GROUP * count,
            bytes_accessed=40 * BLOCK * count * 1024,
            transcendentals=0,
        ),
    )(*operands)


def exact(value, selector, dims=NN):
    total = None
    for _ in range(3):
        piece = value.astype(bf16)
        value = value - piece.astype(f32)
        total = mul(piece, selector, dims) if total is None else total + mul(piece, selector, dims)
    return total


def ones_where(condition):
    return jnp.where(condition, 1.0, 0.0).astype(bf16)


def by_token_order(pairs, tokens):
    ranks = pairs // tokens
    row = lax.broadcasted_iota(jnp.int32, (pairs, pairs), 0)
    lane = lax.broadcasted_iota(jnp.int32, (pairs, pairs), 1)
    return ones_where((row % tokens) * ranks + row // tokens == lane)


def small_rows(tokens, pairs, units, width, features):
    counts = [tokens, pairs // 128, pairs // 128, units // 128, width // 128, -(-features // 128)]
    counts.append(counts[-1])
    starts = np.cumsum([0] + counts)
    return [(int(start), count) for start, count in zip(starts, counts)], -(-int(starts[-1]) // 8) * 8


def small_kernel(tokens, places, gain_acc, bias_acc, mix_fm, mix_comp, project, up, down, gains, biases, out):
    def put(place, row):
        start, count = place
        for i in range(count):
            piece = row[:, i * 128 : i * 128 + 128]
            out[start + i : start + i + 1, : piece.shape[1]] = piece

    def lying(column):
        return jnp.sum(column.T, axis=0, keepdims=True)

    out[...] = jnp.zeros_like(out)
    lanes = mix_fm.shape[1]
    ranked = project.shape[1]
    per_tile = 128 // tokens
    mix = jnp.concatenate([mix_fm[...], mix_comp[...]], axis=0)
    row = lax.broadcasted_iota(jnp.int32, mix.shape, 0) % GROUP
    lane = lax.broadcasted_iota(jnp.int32, mix.shape, 1) // tokens
    mix = jnp.where(row == lane, mix, 0.0)
    fold = ones_where(
        lax.broadcasted_iota(jnp.int32, (lanes, tokens), 0) % tokens
        == lax.broadcasted_iota(jnp.int32, (lanes, tokens), 1)
    )
    folded_mix = exact(mix, fold).reshape(tokens, GROUP, tokens)
    row = lax.broadcasted_iota(jnp.int32, project.shape, 0) // tokens
    lane = lax.broadcasted_iota(jnp.int32, project.shape, 1) % GROUP
    cells = jnp.where(row == lane, project[...], 0.0).reshape(GROUP, tokens, ranked)
    cells = jnp.sum(cells, axis=0)
    ranks = ranked // GROUP
    row = lax.broadcasted_iota(jnp.int32, (ranks, ranked), 0)
    lane = lax.broadcasted_iota(jnp.int32, (ranks, ranked), 1)
    slab = lane // GROUP
    rank = slab // per_tile * per_tile + (lane % GROUP + slab % per_tile) % per_tile
    pick = ones_where(row == rank)
    projected = None
    for _ in range(3):
        piece = cells.astype(bf16)
        cells = cells - piece.astype(f32)
        part = mul(pick, piece, NT)
        projected = part if projected is None else projected + part
    out[:ranks, :tokens] = projected
    out[:tokens, tokens : 2 * tokens] = jnp.sum(folded_mix, axis=1)
    both = jnp.concatenate([lying(gain_acc[...]), lying(bias_acc[...])], axis=0)
    both = exact(both, by_token_order(both.shape[1], tokens))
    put(places[1], both[:1])
    put(places[2], both[1:])
    put(places[3], lying(up[...]))
    put(places[4], lying(down[...]))
    put(places[5], lying(gains[0] + gains[1]))
    put(places[6], lying(biases[0] + biases[1]))


def small_stage(tokens, places, rows, gain_acc, bias_acc, mix_fm, mix_comp, project, up, down, gains, biases):
    def kernel(*refs):
        *given, gain_0, gain_1, bias_0, bias_1, out = refs
        small_kernel(tokens, places, *given, (gain_0[...], gain_1[...]), (bias_0[...], bias_1[...]), out)

    operands = (gain_acc, bias_acc, mix_fm, mix_comp, project, up, down, *gains, *biases)
    return pl.pallas_call(
        kernel,
        name="small",
        out_shape=jax.ShapeDtypeStruct((rows, 128), f32),
        compiler_params=params(16),
        cost_estimate=pl.CostEstimate(flops=10**9, bytes_accessed=4 * 10**6, transcendentals=0),
    )(*operands)


def last_kernel(tokens, places, total, more, *refs):
    *vectors, up, down, p_proj, w_res, w_comp, gain_one, bias_one, b_up, b_down, gain_two, bias_two = refs
    pairs = up.shape[1]
    value = total[...] + more[...].astype(f32)
    down[...] = value[:, pairs:]
    up[...] = exact(value[:, :pairs], by_token_order(pairs, tokens))
    vector = sum([ref[...] for ref in vectors])
    p_proj[...] = vector[: p_proj.shape[0], :tokens]
    w_res[...] = vector[:tokens, tokens : 2 * tokens]
    w_comp[...] = vector[tokens - w_comp.shape[0] : tokens, tokens : 2 * tokens]
    rest = (gain_one, bias_one, b_up, b_down, gain_two, bias_two)
    for (start, count), ref in zip(places[1:], rest):
        if ref.shape[0] == 1:
            row = [vector[start + i : start + i + 1] for i in range(count)]
            ref[...] = jnp.concatenate(row, axis=1)[:, : ref.shape[1]]
        else:
            ref[...] = vector[start : start + count]


def last_stage(total, more, vectors, places, pairs, tokens, features, comp_tokens):
    rows, columns = total.shape
    shapes = [(rows, pairs), (rows, columns - pairs), (pairs // tokens, tokens), (tokens, tokens), (comp_tokens, tokens)]
    shapes += [(count, 128) for _, count in places[1:-2]] + [(1, features)] * 2
    return pl.pallas_call(
        functools.partial(last_kernel, tokens, places),
        name="last",
        out_shape=[jax.ShapeDtypeStruct(shape, f32) for shape in shapes],
        compiler_params=params(16),
        cost_estimate=pl.CostEstimate(
            flops=6 * rows * pairs * pairs, bytes_accessed=10 * rows * columns, transcendentals=0
        ),
    )(total, more, *vectors)


def grad_kernel(rows, parts, table, pre, hidden, normed, mix, *refs):
    *outs, picked_s, out_s, leave = refs
    pairs = normed.shape[0]
    part = mix.shape[0] // parts

    def picked(source):
        for i in range(picked_s.shape[0] // rows):
            start = pl.multiple_of(table[i] * rows, rows)
            picked_s[i * rows : (i + 1) * rows, :] = source[pl.ds(start, rows), :]
        return picked_s[...]

    def copies(at, size, number):
        here = pl.ds(at, size)
        first = 0
        found = []
        for i, out in enumerate(outs):
            source = out_s.at[pl.ds(first, out.shape[0]), here]
            found.append(pltpu.make_async_copy(source, out.at[:, here], leave.at[number, i]))
            first += out.shape[0]
        return found

    def place(i):
        return pl.multiple_of(pairs + i * part, 128)

    picked(hidden)

    def down(i, carry):
        here = pl.ds(pl.multiple_of(i * part, 128), part)
        out_s[:, pl.ds(place(i), part)] = mul(picked_s[...], mix[here, :], NT).astype(bf16)
        for copy in copies(place(i), part, i):
            copy.start()
        return carry

    lax.fori_loop(0, parts, down, 0)
    out_s[:, :pairs] = mul(picked(pre), normed[...], NT).astype(bf16)
    last = copies(0, pairs, parts)
    for copy in last:
        copy.start()

    def end(i, carry):
        for copy in copies(place(i), part, i):
            copy.wait()
        return carry

    lax.fori_loop(0, parts, end, 0)
    for copy in last:
        copy.wait()


def grad_stage(tables, pre, hidden, normed, mix, rows):
    units, examples = hidden.shape
    pairs = normed.shape[0]
    columns = pairs + mix.shape[0]
    counts = [table.shape[0] * rows for table in tables]
    count = sum(counts)
    parts = 4
    anywhere = pl.BlockSpec(memory_space=pl.ANY)
    pre, hidden, normed, mix = held(pre, hidden, normed, mix)
    return pl.pallas_call(
        functools.partial(grad_kernel, rows, parts),
        name="weight_grads",
        grid_spec=pltpu.PrefetchScalarGridSpec(
            num_scalar_prefetch=1,
            grid=(1,),
            in_specs=[INSIDE] * 4,
            out_specs=[anywhere] * len(counts),
            scratch_shapes=[
                pltpu.VMEM((count, examples), bf16),
                pltpu.VMEM((count, columns), bf16),
                pltpu.SemaphoreType.DMA((1 + parts, len(counts))),
            ],
        ),
        out_shape=[HBM((size, columns), bf16) for size in counts],
        compiler_params=params(16),
        cost_estimate=pl.CostEstimate(
            flops=2 * count * examples * columns,
            bytes_accessed=2 * count * columns + 2 * examples * (2 * units + columns),
            transcendentals=0,
        ),
    )(jnp.concatenate(tables), pre, hidden, normed, mix)


def spread_stage(first_half, starts, ends, gt, row_total, start, count, previous):
    group_count, features, lanes = gt.shape
    operands = (starts.reshape(-1, 128), ends.reshape(-1, 128), *held(gt))
    previous = away(*previous)
    kernel, aliases = passing(functools.partial(spread_kernel, start), len(operands) + 1, previous)
    return pl.pallas_call(
        kernel,
        name="spread",
        grid_spec=pltpu.PrefetchScalarGridSpec(
            num_scalar_prefetch=1,
            grid=(count,),
            in_specs=[whole(operands[0].shape), whole(operands[1].shape), INSIDE]
            + [pl.BlockSpec(memory_space=pl.ANY)] * len(previous),
            out_specs=pl.BlockSpec((features, SPREAD_ROWS), lambda i, _: (0, start + i)),
        ),
        out_shape=HBM((features, row_total), bf16),
        input_output_aliases=aliases,
        compiler_params=params(16),
        cost_estimate=pl.CostEstimate(
            flops=4 * features * lanes * SPREAD_ROWS * count,
            bytes_accessed=SPREAD_ROWS * count * features * 4,
            transcendentals=0,
        ),
    )(first_half, *operands, *previous)


def bag_bounds(lengths):
    ends = jnp.cumsum(lengths.reshape(-1))
    starts = ends - lengths.reshape(-1)
    return starts, ends


def column(vector, lanes=BLOCK):
    return jnp.broadcast_to(vector[:, None], (vector.shape[0], lanes))


def gelu(v):
    inner = np.sqrt(2 / np.pi).astype(np.float32) * (v + 0.044715 * (v * v * v))
    return 0.5 * v * (1.0 + jnp.tanh(inner))


def gelu_slope(v):
    root = np.sqrt(2 / np.pi).astype(np.float32)
    bent = jnp.tanh(root * (v + 0.044715 * (v * v * v)))
    return 0.5 * (1.0 + bent) + 0.5 * v * (1.0 - bent * bent) * root * (1.0 + 3 * 0.044715 * (v * v))


def shards(
    embed_rows,
    lengths,
    cotangent,
    p_proj,
    gain_one,
    bias_one,
    w_up,
    b_up,
    w_down,
    b_down,
    w_comp,
    w_res,
    gain_two,
    bias_two,
):
    links = Links()
    tokens = w_res.shape[0]
    features = embed_rows.shape[1]
    ranks = p_proj.shape[1]
    pairs = tokens * ranks
    row_total = embed_rows.shape[0]
    fm_width = b_down.shape[0]
    examples = cotangent.shape[0]

    def by_rank(vector):
        return jnp.swapaxes(vector.reshape(-1, tokens, ranks), 1, 2).reshape(vector.shape)

    def by_token(vector):
        return jnp.swapaxes(vector.reshape(-1, ranks, tokens), 1, 2).reshape(vector.shape)

    every = links.gather(jnp.concatenate([by_rank(w_up.T), w_down], axis=1))

    starts, ends = bag_bounds(lengths)
    lanes = GROUP * tokens
    starts = starts.reshape(-1, lanes)
    ends = ends.reshape(-1, lanes)
    offs = jnp.concatenate([starts[:, 0], ends[-1:, -1]])
    bases = jnp.arange(row_total // CHUNK, dtype=jnp.int32) * CHUNK
    half_ends = ends.reshape(-1, 128)[:, 127]
    first_half = jnp.sum((half_ends[None, :] <= bases[:, None]).astype(jnp.int32), axis=1)
    mixer = make_mixer(w_res, w_comp, p_proj)
    gain_a, bias_a = column(by_rank(gain_one)), column(by_rank(bias_one))
    gain_b, bias_b = column(gain_two), column(bias_two)
    down_bias = column(b_down)

    xt, pair, normed, res, res_comp = token_stage(
        offs, starts, ends, embed_rows.T, mixer, gain_a, bias_a, tokens, fm_width // features
    )
    out, mix_comp, cot, gain_acc1, bias_acc1 = final_stage(res_comp, cotangent, gain_b, bias_b, features)
    mix_comp, first_half = lax.optimization_barrier((mix_comp, first_half))
    gt, mix_acc1 = early_stage(mix_comp, xt, mixer)
    gt, normed = lax.optimization_barrier((gt, normed))
    out, mix, hidden, g_pre, g_normed, gain_acc0, bias_acc0, up_acc, down_acc = mlp_stage(
        every, normed, res, cot, b_up[None, :], b_down[None, :], gain_b, bias_b, features, out
    )

    unit_rows = links.unit_rows(w_down.shape[0])
    tables, rows, (g_pre, hidden) = links.shards(unit_rows, g_pre, hidden)
    ring = links.ring(unit_rows)
    gradients = lambda *tables: grad_stage(tables, g_pre, hidden, normed, mix, rows)
    sent_first, sent = gradients(tables[0], tables[2])
    crossing_first = links.to_other_core(sent_first)
    crossing = links.to_other_core(sent)
    g_pre, hidden, sent = lax.optimization_barrier((g_pre, hidden, sent))
    (mine,) = gradients(tables[1])
    ring.add(*lax.optimization_barrier((mine, crossing_first)))
    g_pre, hidden = ring.start((g_pre, hidden))
    (mine,) = gradients(tables[3])
    mine, g_normed, gt = ring.finish((mine, g_normed, gt))
    ring.add(*lax.optimization_barrier((mine, crossing)))

    blocks = examples // BLOCK
    cuts = [blocks * i // 2 for i in range(3)]
    sums = []
    for i in range(2):
        g_normed, gt, sums = ring.start((g_normed, gt, sums))
        gt, *sums = back_stage(
            g_normed, pair, gain_a, mix, xt, mixer, gt, cuts[i], cuts[i + 1] - cuts[i], sums
        )
        g_normed, gt, sums = ring.finish((g_normed, gt, sums))
    gain_acc, bias_acc, mix_acc0, project_acc = sums
    places, rows = small_rows(tokens, pairs, b_up.shape[0], fm_width, features)
    vector = small_stage(
        tokens,
        places,
        rows,
        gain_acc,
        bias_acc,
        mix_acc0,
        mix_acc1,
        project_acc,
        up_acc,
        down_acc,
        (gain_acc0, gain_acc1),
        (bias_acc0, bias_acc1),
    )

    steps = row_total // SPREAD_ROWS
    swaps = links.rounds()
    cuts = [0, steps * 4 // 9, steps * 6 // 9, steps]
    rows_grad = ()
    for i in range(3):
        if i < 2:
            vector, gt, rows_grad = ring.start((vector, gt, rows_grad))
        far = [swap(vector) for swap in swaps[i]]
        rows_grad = spread_stage(
            first_half, starts, ends, gt, row_total, cuts[i], cuts[i + 1] - cuts[i], rows_grad
        )
        far, gt, rows_grad = lax.optimization_barrier((far, gt, (rows_grad,)))
        vector = sum(far, vector)
        if i != 1:
            vector, gt, rows_grad = ring.finish((vector, gt, rows_grad))
    for some in swaps[3:]:
        vector = sum([swap(vector) for swap in some], vector)
    vectors = [vector]
    up_grad, down_grad, proj_grad, res_grad, comp_grad, *rest = last_stage(
        *ring.end(), vectors, places, pairs, tokens, features, w_comp.shape[0]
    )
    rest = [item.reshape(-1) for item in rest]
    return (
        out,
        rows_grad[0].T,
        proj_grad.T,
        rest[0],
        rest[1],
        up_grad.T,
        rest[2],
        down_grad,
        rest[3],
        comp_grad,
        res_grad,
        rest[4],
        rest[5],
    )


def ring_order(chips):
    return list(range(0, chips, 2)) + list(range(chips - 1, 0, -2))


def added(*terms):
    return sum([term.astype(f32) for term in terms[1:]], terms[0].astype(f32))


def ring_shards(chips):
    order = ring_order(chips)
    reach = chips // 2
    steps = [reach]
    for distance in range(reach - 1, 0, -1):
        steps += [distance, -distance]
    steps.append(0)
    return [[order[(order.index(chip) + step) % chips] for step in steps] for chip in range(chips)]


class Ring:
    def __init__(self, rows):
        self.rows = rows
        self.chips = lax.axis_size("dp") // 2
        self.order = ring_order(self.chips)
        self.reach = self.chips // 2
        self.shards = []
        self.left = self.reach
        self.flying = None
        self.send = None
        self.total = None

    def add(self, *terms):
        terms = [term.reshape(-1, self.rows, term.shape[-1]) for term in terms]
        self.shards += [[term[i] for term in terms] for i in range(terms[0].shape[0])]

    def ahead(self, distance):
        return self.shards[1 + 2 * (self.reach - 1 - distance)]

    def behind(self, distance):
        return self.shards[2 + 2 * (self.reach - 1 - distance)]

    def along(self, value, step):
        order, chips = self.order, self.chips
        pairs = [
            (2 * order[i] + core, 2 * order[(i + step) % chips] + core)
            for i in range(chips)
            for core in range(2)
        ]
        return lax.ppermute(value, "dp", pairs)

    def start(self, others):
        if self.left < 0:
            return others
        if self.send is None:
            middle = added(*self.shards[0]).astype(bf16)
            rows = middle.shape[0] // 2
            self.send = [middle[:rows], middle[rows:]]
        self.send, others = lax.optimization_barrier((self.send, others))
        if self.left > 0:
            self.flying = (self.along(self.send[0], 1), self.along(self.send[1], -1))
        else:
            pairs = [(i, i ^ 1) for i in range(lax.axis_size("branch"))]
            self.flying = (lax.ppermute(self.send[0], "branch", pairs),)
        return others

    def finish(self, others):
        if self.flying is None:
            return others
        arrived, others = lax.optimization_barrier((self.flying, others))
        self.flying = None
        self.left -= 1
        if self.left < 0:
            self.more = arrived[0]
        elif self.left == 0:
            self.total = added(*self.shards[-1], *arrived)
            self.send = [self.total.astype(bf16)]
        else:
            one, two = added(*self.ahead(self.left)), added(*self.behind(self.left))
            first, second = arrived[0].astype(f32), arrived[1].astype(f32)
            if self.left == self.reach - 1:
                rows = first.shape[0]
                first = jnp.pad(first, ((0, one.shape[0] - rows), (0, 0)))
                second = jnp.pad(second, ((two.shape[0] - rows, 0), (0, 0)))
            self.send = [(one + first).astype(bf16), (two + second).astype(bf16)]
        return others

    def end(self):
        while self.left >= 0:
            self.start(())
            self.finish(())
        return self.total, self.more


class Links:
    def swaps(self, bits):
        dp, branch = lax.axis_size("dp"), lax.axis_size("branch")
        found = []
        for chosen in range(1, 1 << len(bits)):
            flip = functools.reduce(lambda a, b: a | b, [bit for i, bit in enumerate(bits) if chosen >> i & 1])
            pairs = [(i, i ^ flip) for i in range(dp * branch)]
            found.append(lambda value, pairs=pairs: lax.ppermute(value, ("dp", "branch"), pairs))
        return found

    def rounds(self):
        size = lax.axis_size("dp") * lax.axis_size("branch")
        bits = [1 << i for i in range(size.bit_length() - 1)]
        return [self.swaps(bits[i : i + 2]) for i in range(0, len(bits), 2)]

    def gather(self, own):
        return lax.all_gather(own, "dp", axis=0, tiled=True)

    def unit_rows(self, rows):
        return rows

    def owners(self):
        owners = np.asarray(ring_shards(lax.axis_size("dp") // 2), np.int32)
        table = np.stack([2 * owners + 1, 2 * owners, 2 * owners, 2 * owners + 1], axis=1)
        table = table.reshape(-1, 2 * owners.shape[1])
        return lax.dynamic_index_in_dim(jnp.asarray(table), lax.axis_index("dp"), 0, keepdims=False)

    def shards(self, rows, *units):
        table = self.owners()
        first = 3
        if rows % 16 != 0:
            units = [item.reshape(table.shape[0], rows, -1)[table].reshape(item.shape) for item in units]
            table = jnp.arange(units[0].shape[0] // 96, dtype=jnp.int32)
            rows, first = 96, 1
        half = table.shape[0] // 2
        cuts = [(0, first), (half, half + first), (first, half), (half + first, 2 * half)]
        return [table[a:b] for a, b in cuts], rows, units

    def to_other_core(self, value):
        return lax.ppermute(value, "dp", [(i, i ^ 1) for i in range(lax.axis_size("dp"))])

    def ring(self, rows):
        return Ring(rows)


def solution(mesh):
    spread = P(("dp", "branch"), None)
    in_specs = (
        spread,
        spread,
        spread,
        P(),
        P(),
        P(),
        P(None, "dp"),
        P(),
        P("dp", None),
        P(),
        P(),
        P(),
        P(),
        P(),
    )
    out_specs = (
        spread,
        spread,
        P(),
        P(),
        P(),
        P(None, "dp"),
        P(),
        P("dp", None),
        P(),
        P(),
        P(),
        P(),
        P(),
    )
    return jax.shard_map(shards, mesh=mesh, in_specs=in_specs, out_specs=out_specs, check_vma=False)
```

```python
import functools

import jax
import jax.numpy as jnp
import numpy as np
from jax import lax
from jax.experimental import pallas as pl
from jax.experimental.pallas import tpu as pltpu
from jax.sharding import PartitionSpec as P

EPS = 1e-05
GROUP = 8
BLOCK = 128
CHUNK = 256
SPREAD_ROWS = 16 * CHUNK

f32 = jnp.float32
bf16 = jnp.bfloat16

NN = (((1,), (0,)), ((), ()))
NT = (((1,), (1,)), ((), ()))
TN = (((0,), (0,)), ((), ()))


def mul(left, right, dims=NN):
    return lax.dot_general(left, right, dims, preferred_element_type=f32)


def params(mebibytes):
    return pltpu.CompilerParams(vmem_limit_bytes=mebibytes * 1024 * 1024)


def one_hot(low, high, rows):
    row = lax.broadcasted_iota(jnp.int16, (rows, low.shape[1]), 0)
    inside = jnp.logical_and(row >= low.astype(jnp.int16), row < high.astype(jnp.int16))
    return jnp.where(inside, jnp.ones((), bf16), jnp.zeros((), bf16))


def turn(tile, shift):
    return pltpu.roll(tile, shift % 128, 1) if shift % 128 else tile


def tokens_kernel(
    offs, starts, ends, rows, mixer, gain, bias, xt_ref, pair_ref, normed_ref, fm_ref, comp_ref, pair_s, nat_s, sum_s
):
    step = pl.program_id(0)
    groups = pair_s.shape[0] // GROUP
    row_total = rows.shape[1]
    features = rows.shape[0]
    tokens = nat_s.shape[0]
    ranks = pair_s.shape[1] // tokens
    lanes = tokens * GROUP
    per_tile = 128 // tokens
    span = 2 * CHUNK
    example = lax.broadcasted_iota(jnp.int32, (GROUP, 128), 0)
    place = lax.broadcasted_iota(jnp.int32, (GROUP, 128), 1) // tokens

    def all_groups():
        todo = range(groups)
        bases = []
        for u, i in enumerate(todo):
            first = offs[step * groups + i]
            base = (first // 128) * 128
            bases.append(base)
            low = starts[i : i + 1, :]
            high = ends[i : i + 1, :]
            at = pl.multiple_of(jnp.minimum(base, row_total - span), 128)
            sum_s[u] = mul(rows[:, pl.ds(at, span)], one_hot(low - at, high - at, span))
        for u, i in enumerate(todo):
            base = bases[u] + span
            left = offs[step * groups + i + 1] - base

            @pl.when(left > 0)
            def more(u=u, i=i, base=base, left=left):
                low = starts[i : i + 1, :]
                high = ends[i : i + 1, :]

                def chunk(c, total):
                    wanted = base + c * CHUNK
                    at = pl.multiple_of(jnp.minimum(wanted, row_total - CHUNK), 128)
                    hot = one_hot(jnp.maximum(low, wanted) - at, high - at, CHUNK)
                    return total + mul(rows[:, pl.ds(at, CHUNK)], hot)

                sum_s[u] = lax.fori_loop(0, (left + CHUNK - 1) // CHUNK, chunk, sum_s[u])

        for u, i in enumerate(todo):
            x = sum_s[u].astype(bf16)
            xt_ref[i] = x
            nat = mul(mixer[...], x, NT)
            m = mul(nat[lanes:].astype(bf16), x)
            here = slice(i * GROUP, (i + 1) * GROUP)
            for c in range(ranks // per_tile):
                tile = None
                for s in range(per_tile):
                    at = GROUP * (c * per_tile + s)
                    slab = m[at : at + GROUP]
                    one = jnp.where(example < per_tile, slab[:, :128], slab[:, 128:])
                    one = turn(one, s * tokens)
                    mine = place == (example + s) % per_tile
                    tile = one if s == 0 else jnp.where(mine, one, tile)
                pair_s[here, c * 128 : c * 128 + 128] = tile
            for t in range(tokens):
                nat_s[t, here, :features] = nat[GROUP * t : GROUP * t + GROUP]

    all_groups()
    pair = pair_s[...].T
    pair_ref[...] = pair
    centred = pair - jnp.mean(pair, axis=0, keepdims=True)
    scale = lax.rsqrt(jnp.mean(centred * centred, axis=0, keepdims=True) + EPS)
    normed_ref[...] = (centred * scale * gain[...] + bias[...]).astype(bf16)

    fm_tokens = fm_ref.shape[0] // features
    for t in range(tokens):
        turned = nat_s[t].astype(bf16).T[:features]
        if t < fm_tokens:
            fm_ref[t * features : (t + 1) * features, :] = turned
        else:
            comp_ref[(t - fm_tokens) * features : (t - fm_tokens + 1) * features, :] = turned


def norm_token(summed, g, gain, bias):
    centred = summed - jnp.mean(summed, axis=0, keepdims=True)
    scale = lax.rsqrt(jnp.mean(centred * centred, axis=0, keepdims=True) + EPS)
    hat = centred * scale
    q = g * gain
    g_hat = g * hat
    mean_q = jnp.mean(q, axis=0, keepdims=True)
    mean_qx = jnp.mean(q * hat, axis=0, keepdims=True)
    return (hat * gain + bias).astype(bf16), (scale * (q - mean_q - hat * mean_qx)).astype(bf16), g_hat


def standing(row):
    return jnp.broadcast_to(row[...], (128, row.shape[1])).T


def folded(value):
    return sum(value[:, i : i + 128] for i in range(0, value.shape[1], 128))


def doubled(value, lanes):
    return jnp.concatenate([value] * (lanes // value.shape[1]), axis=1)


def final_kernel(features, res, cot, cot_fm, gain, bias, out, gmix, turned, gain_acc, bias_acc, cot_s, out_s):
    @pl.when(pl.program_id(0) == 0)
    def clear():
        gain_acc[...] = jnp.zeros_like(gain_acc)
        bias_acc[...] = jnp.zeros_like(bias_acc)

    cot_s[...] = cot[...].T
    turned[...] = cot_fm[...].T
    unroll = 4

    def some(k, carry):
        hats, gs = [], []
        for u in range(unroll):
            at = pl.ds(pl.multiple_of((k * unroll + u) * features, 32), features)
            g = cot_s[at, :].astype(f32)
            out_s[at, :], gmix[at, :], g_hat = norm_token(res[at, :].astype(f32), g, gain[...], bias[...])
            hats.append(g_hat)
            gs.append(g)
        gain_acc[...] += sum(hats)
        bias_acc[...] += sum(gs)
        return carry

    lax.fori_loop(0, res.shape[0] // features // unroll, some, 0)
    out[...] = out_s[...].T


def mlp_kernel(features, *refs):
    every, normed_hbm, res_hbm, cot_hbm, b_up, b_down, gain, bias = refs[:8]
    out, mix, hidden, g_pre, g_normed, gain_acc, bias_acc, up_acc, down_acc = refs[8:17]
    pre_s, out_s, up_s, down_s, up_w, down_w, normed, res, cot, arrive = refs[17:]
    step = pl.program_id(0)
    pairs, lanes = g_normed.shape
    units = hidden.shape[0]
    width = res.shape[0]
    unit_tile = 256
    token_tile = 4 * features
    bring_normed = pltpu.make_async_copy(normed_hbm, normed, arrive.at[0])
    bring_up = pltpu.make_async_copy(every.at[:, pl.ds(0, pairs)], up_w, arrive.at[1])
    bring_down = pltpu.make_async_copy(every.at[:, pl.ds(pairs, width)], down_w, arrive.at[2])
    blocks = normed.shape[1] // lanes

    def bring_block(i):
        here = pl.ds(pl.multiple_of(i * lanes, lanes), lanes)
        return [
            pltpu.make_async_copy(res_hbm.at[:, here], res.at[:, here], arrive.at[3 + i]),
            pltpu.make_async_copy(cot_hbm.at[:, here], cot.at[:, here], arrive.at[3 + blocks + i]),
        ]

    @pl.when(step == 0)
    def up():
        bring_normed.start()
        bring_up.start()
        bring_down.start()
        for i in range(blocks):
            for copy in bring_block(i):
                copy.start()
        for acc in (gain_acc, bias_acc, up_acc, down_acc):
            acc[...] = jnp.zeros_like(acc)
        up_s[...] = standing(b_up)
        down_s[...] = standing(b_down)
        bring_normed.wait()
        bring_up.wait()
        for at in range(0, units, unit_tile):
            here = slice(at, at + unit_tile)
            pre = mul(up_w[here, :], normed[...]) + doubled(up_s[here, :], normed.shape[1])
            pre_s[here, :] = pre
            hidden[here, :] = gelu(pre).astype(bf16)
        bring_down.wait()

    @pl.when(step > 0)
    def rest():
        now = pl.ds(pl.multiple_of((step - 1) * lanes, lanes), lanes)
        for copy in bring_block(step - 1):
            copy.wait()
        wide_gain, wide_bias = doubled(gain[...], lanes), doubled(bias[...], lanes)

        def fm_tile(first):
            return mul(down_w[:, first : first + token_tile], hidden[:, now], TN)

        ahead = fm_tile(0)
        for first in range(0, width, token_tile):
            tile = ahead
            if first + token_tile < width:
                ahead = fm_tile(first + token_tile)
            hats, gs = [], []
            for u in range(4):
                here = slice(first + u * features, first + (u + 1) * features)
                fm = tile[u * features : (u + 1) * features, :] + doubled(down_s[here, :], lanes)
                g = cot[here, now].astype(f32)
                summed = res[here, now].astype(f32) + fm.astype(bf16).astype(f32)
                out_s[here, :], g_mix, g_hat = norm_token(summed, g, wide_gain, wide_bias)
                mix[here, now] = g_mix
                down_acc[here, :] += folded(g_mix.astype(f32))
                hats.append(folded(g_hat))
                gs.append(folded(g))
            gain_acc[...] += sum(hats)
            bias_acc[...] += sum(gs)
        for at in range(0, units, unit_tile):
            here = slice(at, at + unit_tile)
            g_hidden = mul(down_w[here, :], mix[:, now])
            value = (g_hidden * gelu_slope(pre_s[here, now])).astype(bf16)
            g_pre[here, now] = value
            up_acc[here, :] += folded(value.astype(f32))
        g_normed[...] = mul(up_w[...], g_pre[:, now], TN)
        out[...] = out_s[...].T


def to_natural(mix, nat_s, features, block=0):
    count, examples, _ = nat_s.shape
    now = pl.ds(pl.multiple_of(block * examples, examples), examples)

    for t in range(count):
        nat_s[t, :, :features] = mix[t * features : (t + 1) * features, now].T


def natural_groups(nat_s, features):
    found = []
    for first in range(0, nat_s.shape[1], 2 * GROUP):
        mixes = nat_s[:, first : first + 2 * GROUP, :features].astype(f32)
        found += [mixes[:, :GROUP], mixes[:, GROUP:]]
    return [item.reshape(-1, features).astype(bf16) for item in found]


def early_kernel(gmix, xt, mixer, gt, mix_acc, nat_s):
    _, features, lanes = xt.shape
    groups = nat_s.shape[1] // GROUP
    base = pl.program_id(0) * groups
    rows = nat_s.shape[0] * GROUP
    own = slice(lanes - rows, lanes)

    @pl.when(pl.program_id(0) == 0)
    def clear():
        mix_acc[...] = jnp.zeros_like(mix_acc)

    to_natural(gmix, nat_s, features)

    total = mix_acc[...]
    for u, g_mix in enumerate(natural_groups(nat_s, features)):
        total = total + mul(g_mix, xt[u])
        gt[base + u] = mul(g_mix, mixer[own], TN).astype(bf16)
    mix_acc[...] = total


def back_kernel(start, gn, pair, gain, gmix, xt, mixer, early, *refs):
    *before, gt, gain_acc, bias_acc, mix_acc, project_acc, gp_s, nat_s = refs
    sums = (gain_acc, bias_acc, mix_acc, project_acc)
    _, features, lanes = xt.shape
    block = start + pl.program_id(0)
    groups = gp_s.shape[0] // GROUP
    base = block * groups
    tokens = lanes // GROUP
    ranks = gp_s.shape[1] // tokens
    per_tile = 128 // tokens
    rows = nat_s.shape[0] * GROUP

    @pl.when(pl.program_id(0) == 0)
    def clear():
        for i, acc in enumerate(sums):
            acc[...] = before[i][...] if before else jnp.zeros_like(acc)

    values = pair[...]
    centred = values - jnp.mean(values, axis=0, keepdims=True)
    scale = lax.rsqrt(jnp.mean(centred * centred, axis=0, keepdims=True) + EPS)
    hat = centred * scale
    g = gn[...]
    gain_acc[...] += g * hat
    bias_acc[...] += g
    h = g * gain[...]
    mean_h = jnp.mean(h, axis=0, keepdims=True)
    mean_hx = jnp.mean(h * hat, axis=0, keepdims=True)
    gp_s[...] = (scale * (h - mean_h - hat * mean_hx)).T
    to_natural(gmix, nat_s, features, block)
    example = lax.broadcasted_iota(jnp.int32, (GROUP, 128), 0)
    place = lax.broadcasted_iota(jnp.int32, (GROUP, 128), 1) // tokens
    own = place == example % per_tile
    keep_low = jnp.logical_and(own, example < per_tile)
    keep_high = jnp.logical_and(own, example >= per_tile)

    project = mixer[lanes:]
    stacked = xt[...].reshape(groups * features, lanes)
    projected = mul(stacked, project, NT).astype(bf16)
    g_pairs, g_parts = [], []
    for u in range(groups):
        here = slice(u * GROUP, (u + 1) * GROUP)
        slabs = []
        for j in range(ranks):
            c, s = j // per_tile, j % per_tile
            one = turn(gp_s[here, c * 128 : c * 128 + 128], -s * tokens)
            slabs.append(
                jnp.concatenate([jnp.where(keep_low, one, 0.0), jnp.where(keep_high, one, 0.0)], axis=1)
            )
        g_pairs.append(jnp.concatenate(slabs, axis=0).astype(bf16))
        g_parts.append(mul(xt[u], g_pairs[u], NT).astype(bf16))
    g_projected = jnp.concatenate(g_parts, axis=0)
    project_acc[...] += mul(stacked, g_projected, TN)
    shared = mul(g_projected, project)
    mix_total = mix_acc[...]
    for u, g_mix in enumerate(natural_groups(nat_s, features)):
        mix_total = mix_total + mul(g_mix, xt[u])
        mine = slice(u * features, (u + 1) * features)
        part = mul(projected[mine], g_pairs[u]) + mul(g_mix, mixer[:rows], TN) + shared[mine]
        gt[base + u] = (part + early[base + u].astype(f32)).astype(bf16)
    mix_acc[...] = mix_total


def spread_kernel(start, first_half, starts, ends, gt, out):
    step = start + pl.program_id(0)
    chunks = out.shape[1] // CHUNK
    last = starts.shape[0] - 1
    span = CHUNK // 128 + 1

    for c in range(chunks):
        number = step * chunks + c
        first = jnp.minimum(first_half[number], last + 1 - span)
        lows, highs, values = [], [], []
        for i in range(span):
            half = first + i
            lows.append(starts[pl.ds(half, 1), :])
            highs.append(ends[pl.ds(half, 1), :])
            values.append(gt[half // 2, :, pl.ds(pl.multiple_of(half % 2 * 128, 128), 128)])
        low = jnp.concatenate(lows, axis=1) - number * CHUNK
        high = jnp.concatenate(highs, axis=1) - number * CHUNK
        hot = one_hot(low, high, CHUNK)
        part = mul(jnp.concatenate(values, axis=1), hot, NT)
        out[:, c * CHUNK : (c + 1) * CHUNK] = part.astype(bf16)


def passing(kernel, given, previous):
    if not previous:
        return kernel, {}
    more = len(previous)
    skip = lambda *refs: kernel(*refs[:given], *refs[given + more :])
    return skip, {given + i: i for i in range(more)}


HBM, VMEM = pltpu.HBM, pltpu.VMEM
INSIDE = pl.BlockSpec(memory_space=pltpu.VMEM)


def held(*arrays):
    return [pltpu.with_memory_space_constraint(array, pltpu.VMEM) for array in arrays]


def away(*arrays):
    return [pltpu.with_memory_space_constraint(array, pltpu.HBM) for array in arrays]


def whole(shape):
    return pl.BlockSpec(shape, lambda *_: (0,) * len(shape))


def rank_of(tokens):
    per_tile = 128 // tokens
    slab, example = np.arange(per_tile)[:, None], np.arange(GROUP)[None, :]
    return np.eye(per_tile, dtype=np.float32)[(slab + example) % per_tile]


def make_mixer(w_res, w_comp, p_proj):
    tokens = w_res.shape[0]
    fm_tokens = tokens - w_comp.shape[0]
    mix = w_res.astype(f32) + jnp.pad(w_comp.astype(f32), ((fm_tokens, 0), (0, 0)))
    mix = jnp.broadcast_to(mix[:, None, :], (tokens, GROUP, tokens))
    by_tile = p_proj.T.astype(f32).reshape(-1, 128 // tokens, tokens)
    project = jnp.einsum("cqt,seq->cset", by_tile, rank_of(tokens))
    both = jnp.concatenate([mix, project.reshape(-1, GROUP, tokens)], axis=0)
    wide = both[:, :, None, :] * np.eye(GROUP, dtype=np.float32)[None, :, :, None]
    return wide.reshape(both.shape[0] * GROUP, GROUP * tokens).astype(bf16)


def token_stage(offs, starts, ends, rows, mixer, gain, bias, tokens, fm_tokens):
    features, row_total = rows.shape
    group_count, lanes = starts.shape
    examples = group_count * GROUP
    pairs = gain.shape[0]
    groups = BLOCK // GROUP
    return pl.pallas_call(
        tokens_kernel,
        name="tokens",
        grid_spec=pltpu.PrefetchScalarGridSpec(
            num_scalar_prefetch=1,
            grid=(examples // BLOCK,),
            in_specs=[
                pl.BlockSpec((groups, lanes), lambda i, _: (i, 0)),
                pl.BlockSpec((groups, lanes), lambda i, _: (i, 0)),
                pl.BlockSpec(memory_space=pltpu.VMEM),
                whole(mixer.shape),
                whole(gain.shape),
                whole(bias.shape),
            ],
            out_specs=[
                pl.BlockSpec((groups, features, lanes), lambda i, _: (i, 0, 0)),
                pl.BlockSpec((pairs, BLOCK), lambda i, _: (0, i)),
                pl.BlockSpec((pairs, BLOCK), lambda i, _: (0, i)),
                pl.BlockSpec((fm_tokens * features, BLOCK), lambda i, _: (0, i)),
                pl.BlockSpec(((tokens - fm_tokens) * features, BLOCK), lambda i, _: (0, i)),
            ],
            scratch_shapes=[
                pltpu.VMEM((BLOCK, pairs), f32),
                pltpu.VMEM((tokens, BLOCK, 256), f32),
                pltpu.VMEM((groups, features, lanes), f32),
            ],
        ),
        out_shape=[
            HBM((group_count, features, lanes), bf16),
            HBM((pairs, examples), f32),
            HBM((pairs, examples), bf16),
            HBM((fm_tokens * features, examples), bf16),
            HBM(((tokens - fm_tokens) * features, examples), bf16),
        ],
        compiler_params=params(36),
        cost_estimate=pl.CostEstimate(
            flops=2 * features * lanes * (row_total * 2 + 1000 * group_count),
            bytes_accessed=row_total * features * 2 + 30 * examples * 1024,
            transcendentals=0,
        ),
    )(offs, starts, ends, *away(rows), mixer, gain, bias)


def final_stage(res, cot, gain, bias, features):
    part, examples = res.shape
    width = cot.shape[1]
    tall = pl.BlockSpec((part, BLOCK), lambda i: (0, i))
    flat = pl.BlockSpec((BLOCK, part), lambda i: (i, 1))
    first = pl.BlockSpec((BLOCK, width - part), lambda i: (i, 0))
    turned = pl.BlockSpec((width - part, BLOCK), lambda i: (0, i))
    res, cot = away(res, cot)
    return pl.pallas_call(
        functools.partial(final_kernel, features),
        name="final_comp",
        grid=(examples // BLOCK,),
        in_specs=[tall, flat, first, whole(gain.shape), whole(bias.shape)],
        out_specs=[flat, tall, turned, whole((features, BLOCK)), whole((features, BLOCK))],
        out_shape=[
            HBM((examples, width), bf16),
            HBM((part, examples), bf16),
            HBM((width - part, examples), bf16),
            jax.ShapeDtypeStruct((features, BLOCK), f32),
            jax.ShapeDtypeStruct((features, BLOCK), f32),
        ],
        scratch_shapes=[pltpu.VMEM((part, BLOCK), bf16), pltpu.VMEM((part, BLOCK), bf16)],
        compiler_params=params(16),
        cost_estimate=pl.CostEstimate(
            flops=200 * part * examples, bytes_accessed=8 * part * examples, transcendentals=0
        ),
    )(res, cot, cot, gain, bias)


def mlp_stage(every, normed, res, cot, b_up, b_down, gain, bias, features, previous):
    units, columns = every.shape
    pairs, examples = normed.shape
    part = columns - pairs
    lanes = 2 * BLOCK
    block = lambda i: jnp.maximum(i - 1, 0)
    every, normed, res, cot, previous = away(every, normed, res, cot, previous)
    operands = (every, normed, res, cot, b_up, b_down, gain, bias)
    kernel, aliases = passing(functools.partial(mlp_kernel, features), len(operands), (previous,))
    return pl.pallas_call(
        kernel,
        name="mlp",
        grid=(1 + examples // lanes,),
        in_specs=[
            pl.BlockSpec(memory_space=pl.ANY),
            pl.BlockSpec(memory_space=pl.ANY),
            pl.BlockSpec(memory_space=pl.ANY),
            pl.BlockSpec(memory_space=pl.ANY),
            whole(b_up.shape),
            whole(b_down.shape),
            whole(gain.shape),
            whole(bias.shape),
            pl.BlockSpec(memory_space=pl.ANY),
        ],
        out_specs=[
            pl.BlockSpec((lanes, part), lambda i: (block(i), 0)),
            INSIDE,
            INSIDE,
            INSIDE,
            pl.BlockSpec((pairs, lanes), lambda i: (0, block(i))),
            whole((features, BLOCK)),
            whole((features, BLOCK)),
            whole((units, BLOCK)),
            whole((part, BLOCK)),
        ],
        out_shape=[
            HBM(previous.shape, bf16),
            VMEM((part, examples), bf16),
            VMEM((units, examples), bf16),
            VMEM((units, examples), bf16),
            HBM((pairs, examples), f32),
            jax.ShapeDtypeStruct((features, BLOCK), f32),
            jax.ShapeDtypeStruct((features, BLOCK), f32),
            jax.ShapeDtypeStruct((units, BLOCK), f32),
            jax.ShapeDtypeStruct((part, BLOCK), f32),
        ],
        scratch_shapes=[
            pltpu.VMEM((units, examples), f32),
            pltpu.VMEM((part, lanes), bf16),
            pltpu.VMEM((units, BLOCK), f32),
            pltpu.VMEM((part, BLOCK), f32),
            pltpu.VMEM((units, pairs), bf16),
            pltpu.VMEM((units, part), bf16),
            pltpu.VMEM((pairs, examples), bf16),
            pltpu.VMEM((part, examples), bf16),
            pltpu.VMEM((part, examples), bf16),
            pltpu.SemaphoreType.DMA((3 + 2 * (examples // lanes),)),
        ],
        input_output_aliases=aliases,
        compiler_params=params(43),
        cost_estimate=pl.CostEstimate(
            flops=4 * units * columns * examples,
            bytes_accessed=2 * units * columns + 10 * part * examples,
            transcendentals=2 * units * examples,
        ),
    )(*operands, previous)


def early_stage(gmix, xt, mixer):
    group_count, features, lanes = xt.shape
    part, examples = gmix.shape
    count = part // features
    return pl.pallas_call(
        early_kernel,
        name="early",
        grid=(examples // BLOCK,),
        in_specs=[
            pl.BlockSpec((part, BLOCK), lambda i: (0, i)),
            pl.BlockSpec((BLOCK // GROUP, features, lanes), lambda i: (i, 0, 0)),
            whole(mixer.shape),
        ],
        out_specs=[INSIDE, whole((count * GROUP, lanes))],
        out_shape=[
            VMEM((group_count, features, lanes), bf16),
            jax.ShapeDtypeStruct((count * GROUP, lanes), f32),
        ],
        scratch_shapes=[pltpu.VMEM((count, BLOCK, 256), bf16)],
        compiler_params=params(16),
        cost_estimate=pl.CostEstimate(
            flops=2 * features * lanes * 500 * group_count,
            bytes_accessed=group_count * features * lanes * 8,
            transcendentals=0,
        ),
    )(*away(gmix, xt), mixer)


def back_stage(gn, pair, gain, gmix, xt, mixer, gt, start, count, before):
    pairs, examples = pair.shape
    group_count, features, lanes = xt.shape
    ranked = mixer.shape[0] - lanes
    fm_tokens = gmix.shape[0] // features
    wide = pl.BlockSpec((pairs, BLOCK), lambda i: (0, start + i))
    sums = [(pairs, BLOCK), (pairs, BLOCK), (fm_tokens * GROUP, lanes), (lanes, ranked)]
    gn, pair, xt = away(gn, pair, xt)
    gmix, gt = held(gmix, gt)
    by_group = pl.BlockSpec((BLOCK // GROUP, features, lanes), lambda i: (start + i, 0, 0))
    operands = (gn, pair, gain, gmix, xt, mixer, gt, *before)
    return pl.pallas_call(
        functools.partial(back_kernel, start),
        name="back",
        grid=(count,),
        in_specs=[wide, wide, whole(gain.shape), INSIDE, by_group, whole(mixer.shape), INSIDE]
        + [whole(item.shape) for item in before],
        out_specs=[INSIDE] + [whole(shape) for shape in sums],
        out_shape=[VMEM((group_count, features, lanes), bf16)]
        + [jax.ShapeDtypeStruct(shape, f32) for shape in sums],
        scratch_shapes=[
            pltpu.VMEM((BLOCK, pairs), f32),
            pltpu.VMEM((fm_tokens, BLOCK, 256), bf16),
        ],
        input_output_aliases={6: 0},
        compiler_params=params(20),
        cost_estimate=pl.CostEstimate(
            flops=2 * features * lanes * 1400 * BLOCK // GROUP * count,
            bytes_accessed=40 * BLOCK * count * 1024,
            transcendentals=0,
        ),
    )(*operands)


def exact(value, selector, dims=NN):
    total = None
    for _ in range(3):
        piece = value.astype(bf16)
        value = value - piece.astype(f32)
        total = mul(piece, selector, dims) if total is None else total + mul(piece, selector, dims)
    return total


def ones_where(condition):
    return jnp.where(condition, 1.0, 0.0).astype(bf16)


def by_token_order(pairs, tokens):
    ranks = pairs // tokens
    row = lax.broadcasted_iota(jnp.int32, (pairs, pairs), 0)
    lane = lax.broadcasted_iota(jnp.int32, (pairs, pairs), 1)
    return ones_where((row % tokens) * ranks + row // tokens == lane)


def small_rows(tokens, pairs, units, width, features):
    counts = [tokens, pairs // 128, pairs // 128, units // 128, width // 128, -(-features // 128)]
    counts.append(counts[-1])
    starts = np.cumsum([0] + counts)
    return [(int(start), count) for start, count in zip(starts, counts)], -(-int(starts[-1]) // 8) * 8


def small_kernel(tokens, places, gain_acc, bias_acc, mix_fm, mix_comp, project, up, down, gains, biases, out):
    def put(place, row):
        start, count = place
        for i in range(count):
            piece = row[:, i * 128 : i * 128 + 128]
            out[start + i : start + i + 1, : piece.shape[1]] = piece

    def lying(column):
        return jnp.sum(column.T, axis=0, keepdims=True)

    out[...] = jnp.zeros_like(out)
    lanes = mix_fm.shape[1]
    ranked = project.shape[1]
    per_tile = 128 // tokens
    mix = jnp.concatenate([mix_fm[...], mix_comp[...]], axis=0)
    row = lax.broadcasted_iota(jnp.int32, mix.shape, 0) % GROUP
    lane = lax.broadcasted_iota(jnp.int32, mix.shape, 1) // tokens
    mix = jnp.where(row == lane, mix, 0.0)
    fold = ones_where(
        lax.broadcasted_iota(jnp.int32, (lanes, tokens), 0) % tokens
        == lax.broadcasted_iota(jnp.int32, (lanes, tokens), 1)
    )
    folded_mix = exact(mix, fold).reshape(tokens, GROUP, tokens)
    row = lax.broadcasted_iota(jnp.int32, project.shape, 0) // tokens
    lane = lax.broadcasted_iota(jnp.int32, project.shape, 1) % GROUP
    cells = jnp.where(row == lane, project[...], 0.0).reshape(GROUP, tokens, ranked)
    cells = jnp.sum(cells, axis=0)
    ranks = ranked // GROUP
    row = lax.broadcasted_iota(jnp.int32, (ranks, ranked), 0)
    lane = lax.broadcasted_iota(jnp.int32, (ranks, ranked), 1)
    slab = lane // GROUP
    rank = slab // per_tile * per_tile + (lane % GROUP + slab % per_tile) % per_tile
    pick = ones_where(row == rank)
    projected = None
    for _ in range(3):
        piece = cells.astype(bf16)
        cells = cells - piece.astype(f32)
        part = mul(pick, piece, NT)
        projected = part if projected is None else projected + part
    out[:ranks, :tokens] = projected
    out[:tokens, tokens : 2 * tokens] = jnp.sum(folded_mix, axis=1)
    both = jnp.concatenate([lying(gain_acc[...]), lying(bias_acc[...])], axis=0)
    both = exact(both, by_token_order(both.shape[1], tokens))
    put(places[1], both[:1])
    put(places[2], both[1:])
    put(places[3], lying(up[...]))
    put(places[4], lying(down[...]))
    put(places[5], lying(gains[0] + gains[1]))
    put(places[6], lying(biases[0] + biases[1]))


def small_stage(tokens, places, rows, gain_acc, bias_acc, mix_fm, mix_comp, project, up, down, gains, biases):
    def kernel(*refs):
        *given, gain_0, gain_1, bias_0, bias_1, out = refs
        small_kernel(tokens, places, *given, (gain_0[...], gain_1[...]), (bias_0[...], bias_1[...]), out)

    operands = (gain_acc, bias_acc, mix_fm, mix_comp, project, up, down, *gains, *biases)
    return pl.pallas_call(
        kernel,
        name="small",
        out_shape=jax.ShapeDtypeStruct((rows, 128), f32),
        compiler_params=params(16),
        cost_estimate=pl.CostEstimate(flops=10**9, bytes_accessed=4 * 10**6, transcendentals=0),
    )(*operands)


def last_kernel(tokens, places, total, more, *refs):
    *vectors, up, down, p_proj, w_res, w_comp, gain_one, bias_one, b_up, b_down, gain_two, bias_two = refs
    pairs = up.shape[1]
    value = total[...] + more[...].astype(f32)
    down[...] = value[:, pairs:]
    up[...] = exact(value[:, :pairs], by_token_order(pairs, tokens))
    vector = sum([ref[...] for ref in vectors])
    p_proj[...] = vector[: p_proj.shape[0], :tokens]
    w_res[...] = vector[:tokens, tokens : 2 * tokens]
    w_comp[...] = vector[tokens - w_comp.shape[0] : tokens, tokens : 2 * tokens]
    rest = (gain_one, bias_one, b_up, b_down, gain_two, bias_two)
    for (start, count), ref in zip(places[1:], rest):
        if ref.shape[0] == 1:
            row = [vector[start + i : start + i + 1] for i in range(count)]
            ref[...] = jnp.concatenate(row, axis=1)[:, : ref.shape[1]]
        else:
            ref[...] = vector[start : start + count]


def last_stage(total, more, vectors, places, pairs, tokens, features, comp_tokens):
    rows, columns = total.shape
    shapes = [(rows, pairs), (rows, columns - pairs), (pairs // tokens, tokens), (tokens, tokens), (comp_tokens, tokens)]
    shapes += [(count, 128) for _, count in places[1:-2]] + [(1, features)] * 2
    return pl.pallas_call(
        functools.partial(last_kernel, tokens, places),
        name="last",
        out_shape=[jax.ShapeDtypeStruct(shape, f32) for shape in shapes],
        compiler_params=params(16),
        cost_estimate=pl.CostEstimate(
            flops=6 * rows * pairs * pairs, bytes_accessed=10 * rows * columns, transcendentals=0
        ),
    )(total, more, *vectors)


def grad_kernel(rows, table, pre, hidden, normed, mix, *refs):
    *outs, picked_s = refs
    pairs = normed.shape[0]
    parts = 2
    part = mix.shape[0] // parts

    def picked(source):
        for i in range(picked_s.shape[0] // rows):
            start = pl.multiple_of(table[i] * rows, rows)
            picked_s[i * rows : (i + 1) * rows, :] = source[pl.ds(start, rows), :]
        return picked_s[...]

    def put(at, right, left):
        value = mul(left, right, NT).astype(bf16)
        first = 0
        for out in outs:
            out[:, at : at + right.shape[0]] = value[first : first + out.shape[0]]
            first += out.shape[0]

    left = picked(hidden)
    for i in range(parts):
        put(pairs + i * part, mix[i * part : (i + 1) * part, :], left)
    put(0, normed[...], picked(pre))


def grad_stage(tables, pre, hidden, normed, mix, rows):
    units, examples = hidden.shape
    pairs = normed.shape[0]
    columns = pairs + mix.shape[0]
    counts = [table.shape[0] * rows for table in tables]
    count = sum(counts)
    pre, hidden, normed, mix = held(pre, hidden, normed, mix)
    return pl.pallas_call(
        functools.partial(grad_kernel, rows),
        name="weight_grads",
        grid_spec=pltpu.PrefetchScalarGridSpec(
            num_scalar_prefetch=1,
            grid=(1,),
            in_specs=[INSIDE] * 4,
            out_specs=[INSIDE] * len(counts),
            scratch_shapes=[pltpu.VMEM((count, examples), bf16)],
        ),
        out_shape=[VMEM((size, columns), bf16) for size in counts],
        compiler_params=params(16),
        cost_estimate=pl.CostEstimate(
            flops=2 * count * examples * columns,
            bytes_accessed=2 * count * columns + 2 * examples * (2 * units + columns),
            transcendentals=0,
        ),
    )(jnp.concatenate(tables), pre, hidden, normed, mix)


def spread_stage(first_half, starts, ends, gt, row_total, start, count, previous):
    group_count, features, lanes = gt.shape
    operands = (starts.reshape(-1, 128), ends.reshape(-1, 128), *held(gt))
    previous = away(*previous)
    kernel, aliases = passing(functools.partial(spread_kernel, start), len(operands) + 1, previous)
    return pl.pallas_call(
        kernel,
        name="spread",
        grid_spec=pltpu.PrefetchScalarGridSpec(
            num_scalar_prefetch=1,
            grid=(count,),
            in_specs=[whole(operands[0].shape), whole(operands[1].shape), INSIDE]
            + [pl.BlockSpec(memory_space=pl.ANY)] * len(previous),
            out_specs=pl.BlockSpec((features, SPREAD_ROWS), lambda i, _: (0, start + i)),
        ),
        out_shape=HBM((features, row_total), bf16),
        input_output_aliases=aliases,
        compiler_params=params(16),
        cost_estimate=pl.CostEstimate(
            flops=4 * features * lanes * SPREAD_ROWS * count,
            bytes_accessed=SPREAD_ROWS * count * features * 4,
            transcendentals=0,
        ),
    )(first_half, *operands, *previous)


def bag_bounds(lengths):
    ends = jnp.cumsum(lengths.reshape(-1))
    starts = ends - lengths.reshape(-1)
    return starts, ends


def column(vector, lanes=BLOCK):
    return jnp.broadcast_to(vector[:, None], (vector.shape[0], lanes))


def gelu(v):
    inner = np.sqrt(2 / np.pi).astype(np.float32) * (v + 0.044715 * (v * v * v))
    return 0.5 * v * (1.0 + jnp.tanh(inner))


def gelu_slope(v):
    root = np.sqrt(2 / np.pi).astype(np.float32)
    bent = jnp.tanh(root * (v + 0.044715 * (v * v * v)))
    return 0.5 * (1.0 + bent) + 0.5 * v * (1.0 - bent * bent) * root * (1.0 + 3 * 0.044715 * (v * v))


def shards(
    embed_rows,
    lengths,
    cotangent,
    p_proj,
    gain_one,
    bias_one,
    w_up,
    b_up,
    w_down,
    b_down,
    w_comp,
    w_res,
    gain_two,
    bias_two,
):
    links = Links()
    tokens = w_res.shape[0]
    features = embed_rows.shape[1]
    ranks = p_proj.shape[1]
    pairs = tokens * ranks
    row_total = embed_rows.shape[0]
    fm_width = b_down.shape[0]
    examples = cotangent.shape[0]

    def by_rank(vector):
        return jnp.swapaxes(vector.reshape(-1, tokens, ranks), 1, 2).reshape(vector.shape)

    def by_token(vector):
        return jnp.swapaxes(vector.reshape(-1, ranks, tokens), 1, 2).reshape(vector.shape)

    every = links.gather(jnp.concatenate([by_rank(w_up.T), w_down], axis=1))

    starts, ends = bag_bounds(lengths)
    lanes = GROUP * tokens
    starts = starts.reshape(-1, lanes)
    ends = ends.reshape(-1, lanes)
    offs = jnp.concatenate([starts[:, 0], ends[-1:, -1]])
    bases = jnp.arange(row_total // CHUNK, dtype=jnp.int32) * CHUNK
    half_ends = ends.reshape(-1, 128)[:, 127]
    first_half = jnp.sum((half_ends[None, :] <= bases[:, None]).astype(jnp.int32), axis=1)
    mixer = make_mixer(w_res, w_comp, p_proj)
    gain_a, bias_a = column(by_rank(gain_one)), column(by_rank(bias_one))
    gain_b, bias_b = column(gain_two), column(bias_two)
    down_bias = column(b_down)

    xt, pair, normed, res, res_comp = token_stage(
        offs, starts, ends, embed_rows.T, mixer, gain_a, bias_a, tokens, fm_width // features
    )
    out, mix_comp, cot, gain_acc1, bias_acc1 = final_stage(res_comp, cotangent, gain_b, bias_b, features)
    mix_comp, first_half = lax.optimization_barrier((mix_comp, first_half))
    gt, mix_acc1 = early_stage(mix_comp, xt, mixer)
    gt, normed = lax.optimization_barrier((gt, normed))
    out, mix, hidden, g_pre, g_normed, gain_acc0, bias_acc0, up_acc, down_acc = mlp_stage(
        every, normed, res, cot, b_up[None, :], b_down[None, :], gain_b, bias_b, features, out
    )

    unit_rows = links.unit_rows(w_down.shape[0])
    tables, rows, (g_pre, hidden) = links.shards(unit_rows, g_pre, hidden)
    ring = links.ring(unit_rows)
    gradients = lambda *tables: grad_stage(tables, g_pre, hidden, normed, mix, rows)
    (sent,) = gradients(tables[0])
    crossing = links.to_other_core(sent)
    g_pre, hidden, sent = lax.optimization_barrier((g_pre, hidden, sent))
    (mine,) = gradients(tables[1])
    ring.add(*lax.optimization_barrier((mine, crossing)))
    g_pre, hidden = ring.start((g_pre, hidden))
    sent, mine = gradients(tables[2], tables[3])
    sent, mine, g_normed = ring.finish((sent, mine, g_normed))
    sent, mine, g_normed = ring.start((sent, mine, g_normed))
    crossing = links.to_other_core(sent)

    blocks = examples // BLOCK
    cuts = [0, blocks // 2, blocks]
    sums = []
    for i in range(2):
        if i > 0:
            g_normed, gt, sums = ring.start((g_normed, gt, sums))
        gt, *sums = back_stage(
            g_normed, pair, gain_a, mix, xt, mixer, gt, cuts[i], cuts[i + 1] - cuts[i], sums
        )
        if i == 0:
            g_normed, gt, sums, crossing, mine = lax.optimization_barrier((g_normed, gt, sums, crossing, mine))
            ring.add(mine, crossing)
        g_normed, gt, sums = ring.finish((g_normed, gt, sums))
    gt, sums = ring.start((gt, sums))
    gain_acc, bias_acc, mix_acc0, project_acc = sums
    places, rows = small_rows(tokens, pairs, b_up.shape[0], fm_width, features)
    vector = small_stage(
        tokens,
        places,
        rows,
        gain_acc,
        bias_acc,
        mix_acc0,
        mix_acc1,
        project_acc,
        up_acc,
        down_acc,
        (gain_acc0, gain_acc1),
        (bias_acc0, bias_acc1),
    )

    steps = row_total // SPREAD_ROWS
    swaps = links.rounds()
    cuts = [0, steps * 5 // 9, steps * 7 // 9, steps]
    rows_grad = ()
    for i in range(3):
        if i == 1:
            vector, gt, rows_grad = ring.start((vector, gt, rows_grad))
        far = [swap(vector) for swap in swaps[i]]
        rows_grad = spread_stage(
            first_half, starts, ends, gt, row_total, cuts[i], cuts[i + 1] - cuts[i], rows_grad
        )
        far, gt, rows_grad = lax.optimization_barrier((far, gt, (rows_grad,)))
        vector = sum(far, vector)
        if i != 1:
            vector, gt, rows_grad = ring.finish((vector, gt, rows_grad))
    for some in swaps[3:]:
        vector = sum([swap(vector) for swap in some], vector)
    vectors = [vector]
    up_grad, down_grad, proj_grad, res_grad, comp_grad, *rest = last_stage(
        *ring.end(), vectors, places, pairs, tokens, features, w_comp.shape[0]
    )
    rest = [item.reshape(-1) for item in rest]
    return (
        out,
        rows_grad[0].T,
        proj_grad.T,
        rest[0],
        rest[1],
        up_grad.T,
        rest[2],
        down_grad,
        rest[3],
        comp_grad,
        res_grad,
        rest[4],
        rest[5],
    )


def ring_order(chips):
    return list(range(0, chips, 2)) + list(range(chips - 1, 0, -2))


def added(*terms):
    return sum([term.astype(f32) for term in terms[1:]], terms[0].astype(f32))


def ring_shards(chips):
    order = ring_order(chips)
    reach = chips // 2
    steps = [reach]
    for distance in range(reach - 1, 0, -1):
        steps += [distance, -distance]
    steps.append(0)
    return [[order[(order.index(chip) + step) % chips] for step in steps] for chip in range(chips)]


class Ring:
    def __init__(self, rows):
        self.rows = rows
        self.chips = lax.axis_size("dp") // 2
        self.order = ring_order(self.chips)
        self.reach = self.chips // 2
        self.shards = []
        self.left = self.reach
        self.flying = None
        self.send = None
        self.total = None

    def add(self, *terms):
        terms = [term.reshape(-1, self.rows, term.shape[-1]) for term in terms]
        self.shards += [[term[i] for term in terms] for i in range(terms[0].shape[0])]

    def ahead(self, distance):
        return self.shards[1 + 2 * (self.reach - 1 - distance)]

    def behind(self, distance):
        return self.shards[2 + 2 * (self.reach - 1 - distance)]

    def along(self, value, step):
        order, chips = self.order, self.chips
        pairs = [
            (2 * order[i] + core, 2 * order[(i + step) % chips] + core)
            for i in range(chips)
            for core in range(2)
        ]
        return lax.ppermute(value, "dp", pairs)

    def start(self, others):
        if self.left < 0:
            return others
        if self.send is None:
            middle = added(*self.shards[0]).astype(bf16)
            rows = middle.shape[0] // 2
            self.send = [middle[:rows], middle[rows:]]
        self.send, others = lax.optimization_barrier((self.send, others))
        if self.left > 0:
            self.flying = (self.along(self.send[0], 1), self.along(self.send[1], -1))
        else:
            pairs = [(i, i ^ 1) for i in range(lax.axis_size("branch"))]
            self.flying = (lax.ppermute(self.send[0], "branch", pairs),)
        return others

    def finish(self, others):
        if self.flying is None:
            return others
        arrived, others = lax.optimization_barrier((self.flying, others))
        self.flying = None
        self.left -= 1
        if self.left < 0:
            self.more = arrived[0]
        elif self.left == 0:
            self.total = added(*self.shards[-1], *arrived)
            self.send = [self.total.astype(bf16)]
        else:
            one, two = added(*self.ahead(self.left)), added(*self.behind(self.left))
            first, second = arrived[0].astype(f32), arrived[1].astype(f32)
            if self.left == self.reach - 1:
                rows = first.shape[0]
                first = jnp.pad(first, ((0, one.shape[0] - rows), (0, 0)))
                second = jnp.pad(second, ((two.shape[0] - rows, 0), (0, 0)))
            self.send = [(one + first).astype(bf16), (two + second).astype(bf16)]
        return others

    def end(self):
        while self.left >= 0:
            self.start(())
            self.finish(())
        return self.total, self.more


class Links:
    def swaps(self, bits):
        dp, branch = lax.axis_size("dp"), lax.axis_size("branch")
        found = []
        for chosen in range(1, 1 << len(bits)):
            flip = functools.reduce(lambda a, b: a | b, [bit for i, bit in enumerate(bits) if chosen >> i & 1])
            pairs = [(i, i ^ flip) for i in range(dp * branch)]
            found.append(lambda value, pairs=pairs: lax.ppermute(value, ("dp", "branch"), pairs))
        return found

    def rounds(self):
        size = lax.axis_size("dp") * lax.axis_size("branch")
        bits = [1 << i for i in range(size.bit_length() - 1)]
        return [self.swaps(bits[i : i + 2]) for i in range(0, len(bits), 2)]

    def gather(self, own):
        return lax.all_gather(own, "dp", axis=0, tiled=True)

    def unit_rows(self, rows):
        return rows

    def owners(self):
        owners = np.asarray(ring_shards(lax.axis_size("dp") // 2), np.int32)
        table = np.stack([2 * owners + 1, 2 * owners, 2 * owners, 2 * owners + 1], axis=1)
        table = table.reshape(-1, 2 * owners.shape[1])
        return lax.dynamic_index_in_dim(jnp.asarray(table), lax.axis_index("dp"), 0, keepdims=False)

    def shards(self, rows, *units):
        table = self.owners()
        first = 3
        if rows % 16 != 0:
            units = [item.reshape(table.shape[0], rows, -1)[table].reshape(item.shape) for item in units]
            table = jnp.arange(units[0].shape[0] // 96, dtype=jnp.int32)
            rows, first = 96, 1
        half = table.shape[0] // 2
        cuts = [(0, first), (half, half + first), (first, half), (half + first, 2 * half)]
        return [table[a:b] for a, b in cuts], rows, units

    def to_other_core(self, value):
        return lax.ppermute(value, "dp", [(i, i ^ 1) for i in range(lax.axis_size("dp"))])

    def ring(self, rows):
        return Ring(rows)


def solution(mesh):
    spread = P(("dp", "branch"), None)
    in_specs = (
        spread,
        spread,
        spread,
        P(),
        P(),
        P(),
        P(None, "dp"),
        P(),
        P("dp", None),
        P(),
        P(),
        P(),
        P(),
        P(),
    )
    out_specs = (
        spread,
        spread,
        P(),
        P(),
        P(),
        P(None, "dp"),
        P(),
        P("dp", None),
        P(),
        P(),
        P(),
        P(),
        P(),
    )
    return jax.shard_map(shards, mesh=mesh, in_specs=in_specs, out_specs=out_specs, check_vma=False)
```

```python
import functools

import jax
import jax.numpy as jnp
import numpy as np
from jax import lax
from jax.experimental import pallas as pl
from jax.experimental.pallas import tpu as pltpu
from jax.sharding import PartitionSpec as P

EPS = 1e-05
GROUP = 8
BLOCK = 128
CHUNK = 256
TOGETHER = 8
SPREAD_ROWS = 16 * CHUNK

f32 = jnp.float32
bf16 = jnp.bfloat16

NN = (((1,), (0,)), ((), ()))
NT = (((1,), (1,)), ((), ()))
TN = (((0,), (0,)), ((), ()))


def mul(left, right, dims=NN):
    return lax.dot_general(left, right, dims, preferred_element_type=f32)


def params(mebibytes):
    return pltpu.CompilerParams(vmem_limit_bytes=mebibytes * 1024 * 1024)


def one_hot(low, high, rows):
    row = lax.broadcasted_iota(jnp.int16, (rows, low.shape[1]), 0)
    inside = jnp.logical_and(row >= low.astype(jnp.int16), row < high.astype(jnp.int16))
    return jnp.where(inside, jnp.ones((), bf16), jnp.zeros((), bf16))


def turn(tile, shift):
    return pltpu.roll(tile, shift % 128, 1) if shift % 128 else tile


def tokens_kernel(
    offs, starts, ends, rows, mixer, gain, bias, xt_ref, pair_ref, normed_ref, fm_ref, comp_ref, pair_s, nat_s, sum_s
):
    step = pl.program_id(0)
    groups = pair_s.shape[0] // GROUP
    row_total = rows.shape[1]
    features = rows.shape[0]
    tokens = nat_s.shape[0]
    ranks = pair_s.shape[1] // tokens
    lanes = tokens * GROUP
    per_tile = 128 // tokens
    span = 2 * CHUNK
    example = lax.broadcasted_iota(jnp.int32, (GROUP, 128), 0)
    place = lax.broadcasted_iota(jnp.int32, (GROUP, 128), 1) // tokens

    def some(k, carry):
        todo = [k * TOGETHER + u for u in range(TOGETHER)]
        bases = []
        for u, i in enumerate(todo):
            first = offs[step * groups + i]
            base = (first // 128) * 128
            bases.append(base)
            low = starts[pl.ds(i, 1), :]
            high = ends[pl.ds(i, 1), :]
            at = pl.multiple_of(jnp.minimum(base, row_total - span), 128)
            sum_s[u] = mul(rows[:, pl.ds(at, span)], one_hot(low - at, high - at, span))
        for u, i in enumerate(todo):
            base = bases[u] + span
            left = offs[step * groups + i + 1] - base

            @pl.when(left > 0)
            def more(u=u, i=i, base=base, left=left):
                low = starts[pl.ds(i, 1), :]
                high = ends[pl.ds(i, 1), :]

                def chunk(c, total):
                    wanted = base + c * CHUNK
                    at = pl.multiple_of(jnp.minimum(wanted, row_total - CHUNK), 128)
                    hot = one_hot(jnp.maximum(low, wanted) - at, high - at, CHUNK)
                    return total + mul(rows[:, pl.ds(at, CHUNK)], hot)

                sum_s[u] = lax.fori_loop(0, (left + CHUNK - 1) // CHUNK, chunk, sum_s[u])

        for u, i in enumerate(todo):
            x = sum_s[u].astype(bf16)
            xt_ref[i] = x
            nat = mul(mixer[...], x, NT)
            m = mul(nat[lanes:].astype(bf16), x)
            here = pl.ds(pl.multiple_of(i * GROUP, GROUP), GROUP)
            for c in range(ranks // per_tile):
                tile = None
                for s in range(per_tile):
                    at = GROUP * (c * per_tile + s)
                    slab = m[at : at + GROUP]
                    one = jnp.where(example < per_tile, slab[:, :128], slab[:, 128:])
                    one = turn(one, s * tokens)
                    mine = place == (example + s) % per_tile
                    tile = one if s == 0 else jnp.where(mine, one, tile)
                pair_s[here, c * 128 : c * 128 + 128] = tile
            for t in range(tokens):
                nat_s[t, here, :features] = nat[GROUP * t : GROUP * t + GROUP]
        return carry

    lax.fori_loop(0, groups // TOGETHER, some, 0)
    pair = pair_s[...].T
    pair_ref[...] = pair
    centred = pair - jnp.mean(pair, axis=0, keepdims=True)
    scale = lax.rsqrt(jnp.mean(centred * centred, axis=0, keepdims=True) + EPS)
    normed_ref[...] = (centred * scale * gain[...] + bias[...]).astype(bf16)

    fm_tokens = fm_ref.shape[0] // features
    for t in range(tokens):
        turned = nat_s[t].astype(bf16).T[:features]
        if t < fm_tokens:
            fm_ref[t * features : (t + 1) * features, :] = turned
        else:
            comp_ref[(t - fm_tokens) * features : (t - fm_tokens + 1) * features, :] = turned


def norm_token(summed, g, gain, bias):
    centred = summed - jnp.mean(summed, axis=0, keepdims=True)
    scale = lax.rsqrt(jnp.mean(centred * centred, axis=0, keepdims=True) + EPS)
    hat = centred * scale
    q = g * gain
    g_hat = g * hat
    mean_q = jnp.mean(q, axis=0, keepdims=True)
    mean_qx = jnp.mean(q * hat, axis=0, keepdims=True)
    return (hat * gain + bias).astype(bf16), (scale * (q - mean_q - hat * mean_qx)).astype(bf16), g_hat


def standing(row):
    return jnp.broadcast_to(row[...], (128, row.shape[1])).T


def folded(value):
    return sum(value[:, i : i + 128] for i in range(0, value.shape[1], 128))


def doubled(value, lanes):
    return jnp.concatenate([value] * (lanes // value.shape[1]), axis=1)


def final_kernel(features, res, cot, cot_fm, gain, bias, out, gmix, turned, gain_acc, bias_acc, cot_s, out_s):
    @pl.when(pl.program_id(0) == 0)
    def clear():
        gain_acc[...] = jnp.zeros_like(gain_acc)
        bias_acc[...] = jnp.zeros_like(bias_acc)

    cot_s[...] = cot[...].T
    turned[...] = cot_fm[...].T
    unroll = 4

    def some(k, carry):
        hats, gs = [], []
        for u in range(unroll):
            at = pl.ds(pl.multiple_of((k * unroll + u) * features, 32), features)
            g = cot_s[at, :].astype(f32)
            out_s[at, :], gmix[at, :], g_hat = norm_token(res[at, :].astype(f32), g, gain[...], bias[...])
            hats.append(g_hat)
            gs.append(g)
        gain_acc[...] += sum(hats)
        bias_acc[...] += sum(gs)
        return carry

    lax.fori_loop(0, res.shape[0] // features // unroll, some, 0)
    out[...] = out_s[...].T


def mlp_kernel(features, *refs):
    every, normed_hbm, res_hbm, cot_hbm, b_up, b_down, gain, bias = refs[:8]
    out, mix, hidden, g_pre, gain_acc, bias_acc, up_acc, down_acc = refs[8:16]
    pre_s, out_s, up_s, down_s, up_w, down_w, normed, res, cot, arrive = refs[16:]
    step = pl.program_id(0)
    pairs = normed.shape[0]
    lanes = out.shape[0]
    units = hidden.shape[0]
    width = res.shape[0]
    unit_tile = 256
    token_tile = 4 * features
    bring_normed = pltpu.make_async_copy(normed_hbm, normed, arrive.at[0])
    bring_up = pltpu.make_async_copy(every.at[:, pl.ds(0, pairs)], up_w, arrive.at[1])
    bring_down = pltpu.make_async_copy(every.at[:, pl.ds(pairs, width)], down_w, arrive.at[2])
    blocks = normed.shape[1] // lanes

    def bring_block(i):
        here = pl.ds(pl.multiple_of(i * lanes, lanes), lanes)
        return [
            pltpu.make_async_copy(res_hbm.at[:, here], res.at[:, here], arrive.at[3 + i]),
            pltpu.make_async_copy(cot_hbm.at[:, here], cot.at[:, here], arrive.at[3 + blocks + i]),
        ]

    @pl.when(step == 0)
    def up():
        bring_normed.start()
        bring_up.start()
        bring_down.start()
        for i in range(blocks):
            for copy in bring_block(i):
                copy.start()
        for acc in (gain_acc, bias_acc, up_acc, down_acc):
            acc[...] = jnp.zeros_like(acc)
        up_s[...] = standing(b_up)
        down_s[...] = standing(b_down)
        bring_normed.wait()
        bring_up.wait()
        for at in range(0, units, unit_tile):
            here = slice(at, at + unit_tile)
            pre = mul(up_w[here, :], normed[...]) + doubled(up_s[here, :], normed.shape[1])
            pre_s[here, :] = pre
            hidden[here, :] = gelu(pre).astype(bf16)
        bring_down.wait()

    @pl.when(step > 0)
    def rest():
        now = pl.ds(pl.multiple_of((step - 1) * lanes, lanes), lanes)
        for copy in bring_block(step - 1):
            copy.wait()
        wide_gain, wide_bias = doubled(gain[...], lanes), doubled(bias[...], lanes)

        def fm_tile(first):
            return mul(down_w[:, first : first + token_tile], hidden[:, now], TN)

        ahead = fm_tile(0)
        for first in range(0, width, token_tile):
            tile = ahead
            if first + token_tile < width:
                ahead = fm_tile(first + token_tile)
            hats, gs = [], []
            for u in range(4):
                here = slice(first + u * features, first + (u + 1) * features)
                fm = tile[u * features : (u + 1) * features, :] + doubled(down_s[here, :], lanes)
                g = cot[here, now].astype(f32)
                summed = res[here, now].astype(f32) + fm.astype(bf16).astype(f32)
                out_s[here, :], g_mix, g_hat = norm_token(summed, g, wide_gain, wide_bias)
                mix[here, now] = g_mix
                down_acc[here, :] += folded(g_mix.astype(f32))
                hats.append(folded(g_hat))
                gs.append(folded(g))
            gain_acc[...] += sum(hats)
            bias_acc[...] += sum(gs)
        for at in range(0, units, unit_tile):
            here = slice(at, at + unit_tile)
            g_hidden = mul(down_w[here, :], mix[:, now])
            value = (g_hidden * gelu_slope(pre_s[here, now])).astype(bf16)
            g_pre[here, now] = value
            up_acc[here, :] += folded(value.astype(f32))
        out[...] = out_s[...].T


def to_natural(mix, nat_s, features, block=0):
    count, examples, _ = nat_s.shape
    now = pl.ds(pl.multiple_of(block * examples, examples), examples)

    for t in range(count):
        nat_s[t, :, :features] = mix[t * features : (t + 1) * features, now].T


def natural_groups(nat_s, features):
    found = []
    for first in range(0, nat_s.shape[1], 2 * GROUP):
        mixes = nat_s[:, first : first + 2 * GROUP, :features].astype(f32)
        found += [mixes[:, :GROUP], mixes[:, GROUP:]]
    return [item.reshape(-1, features).astype(bf16) for item in found]


def early_kernel(gmix, xt, mixer, gt, mix_acc, nat_s):
    _, features, lanes = xt.shape
    groups = nat_s.shape[1] // GROUP
    base = pl.program_id(0) * groups
    rows = nat_s.shape[0] * GROUP
    own = slice(lanes - rows, lanes)

    @pl.when(pl.program_id(0) == 0)
    def clear():
        mix_acc[...] = jnp.zeros_like(mix_acc)

    to_natural(gmix, nat_s, features)

    total = mix_acc[...]
    for u, g_mix in enumerate(natural_groups(nat_s, features)):
        total = total + mul(g_mix, xt[u])
        gt[base + u] = mul(g_mix, mixer[own], TN).astype(bf16)
    mix_acc[...] = total


def back_kernel(start, gn, pair, gain, gmix, xt, mixer, early, *refs):
    *before, gt, gain_acc, bias_acc, mix_acc, project_acc, gp_s, nat_s = refs
    sums = (gain_acc, bias_acc, mix_acc, project_acc)
    _, features, lanes = xt.shape
    block = start + pl.program_id(0)
    groups = gp_s.shape[0] // GROUP
    base = block * groups
    tokens = lanes // GROUP
    ranks = gp_s.shape[1] // tokens
    per_tile = 128 // tokens
    rows = nat_s.shape[0] * GROUP

    @pl.when(pl.program_id(0) == 0)
    def clear():
        for i, acc in enumerate(sums):
            acc[...] = before[i][...] if before else jnp.zeros_like(acc)

    values = pair[...]
    centred = values - jnp.mean(values, axis=0, keepdims=True)
    scale = lax.rsqrt(jnp.mean(centred * centred, axis=0, keepdims=True) + EPS)
    hat = centred * scale
    examples = gp_s.shape[0]
    g = gn[:, pl.ds(pl.multiple_of(block * examples, examples), examples)]
    gain_acc[...] += g * hat
    bias_acc[...] += g
    h = g * gain[...]
    mean_h = jnp.mean(h, axis=0, keepdims=True)
    mean_hx = jnp.mean(h * hat, axis=0, keepdims=True)
    gp_s[...] = (scale * (h - mean_h - hat * mean_hx)).T
    to_natural(gmix, nat_s, features, block)
    example = lax.broadcasted_iota(jnp.int32, (GROUP, 128), 0)
    place = lax.broadcasted_iota(jnp.int32, (GROUP, 128), 1) // tokens
    own = place == example % per_tile
    keep_low = jnp.logical_and(own, example < per_tile)
    keep_high = jnp.logical_and(own, example >= per_tile)

    project = mixer[lanes:]
    stacked = xt[...].reshape(groups * features, lanes)
    projected = mul(stacked, project, NT).astype(bf16)
    g_pairs, g_parts = [], []
    for u in range(groups):
        here = slice(u * GROUP, (u + 1) * GROUP)
        slabs = []
        for j in range(ranks):
            c, s = j // per_tile, j % per_tile
            one = turn(gp_s[here, c * 128 : c * 128 + 128], -s * tokens)
            slabs.append(
                jnp.concatenate([jnp.where(keep_low, one, 0.0), jnp.where(keep_high, one, 0.0)], axis=1)
            )
        g_pairs.append(jnp.concatenate(slabs, axis=0).astype(bf16))
        g_parts.append(mul(xt[u], g_pairs[u], NT).astype(bf16))
    g_projected = jnp.concatenate(g_parts, axis=0)
    project_acc[...] += mul(stacked, g_projected, TN)
    shared = mul(g_projected, project)
    mix_total = mix_acc[...]
    for u, g_mix in enumerate(natural_groups(nat_s, features)):
        mix_total = mix_total + mul(g_mix, xt[u])
        mine = slice(u * features, (u + 1) * features)
        part = mul(projected[mine], g_pairs[u]) + mul(g_mix, mixer[:rows], TN) + shared[mine]
        gt[base + u] = (part + early[base + u].astype(f32)).astype(bf16)
    mix_acc[...] = mix_total


def spread_kernel(start, first_half, starts, ends, gt, out):
    step = start + pl.program_id(0)
    chunks = out.shape[1] // CHUNK
    last = starts.shape[0] - 1
    span = CHUNK // 128 + 1

    for c in range(chunks):
        number = step * chunks + c
        first = jnp.minimum(first_half[number], last + 1 - span)
        lows, highs, values = [], [], []
        for i in range(span):
            half = first + i
            lows.append(starts[pl.ds(half, 1), :])
            highs.append(ends[pl.ds(half, 1), :])
            values.append(gt[half // 2, :, pl.ds(pl.multiple_of(half % 2 * 128, 128), 128)])
        low = jnp.concatenate(lows, axis=1) - number * CHUNK
        high = jnp.concatenate(highs, axis=1) - number * CHUNK
        hot = one_hot(low, high, CHUNK)
        part = mul(jnp.concatenate(values, axis=1), hot, NT)
        out[:, c * CHUNK : (c + 1) * CHUNK] = part.astype(bf16)


def passing(kernel, given, previous):
    if not previous:
        return kernel, {}
    more = len(previous)
    skip = lambda *refs: kernel(*refs[:given], *refs[given + more :])
    return skip, {given + i: i for i in range(more)}


HBM, VMEM = pltpu.HBM, pltpu.VMEM
INSIDE = pl.BlockSpec(memory_space=pltpu.VMEM)


def held(*arrays):
    return [pltpu.with_memory_space_constraint(array, pltpu.VMEM) for array in arrays]


def away(*arrays):
    return [pltpu.with_memory_space_constraint(array, pltpu.HBM) for array in arrays]


def whole(shape):
    return pl.BlockSpec(shape, lambda *_: (0,) * len(shape))


def rank_of(tokens):
    per_tile = 128 // tokens
    slab, example = np.arange(per_tile)[:, None], np.arange(GROUP)[None, :]
    return np.eye(per_tile, dtype=np.float32)[(slab + example) % per_tile]


def make_mixer(w_res, w_comp, p_proj):
    tokens = w_res.shape[0]
    fm_tokens = tokens - w_comp.shape[0]
    mix = w_res.astype(f32) + jnp.pad(w_comp.astype(f32), ((fm_tokens, 0), (0, 0)))
    mix = jnp.broadcast_to(mix[:, None, :], (tokens, GROUP, tokens))
    by_tile = p_proj.T.astype(f32).reshape(-1, 128 // tokens, tokens)
    project = jnp.einsum("cqt,seq->cset", by_tile, rank_of(tokens))
    both = jnp.concatenate([mix, project.reshape(-1, GROUP, tokens)], axis=0)
    wide = both[:, :, None, :] * np.eye(GROUP, dtype=np.float32)[None, :, :, None]
    return wide.reshape(both.shape[0] * GROUP, GROUP * tokens).astype(bf16)


def token_stage(offs, starts, ends, rows, mixer, gain, bias, tokens, fm_tokens):
    features, row_total = rows.shape
    group_count, lanes = starts.shape
    examples = group_count * GROUP
    pairs = gain.shape[0]
    groups = BLOCK // GROUP
    return pl.pallas_call(
        tokens_kernel,
        name="tokens",
        grid_spec=pltpu.PrefetchScalarGridSpec(
            num_scalar_prefetch=1,
            grid=(examples // BLOCK,),
            in_specs=[
                pl.BlockSpec((groups, lanes), lambda i, _: (i, 0)),
                pl.BlockSpec((groups, lanes), lambda i, _: (i, 0)),
                pl.BlockSpec(memory_space=pltpu.VMEM),
                whole(mixer.shape),
                whole(gain.shape),
                whole(bias.shape),
            ],
            out_specs=[
                pl.BlockSpec((groups, features, lanes), lambda i, _: (i, 0, 0)),
                pl.BlockSpec((pairs, BLOCK), lambda i, _: (0, i)),
                pl.BlockSpec((pairs, BLOCK), lambda i, _: (0, i)),
                pl.BlockSpec((fm_tokens * features, BLOCK), lambda i, _: (0, i)),
                pl.BlockSpec(((tokens - fm_tokens) * features, BLOCK), lambda i, _: (0, i)),
            ],
            scratch_shapes=[
                pltpu.VMEM((BLOCK, pairs), f32),
                pltpu.VMEM((tokens, BLOCK, 256), f32),
                pltpu.VMEM((TOGETHER, features, lanes), f32),
            ],
        ),
        out_shape=[
            HBM((group_count, features, lanes), bf16),
            HBM((pairs, examples), f32),
            HBM((pairs, examples), bf16),
            HBM((fm_tokens * features, examples), bf16),
            HBM(((tokens - fm_tokens) * features, examples), bf16),
        ],
        compiler_params=params(36),
        cost_estimate=pl.CostEstimate(
            flops=2 * features * lanes * (row_total * 2 + 1000 * group_count),
            bytes_accessed=row_total * features * 2 + 30 * examples * 1024,
            transcendentals=0,
        ),
    )(offs, starts, ends, *away(rows), mixer, gain, bias)


def final_stage(res, cot, gain, bias, features):
    part, examples = res.shape
    width = cot.shape[1]
    tall = pl.BlockSpec((part, BLOCK), lambda i: (0, i))
    flat = pl.BlockSpec((BLOCK, part), lambda i: (i, 1))
    first = pl.BlockSpec((BLOCK, width - part), lambda i: (i, 0))
    turned = pl.BlockSpec((width - part, BLOCK), lambda i: (0, i))
    res, cot = away(res, cot)
    return pl.pallas_call(
        functools.partial(final_kernel, features),
        name="final_comp",
        grid=(examples // BLOCK,),
        in_specs=[tall, flat, first, whole(gain.shape), whole(bias.shape)],
        out_specs=[flat, tall, turned, whole((features, BLOCK)), whole((features, BLOCK))],
        out_shape=[
            HBM((examples, width), bf16),
            HBM((part, examples), bf16),
            HBM((width - part, examples), bf16),
            jax.ShapeDtypeStruct((features, BLOCK), f32),
            jax.ShapeDtypeStruct((features, BLOCK), f32),
        ],
        scratch_shapes=[pltpu.VMEM((part, BLOCK), bf16), pltpu.VMEM((part, BLOCK), bf16)],
        compiler_params=params(16),
        cost_estimate=pl.CostEstimate(
            flops=200 * part * examples, bytes_accessed=8 * part * examples, transcendentals=0
        ),
    )(res, cot, cot, gain, bias)


def mlp_stage(every, normed, res, cot, b_up, b_down, gain, bias, features, previous):
    units, columns = every.shape
    pairs, examples = normed.shape
    part = columns - pairs
    lanes = 2 * BLOCK
    block = lambda i: jnp.maximum(i - 1, 0)
    every, normed, res, cot, previous = away(every, normed, res, cot, previous)
    operands = (every, normed, res, cot, b_up, b_down, gain, bias)
    kernel, aliases = passing(functools.partial(mlp_kernel, features), len(operands), (previous,))
    return pl.pallas_call(
        kernel,
        name="mlp",
        grid=(1 + examples // lanes,),
        in_specs=[
            pl.BlockSpec(memory_space=pl.ANY),
            pl.BlockSpec(memory_space=pl.ANY),
            pl.BlockSpec(memory_space=pl.ANY),
            pl.BlockSpec(memory_space=pl.ANY),
            whole(b_up.shape),
            whole(b_down.shape),
            whole(gain.shape),
            whole(bias.shape),
            pl.BlockSpec(memory_space=pl.ANY),
        ],
        out_specs=[
            pl.BlockSpec((lanes, part), lambda i: (block(i), 0)),
            INSIDE,
            INSIDE,
            INSIDE,
            whole((features, BLOCK)),
            whole((features, BLOCK)),
            whole((units, BLOCK)),
            whole((part, BLOCK)),
        ],
        out_shape=[
            HBM(previous.shape, bf16),
            VMEM((part, examples), bf16),
            VMEM((units, examples), bf16),
            VMEM((units, examples), bf16),
            jax.ShapeDtypeStruct((features, BLOCK), f32),
            jax.ShapeDtypeStruct((features, BLOCK), f32),
            jax.ShapeDtypeStruct((units, BLOCK), f32),
            jax.ShapeDtypeStruct((part, BLOCK), f32),
        ],
        scratch_shapes=[
            pltpu.VMEM((units, examples), f32),
            pltpu.VMEM((part, lanes), bf16),
            pltpu.VMEM((units, BLOCK), f32),
            pltpu.VMEM((part, BLOCK), f32),
            pltpu.VMEM((units, pairs), bf16),
            pltpu.VMEM((units, part), bf16),
            pltpu.VMEM((pairs, examples), bf16),
            pltpu.VMEM((part, examples), bf16),
            pltpu.VMEM((part, examples), bf16),
            pltpu.SemaphoreType.DMA((3 + 2 * (examples // lanes),)),
        ],
        input_output_aliases=aliases,
        compiler_params=params(43),
        cost_estimate=pl.CostEstimate(
            flops=4 * units * columns * examples,
            bytes_accessed=2 * units * columns + 10 * part * examples,
            transcendentals=2 * units * examples,
        ),
    )(*operands, previous)


def early_stage(gmix, xt, mixer):
    group_count, features, lanes = xt.shape
    part, examples = gmix.shape
    count = part // features
    return pl.pallas_call(
        early_kernel,
        name="early",
        grid=(examples // BLOCK,),
        in_specs=[
            pl.BlockSpec((part, BLOCK), lambda i: (0, i)),
            pl.BlockSpec((BLOCK // GROUP, features, lanes), lambda i: (i, 0, 0)),
            whole(mixer.shape),
        ],
        out_specs=[INSIDE, whole((count * GROUP, lanes))],
        out_shape=[
            VMEM((group_count, features, lanes), bf16),
            jax.ShapeDtypeStruct((count * GROUP, lanes), f32),
        ],
        scratch_shapes=[pltpu.VMEM((count, BLOCK, 256), bf16)],
        compiler_params=params(16),
        cost_estimate=pl.CostEstimate(
            flops=2 * features * lanes * 500 * group_count,
            bytes_accessed=group_count * features * lanes * 8,
            transcendentals=0,
        ),
    )(*away(gmix, xt), mixer)


def back_stage(gn, pair, gain, gmix, xt, mixer, gt, start, count, before):
    pairs, examples = pair.shape
    group_count, features, lanes = xt.shape
    ranked = mixer.shape[0] - lanes
    fm_tokens = gmix.shape[0] // features
    wide = pl.BlockSpec((pairs, BLOCK), lambda i: (0, start + i))
    sums = [(pairs, BLOCK), (pairs, BLOCK), (fm_tokens * GROUP, lanes), (lanes, ranked)]
    pair, xt = away(pair, xt)
    gn, gmix, gt = held(gn, gmix, gt)
    by_group = pl.BlockSpec((BLOCK // GROUP, features, lanes), lambda i: (start + i, 0, 0))
    operands = (gn, pair, gain, gmix, xt, mixer, gt, *before)
    return pl.pallas_call(
        functools.partial(back_kernel, start),
        name="back",
        grid=(count,),
        in_specs=[INSIDE, wide, whole(gain.shape), INSIDE, by_group, whole(mixer.shape), INSIDE]
        + [whole(item.shape) for item in before],
        out_specs=[INSIDE] + [whole(shape) for shape in sums],
        out_shape=[VMEM((group_count, features, lanes), bf16)]
        + [jax.ShapeDtypeStruct(shape, f32) for shape in sums],
        scratch_shapes=[
            pltpu.VMEM((BLOCK, pairs), f32),
            pltpu.VMEM((fm_tokens, BLOCK, 256), bf16),
        ],
        input_output_aliases={6: 0},
        compiler_params=params(20),
        cost_estimate=pl.CostEstimate(
            flops=2 * features * lanes * 1400 * BLOCK // GROUP * count,
            bytes_accessed=40 * BLOCK * count * 1024,
            transcendentals=0,
        ),
    )(*operands)


def exact(value, selector, dims=NN):
    total = None
    for _ in range(3):
        piece = value.astype(bf16)
        value = value - piece.astype(f32)
        total = mul(piece, selector, dims) if total is None else total + mul(piece, selector, dims)
    return total


def ones_where(condition):
    return jnp.where(condition, 1.0, 0.0).astype(bf16)


def by_token_order(pairs, tokens):
    ranks = pairs // tokens
    row = lax.broadcasted_iota(jnp.int32, (pairs, pairs), 0)
    lane = lax.broadcasted_iota(jnp.int32, (pairs, pairs), 1)
    return ones_where((row % tokens) * ranks + row // tokens == lane)


def small_rows(tokens, pairs, units, width, features):
    counts = [tokens, pairs // 128, pairs // 128, units // 128, width // 128, -(-features // 128)]
    counts.append(counts[-1])
    starts = np.cumsum([0] + counts)
    return [(int(start), count) for start, count in zip(starts, counts)], -(-int(starts[-1]) // 8) * 8


def small_kernel(tokens, places, gain_acc, bias_acc, mix_fm, mix_comp, project, up, down, gains, biases, out):
    def put(place, row):
        start, count = place
        for i in range(count):
            piece = row[:, i * 128 : i * 128 + 128]
            out[start + i : start + i + 1, : piece.shape[1]] = piece

    def lying(column):
        return jnp.sum(column.T, axis=0, keepdims=True)

    out[...] = jnp.zeros_like(out)
    lanes = mix_fm.shape[1]
    ranked = project.shape[1]
    per_tile = 128 // tokens
    mix = jnp.concatenate([mix_fm[...], mix_comp[...]], axis=0)
    row = lax.broadcasted_iota(jnp.int32, mix.shape, 0) % GROUP
    lane = lax.broadcasted_iota(jnp.int32, mix.shape, 1) // tokens
    mix = jnp.where(row == lane, mix, 0.0)
    fold = ones_where(
        lax.broadcasted_iota(jnp.int32, (lanes, tokens), 0) % tokens
        == lax.broadcasted_iota(jnp.int32, (lanes, tokens), 1)
    )
    folded_mix = exact(mix, fold).reshape(tokens, GROUP, tokens)
    row = lax.broadcasted_iota(jnp.int32, project.shape, 0) // tokens
    lane = lax.broadcasted_iota(jnp.int32, project.shape, 1) % GROUP
    cells = jnp.where(row == lane, project[...], 0.0).reshape(GROUP, tokens, ranked)
    cells = jnp.sum(cells, axis=0)
    ranks = ranked // GROUP
    row = lax.broadcasted_iota(jnp.int32, (ranks, ranked), 0)
    lane = lax.broadcasted_iota(jnp.int32, (ranks, ranked), 1)
    slab = lane // GROUP
    rank = slab // per_tile * per_tile + (lane % GROUP + slab % per_tile) % per_tile
    pick = ones_where(row == rank)
    projected = None
    for _ in range(3):
        piece = cells.astype(bf16)
        cells = cells - piece.astype(f32)
        part = mul(pick, piece, NT)
        projected = part if projected is None else projected + part
    out[:ranks, :tokens] = projected
    out[:tokens, tokens : 2 * tokens] = jnp.sum(folded_mix, axis=1)
    both = jnp.concatenate([lying(gain_acc[...]), lying(bias_acc[...])], axis=0)
    both = exact(both, by_token_order(both.shape[1], tokens))
    put(places[1], both[:1])
    put(places[2], both[1:])
    put(places[3], lying(up[...]))
    put(places[4], lying(down[...]))
    put(places[5], lying(gains[0] + gains[1]))
    put(places[6], lying(biases[0] + biases[1]))


def small_stage(tokens, places, rows, gain_acc, bias_acc, mix_fm, mix_comp, project, up, down, gains, biases):
    def kernel(*refs):
        *given, gain_0, gain_1, bias_0, bias_1, out = refs
        small_kernel(tokens, places, *given, (gain_0[...], gain_1[...]), (bias_0[...], bias_1[...]), out)

    operands = (gain_acc, bias_acc, mix_fm, mix_comp, project, up, down, *gains, *biases)
    return pl.pallas_call(
        kernel,
        name="small",
        out_shape=jax.ShapeDtypeStruct((rows, 128), f32),
        compiler_params=params(16),
        cost_estimate=pl.CostEstimate(flops=10**9, bytes_accessed=4 * 10**6, transcendentals=0),
    )(*operands)


def last_kernel(tokens, places, total, more, *refs):
    *vectors, up, down, p_proj, w_res, w_comp, gain_one, bias_one, b_up, b_down, gain_two, bias_two = refs
    pairs = up.shape[1]
    value = total[...] + more[...].astype(f32)
    down[...] = value[:, pairs:]
    up[...] = exact(value[:, :pairs], by_token_order(pairs, tokens))
    vector = sum([ref[...] for ref in vectors])
    p_proj[...] = vector[: p_proj.shape[0], :tokens]
    w_res[...] = vector[:tokens, tokens : 2 * tokens]
    w_comp[...] = vector[tokens - w_comp.shape[0] : tokens, tokens : 2 * tokens]
    rest = (gain_one, bias_one, b_up, b_down, gain_two, bias_two)
    for (start, count), ref in zip(places[1:], rest):
        if ref.shape[0] == 1:
            row = [vector[start + i : start + i + 1] for i in range(count)]
            ref[...] = jnp.concatenate(row, axis=1)[:, : ref.shape[1]]
        else:
            ref[...] = vector[start : start + count]


def last_stage(total, more, vectors, places, pairs, tokens, features, comp_tokens):
    rows, columns = total.shape
    shapes = [(rows, pairs), (rows, columns - pairs), (pairs // tokens, tokens), (tokens, tokens), (comp_tokens, tokens)]
    shapes += [(count, 128) for _, count in places[1:-2]] + [(1, features)] * 2
    return pl.pallas_call(
        functools.partial(last_kernel, tokens, places),
        name="last",
        out_shape=[jax.ShapeDtypeStruct(shape, f32) for shape in shapes],
        compiler_params=params(16),
        cost_estimate=pl.CostEstimate(
            flops=6 * rows * pairs * pairs, bytes_accessed=10 * rows * columns, transcendentals=0
        ),
    )(total, more, *vectors)


def grad_kernel(rows, table, pre, hidden, normed, mix, *refs):
    *outs, picked_s = refs
    pairs = normed.shape[0]
    parts = 2
    part = mix.shape[0] // parts

    def picked(source):
        for i in range(picked_s.shape[0] // rows):
            start = pl.multiple_of(table[i] * rows, rows)
            picked_s[i * rows : (i + 1) * rows, :] = source[pl.ds(start, rows), :]
        return picked_s[...]

    def put(at, right, left):
        value = mul(left, right, NT).astype(bf16)
        first = 0
        for out in outs:
            out[:, at : at + right.shape[0]] = value[first : first + out.shape[0]]
            first += out.shape[0]

    left = picked(hidden)
    for i in range(parts):
        put(pairs + i * part, mix[i * part : (i + 1) * part, :], left)
    put(0, normed[...], picked(pre))


def grad_stage(tables, pre, hidden, normed, mix, rows):
    units, examples = hidden.shape
    pairs = normed.shape[0]
    columns = pairs + mix.shape[0]
    counts = [table.shape[0] * rows for table in tables]
    count = sum(counts)
    operands = held(pre, hidden, normed, mix)
    return pl.pallas_call(
        functools.partial(grad_kernel, rows),
        name="weight_grads",
        grid_spec=pltpu.PrefetchScalarGridSpec(
            num_scalar_prefetch=1,
            grid=(1,),
            in_specs=[INSIDE] * 4,
            out_specs=[INSIDE] * len(counts),
            scratch_shapes=[pltpu.VMEM((count, examples), bf16)],
        ),
        out_shape=[VMEM((size, columns), bf16) for size in counts],
        compiler_params=params(16),
        cost_estimate=pl.CostEstimate(
            flops=2 * count * examples * columns,
            bytes_accessed=2 * count * columns + 2 * examples * (2 * units + columns),
            transcendentals=0,
        ),
    )(jnp.concatenate(tables), *operands)


def normed_grad_kernel(every, pre, out, up_w, arrive):
    bring = pltpu.make_async_copy(every.at[:, pl.ds(0, out.shape[0])], up_w, arrive.at[0])
    bring.start()
    bring.wait()
    out[...] = mul(up_w[...], pre[...], TN)


def normed_grad_stage(every, pre, pairs):
    units, examples = pre.shape
    return pl.pallas_call(
        normed_grad_kernel,
        name="normed_grad",
        in_specs=[pl.BlockSpec(memory_space=pl.ANY), INSIDE],
        out_specs=INSIDE,
        out_shape=VMEM((pairs, examples), f32),
        scratch_shapes=[pltpu.VMEM((units, pairs), bf16), pltpu.SemaphoreType.DMA((1,))],
        compiler_params=params(12),
        cost_estimate=pl.CostEstimate(
            flops=2 * units * pairs * examples, bytes_accessed=2 * units * pairs, transcendentals=0
        ),
    )(*away(every), *held(pre))


def spread_stage(first_half, starts, ends, gt, row_total, start, count, previous):
    group_count, features, lanes = gt.shape
    operands = (starts.reshape(-1, 128), ends.reshape(-1, 128), *held(gt))
    previous = away(*previous)
    kernel, aliases = passing(functools.partial(spread_kernel, start), len(operands) + 1, previous)
    return pl.pallas_call(
        kernel,
        name="spread",
        grid_spec=pltpu.PrefetchScalarGridSpec(
            num_scalar_prefetch=1,
            grid=(count,),
            in_specs=[whole(operands[0].shape), whole(operands[1].shape), INSIDE]
            + [pl.BlockSpec(memory_space=pl.ANY)] * len(previous),
            out_specs=pl.BlockSpec((features, SPREAD_ROWS), lambda i, _: (0, start + i)),
        ),
        out_shape=HBM((features, row_total), bf16),
        input_output_aliases=aliases,
        compiler_params=params(16),
        cost_estimate=pl.CostEstimate(
            flops=4 * features * lanes * SPREAD_ROWS * count,
            bytes_accessed=SPREAD_ROWS * count * features * 4,
            transcendentals=0,
        ),
    )(first_half, *operands, *previous)


def bag_bounds(lengths):
    ends = jnp.cumsum(lengths.reshape(-1))
    starts = ends - lengths.reshape(-1)
    return starts, ends


def column(vector, lanes=BLOCK):
    return jnp.broadcast_to(vector[:, None], (vector.shape[0], lanes))


def gelu(v):
    inner = np.sqrt(2 / np.pi).astype(np.float32) * (v + 0.044715 * (v * v * v))
    return 0.5 * v * (1.0 + jnp.tanh(inner))


def gelu_slope(v):
    root = np.sqrt(2 / np.pi).astype(np.float32)
    bent = jnp.tanh(root * (v + 0.044715 * (v * v * v)))
    return 0.5 * (1.0 + bent) + 0.5 * v * (1.0 - bent * bent) * root * (1.0 + 3 * 0.044715 * (v * v))


def shards(
    embed_rows,
    lengths,
    cotangent,
    p_proj,
    gain_one,
    bias_one,
    w_up,
    b_up,
    w_down,
    b_down,
    w_comp,
    w_res,
    gain_two,
    bias_two,
):
    links = Links()
    tokens = w_res.shape[0]
    features = embed_rows.shape[1]
    ranks = p_proj.shape[1]
    pairs = tokens * ranks
    row_total = embed_rows.shape[0]
    fm_width = b_down.shape[0]
    examples = cotangent.shape[0]

    def by_rank(vector):
        return jnp.swapaxes(vector.reshape(-1, tokens, ranks), 1, 2).reshape(vector.shape)

    def by_token(vector):
        return jnp.swapaxes(vector.reshape(-1, ranks, tokens), 1, 2).reshape(vector.shape)

    every = links.gather(jnp.concatenate([by_rank(w_up.T), w_down], axis=1))

    starts, ends = bag_bounds(lengths)
    lanes = GROUP * tokens
    starts = starts.reshape(-1, lanes)
    ends = ends.reshape(-1, lanes)
    offs = jnp.concatenate([starts[:, 0], ends[-1:, -1]])
    bases = jnp.arange(row_total // CHUNK, dtype=jnp.int32) * CHUNK
    half_ends = ends.reshape(-1, 128)[:, 127]
    first_half = jnp.sum((half_ends[None, :] <= bases[:, None]).astype(jnp.int32), axis=1)
    mixer = make_mixer(w_res, w_comp, p_proj)
    gain_a, bias_a = column(by_rank(gain_one)), column(by_rank(bias_one))
    gain_b, bias_b = column(gain_two), column(bias_two)
    down_bias = column(b_down)

    xt, pair, normed, res, res_comp = token_stage(
        offs, starts, ends, embed_rows.T, mixer, gain_a, bias_a, tokens, fm_width // features
    )
    out, mix_comp, cot, gain_acc1, bias_acc1 = final_stage(res_comp, cotangent, gain_b, bias_b, features)
    mix_comp, first_half = lax.optimization_barrier((mix_comp, first_half))
    gt, mix_acc1 = early_stage(mix_comp, xt, mixer)
    gt, normed = lax.optimization_barrier((gt, normed))
    out, mix, hidden, g_pre, gain_acc0, bias_acc0, up_acc, down_acc = mlp_stage(
        every, normed, res, cot, b_up[None, :], b_down[None, :], gain_b, bias_b, features, out
    )

    unit_rows = links.unit_rows(w_down.shape[0])
    tables, rows, (g_pre, hidden) = links.shards(unit_rows, g_pre, hidden)
    ring = links.ring(unit_rows)
    gradients = lambda tables: grad_stage(tables, g_pre, hidden, normed, mix, rows)
    (sent,) = gradients(tables[:1])
    crossing = links.to_other_core(sent)
    g_pre, hidden, sent = lax.optimization_barrier((g_pre, hidden, sent))
    (mine,) = gradients(tables[1:2])
    ring.add(*lax.optimization_barrier((mine, crossing)))
    g_pre, hidden = ring.start((g_pre, hidden))
    sent, mine = gradients(tables[2:])
    sent, mine, g_pre = ring.finish((sent, mine, g_pre))
    sent, mine, g_pre = ring.start((sent, mine, g_pre))
    crossing = links.to_other_core(sent)
    g_normed = normed_grad_stage(every, g_pre, pairs)

    blocks = examples // BLOCK
    cuts = [0, blocks // 2, blocks]
    sums = []
    for i in range(2):
        if i > 0:
            g_normed, gt, sums = ring.start((g_normed, gt, sums))
        gt, *sums = back_stage(
            g_normed, pair, gain_a, mix, xt, mixer, gt, cuts[i], cuts[i + 1] - cuts[i], sums
        )
        if i == 0:
            g_normed, gt, sums, crossing, mine = lax.optimization_barrier((g_normed, gt, sums, crossing, mine))
            ring.add(mine, crossing)
        g_normed, gt, sums = ring.finish((g_normed, gt, sums))
    gt, sums = ring.start((gt, sums))
    gain_acc, bias_acc, mix_acc0, project_acc = sums
    places, rows = small_rows(tokens, pairs, b_up.shape[0], fm_width, features)
    vector = small_stage(
        tokens,
        places,
        rows,
        gain_acc,
        bias_acc,
        mix_acc0,
        mix_acc1,
        project_acc,
        up_acc,
        down_acc,
        (gain_acc0, gain_acc1),
        (bias_acc0, bias_acc1),
    )

    steps = row_total // SPREAD_ROWS
    swaps = links.rounds()
    cuts = [0, steps * 5 // 9, steps * 7 // 9, steps]
    rows_grad = ()
    for i in range(3):
        if i == 1:
            vector, gt, rows_grad = ring.start((vector, gt, rows_grad))
        far = [swap(vector) for swap in swaps[i]]
        rows_grad = spread_stage(
            first_half, starts, ends, gt, row_total, cuts[i], cuts[i + 1] - cuts[i], rows_grad
        )
        far, gt, rows_grad = lax.optimization_barrier((far, gt, (rows_grad,)))
        vector = sum(far, vector)
        if i != 1:
            vector, gt, rows_grad = ring.finish((vector, gt, rows_grad))
    for some in swaps[3:]:
        vector = sum([swap(vector) for swap in some], vector)
    vectors = [vector]
    up_grad, down_grad, proj_grad, res_grad, comp_grad, *rest = last_stage(
        *ring.end(), vectors, places, pairs, tokens, features, w_comp.shape[0]
    )
    rest = [item.reshape(-1) for item in rest]
    return (
        out,
        rows_grad[0].T,
        proj_grad.T,
        rest[0],
        rest[1],
        up_grad.T,
        rest[2],
        down_grad,
        rest[3],
        comp_grad,
        res_grad,
        rest[4],
        rest[5],
    )


def ring_order(chips):
    return list(range(0, chips, 2)) + list(range(chips - 1, 0, -2))


def added(*terms):
    return sum([term.astype(f32) for term in terms[1:]], terms[0].astype(f32))


def ring_shards(chips):
    order = ring_order(chips)
    reach = chips // 2
    steps = [reach]
    for distance in range(reach - 1, 0, -1):
        steps += [distance, -distance]
    steps.append(0)
    return [[order[(order.index(chip) + step) % chips] for step in steps] for chip in range(chips)]


class Ring:
    def __init__(self, rows):
        self.rows = rows
        self.chips = lax.axis_size("dp") // 2
        self.order = ring_order(self.chips)
        self.reach = self.chips // 2
        self.shards = []
        self.left = self.reach
        self.flying = None
        self.send = None
        self.total = None

    def add(self, *terms):
        terms = [term.reshape(-1, self.rows, term.shape[-1]) for term in terms]
        self.shards += [[term[i] for term in terms] for i in range(terms[0].shape[0])]

    def ahead(self, distance):
        return self.shards[1 + 2 * (self.reach - 1 - distance)]

    def behind(self, distance):
        return self.shards[2 + 2 * (self.reach - 1 - distance)]

    def along(self, value, step):
        order, chips = self.order, self.chips
        pairs = [
            (2 * order[i] + core, 2 * order[(i + step) % chips] + core)
            for i in range(chips)
            for core in range(2)
        ]
        return lax.ppermute(value, "dp", pairs)

    def start(self, others):
        if self.left < 0:
            return others
        if self.send is None:
            middle = added(*self.shards[0]).astype(bf16)
            rows = middle.shape[0] // 2
            self.send = [middle[:rows], middle[rows:]]
        self.send, others = lax.optimization_barrier((self.send, others))
        if self.left > 0:
            self.flying = (self.along(self.send[0], 1), self.along(self.send[1], -1))
        else:
            pairs = [(i, i ^ 1) for i in range(lax.axis_size("branch"))]
            self.flying = (lax.ppermute(self.send[0], "branch", pairs),)
        return others

    def finish(self, others):
        if self.flying is None:
            return others
        arrived, others = lax.optimization_barrier((self.flying, others))
        self.flying = None
        self.left -= 1
        if self.left < 0:
            self.more = arrived[0]
        elif self.left == 0:
            self.total = added(*self.shards[-1], *arrived)
            self.send = [self.total.astype(bf16)]
        else:
            one, two = added(*self.ahead(self.left)), added(*self.behind(self.left))
            first, second = arrived[0].astype(f32), arrived[1].astype(f32)
            if self.left == self.reach - 1:
                rows = first.shape[0]
                first = jnp.pad(first, ((0, one.shape[0] - rows), (0, 0)))
                second = jnp.pad(second, ((two.shape[0] - rows, 0), (0, 0)))
            self.send = [(one + first).astype(bf16), (two + second).astype(bf16)]
        return others

    def end(self):
        while self.left >= 0:
            self.start(())
            self.finish(())
        return self.total, self.more


class Links:
    def swaps(self, bits):
        dp, branch = lax.axis_size("dp"), lax.axis_size("branch")
        found = []
        for chosen in range(1, 1 << len(bits)):
            flip = functools.reduce(lambda a, b: a | b, [bit for i, bit in enumerate(bits) if chosen >> i & 1])
            pairs = [(i, i ^ flip) for i in range(dp * branch)]
            found.append(lambda value, pairs=pairs: lax.ppermute(value, ("dp", "branch"), pairs))
        return found

    def rounds(self):
        size = lax.axis_size("dp") * lax.axis_size("branch")
        bits = [1 << i for i in range(size.bit_length() - 1)]
        return [self.swaps(bits[i : i + 2]) for i in range(0, len(bits), 2)]

    def gather(self, own):
        return lax.all_gather(own, "dp", axis=0, tiled=True)

    def unit_rows(self, rows):
        return rows

    def owners(self):
        owners = np.asarray(ring_shards(lax.axis_size("dp") // 2), np.int32)
        table = np.stack([2 * owners + 1, 2 * owners, 2 * owners, 2 * owners + 1], axis=1)
        table = table.reshape(-1, 2 * owners.shape[1])
        return lax.dynamic_index_in_dim(jnp.asarray(table), lax.axis_index("dp"), 0, keepdims=False)

    def shards(self, rows, *units):
        table = self.owners()
        first = 3
        if rows % 16 != 0:
            units = [item.reshape(table.shape[0], rows, -1)[table].reshape(item.shape) for item in units]
            table = jnp.arange(units[0].shape[0] // 96, dtype=jnp.int32)
            rows, first = 96, 1
        half = table.shape[0] // 2
        cuts = [(0, first), (half, half + first), (first, half), (half + first, 2 * half)]
        return [table[a:b] for a, b in cuts], rows, units

    def to_other_core(self, value):
        return lax.ppermute(value, "dp", [(i, i ^ 1) for i in range(lax.axis_size("dp"))])

    def ring(self, rows):
        return Ring(rows)


def solution(mesh):
    spread = P(("dp", "branch"), None)
    in_specs = (
        spread,
        spread,
        spread,
        P(),
        P(),
        P(),
        P(None, "dp"),
        P(),
        P("dp", None),
        P(),
        P(),
        P(),
        P(),
        P(),
    )
    out_specs = (
        spread,
        spread,
        P(),
        P(),
        P(),
        P(None, "dp"),
        P(),
        P("dp", None),
        P(),
        P(),
        P(),
        P(),
        P(),
    )
    return jax.shard_map(shards, mesh=mesh, in_specs=in_specs, out_specs=out_specs, check_vma=False)
```
